32 devices in a mesh: gx: 4 (over y, x), gz: 8 (over z, core).
Axes of the slice: x: 2, y: 2, z: 4, core: 2. Of those that a mesh axis runs over, the one named last changes fastest.
Arguments:
- density: float32 [512, 64, 256], P('gx', 'gz'), may hold values from 0 to 1
- bin_rows: int32 [32], replicated, may hold values from 0 to 255
- tf_extinction: float32 [256, 16], replicated, may hold values from 0.5 to 2
- tf_color: float32 [256, 16], replicated, may hold values from 0 to 1
- extinction_scale: float32 [16], replicated, may hold values from 0.3 to 20
- ambient: float32 [16], replicated, may hold values from 0.1 to 1
- backdrop: float32 [16], replicated, may hold values from 0 to 1
Outputs:
- image: float32 [512, 16, 256], P(('gx', 'gz'))
The draws below stay inside these ranges and needn't reach their ends.
All inputs are finite; a program needn't handle non-finite values.
Results may differ from the reference program's by a relative error of at most 0.0003.
Values sent between devices are 32-bit elements; how exact they have to be, the bound alone decides.
No kernel may reach another device: no remote copies, remote signals or barrier semaphores. Data moves between devices by JAX's collectives and lax.ppermute only.
A program may use at most 128 MiB of HBM per device.

```python
import math
import jax
import jax.numpy as jnp
from jax import lax

LAMBDAS = 16
BINS = 32
ROWS = 256
NX = 512
NZ = 64
NY = 256


def draw_bin_rows(key, part):
    key = jax.random.fold_in(key, 7)
    first, second = jax.random.split(key)
    values = jax.random.randint(first, (BINS,), 1, ROWS - 1)
    places = jax.random.permutation(second, BINS)
    values = values.at[places[0]].set(0)
    values = values.at[places[1]].set(ROWS - 1)
    return values.astype(jnp.int32)


def shard_levels(stream_key, shape, cuts, low, top_value):
    gain, own = 1.0, jax.random.fold_in(stream_key, 6)
    for position, parts in cuts:
        heights = jnp.exp(jax.random.uniform(jax.random.fold_in(own, position), (parts,), jnp.float32, low / len(cuts), top_value / len(cuts)))
        gain = gain * jnp.repeat(heights, shape[position] // parts).reshape([-1 if axis == position else 1 for axis in range(len(shape))])
    return gain


def setup_inputs(seed: int = 0) -> dict:
    splits = jax.random.split(jax.random.key(seed), 8)
    return {
        "density": jnp.clip(1.0 * jax.random.uniform(splits[0], (NX, NZ, NY), jnp.float32) ** shard_levels(splits[0], (NX, NZ, NY), ((0, 4), (1, 8)), -0.2, 0.2), 0.0, 1.0),
        "bin_rows": draw_bin_rows(jax.random.fold_in(splits[7], 71), 0),
        "tf_extinction": jnp.clip(jnp.exp(jax.random.uniform(splits[2], (ROWS, LAMBDAS), jnp.float32, math.log(0.5), math.log(2.0))), 0.5, 2.0),
        "tf_color": jnp.clip(jax.random.uniform(splits[3], (ROWS, LAMBDAS), jnp.float32, 0.0, 1.0), 0.0, 1.0),
        "extinction_scale": jnp.clip(jnp.exp(jax.random.uniform(splits[4], (LAMBDAS,), jnp.float32, math.log(0.3), math.log(20.0))), 0.3, 20.0),
        "ambient": jnp.clip(jax.random.uniform(splits[5], (LAMBDAS,), jnp.float32, 0.1, 1.0), 0.1, 1.0),
        "backdrop": jnp.clip(jax.random.uniform(splits[6], (LAMBDAS,), jnp.float32, 0.0, 1.0), 0.0, 1.0),
    }


def blur(padded, axis):
    size = padded.shape[axis]
    low = lax.slice_in_dim(padded, 0, size - 2, axis=axis)
    mid = lax.slice_in_dim(padded, 1, size - 1, axis=axis)
    high = lax.slice_in_dim(padded, 2, size, axis=axis)
    return (low + 2.0 * mid + high) * 0.25


def reference(density, bin_rows, tf_extinction, tf_color, extinction_scale, ambient, backdrop):
    padded = jnp.pad(density, 1)
    smooth = blur(blur(blur(padded, 0), 1), 2)
    table = jnp.concatenate([tf_extinction, tf_color], axis=1)[bin_rows]
    step_x = 1.0 / NX
    step_z = 1.0 / NZ

    def plane(depth, rho):
        scaled = rho * (BINS - 1)
        lower = jnp.clip(jnp.floor(scaled), 0, BINS - 2).astype(jnp.int32)
        frac = (scaled - lower.astype(scaled.dtype))[..., None]
        props = table[lower] * (1.0 - frac) + table[lower + 1] * frac
        sigma = props[..., :LAMBDAS] * extinction_scale
        color = props[..., LAMBDAS:]
        light = jnp.exp(-depth)
        shade = color * (ambient + light)
        inclusive = jnp.cumsum(sigma, axis=0)
        weight = jnp.exp(-step_z * (inclusive - sigma)) * (-jnp.expm1(-step_z * sigma))
        partial_value = jnp.sum(weight * shade, axis=0)
        through = jnp.exp(-step_z * inclusive[-1])
        row = partial_value + through * backdrop
        return depth + step_x * sigma, row.T

    start = jnp.zeros((NZ, NY, LAMBDAS), density.dtype)
    final, rows = lax.scan(plane, start, smooth)
    return rows
```

```python
import functools

import jax
import jax.numpy as jnp
from jax import lax
from jax.experimental import pallas as pl
from jax.experimental.pallas import tpu as pltpu
from jax.sharding import PartitionSpec as P

LANES = 128
LOG2E = 1.4426950408889634
MIB = 1 << 20


def group_ids(shape, width):
    return lax.broadcasted_iota(jnp.int32, shape, len(shape) - 1) // width


def swap_groups(tiles, groups, width):
    tiles = list(tiles)
    lane = group_ids(tiles[0].shape, width)
    bit = 1
    while bit < groups:
        upper = (lane & bit) != 0
        shift = bit * width
        for first in range(groups):
            if first & bit:
                continue
            a, b = tiles[first], tiles[first | bit]
            axis = a.ndim - 1
            tiles[first] = jnp.where(upper, pltpu.roll(b, shift, axis), a)
            tiles[first | bit] = jnp.where(upper, b, pltpu.roll(a, LANES - shift, axis))
        bit *= 2
    return tiles


def pack_kernel(groups, width, x_ref, out_ref):
    tile_count = x_ref.shape[3] // LANES
    steps, depth = x_ref.shape[1], x_ref.shape[2]
    lane = lax.broadcasted_iota(jnp.int32, (depth, LANES), 1)

    def body(step, carry):
        wide = []
        for part in range(groups):
            tiles = [x_ref[part, step, :, t * LANES:(t + 1) * LANES] for t in range(tile_count)]
            up = [pltpu.roll(tile, 1, 1) for tile in tiles]
            down = [pltpu.roll(tile, LANES - 1, 1) for tile in tiles]
            row = []
            for t in range(tile_count):
                before = up[t - 1] if t > 0 else jnp.zeros_like(up[0])
                after = down[t + 1] if t + 1 < tile_count else jnp.zeros_like(up[0])
                low = jnp.where(lane == 0, before, up[t])
                high = jnp.where(lane == LANES - 1, after, down[t])
                row.append(low + 2.0 * tiles[t] + high)
            wide.append(row)
        for t in range(tile_count):
            swapped = swap_groups([wide[part][t] for part in range(groups)], groups, width)
            for part in range(groups):
                out_ref[t * groups + part, step] = swapped[part]
        return carry

    lax.fori_loop(0, steps, body, 0)


def pack(x, groups, width):
    steps = x.shape[0] // groups
    blocks = x.shape[2] // width
    return pl.pallas_call(
        functools.partial(pack_kernel, groups, width),
        out_shape=jax.ShapeDtypeStruct((blocks, steps, x.shape[1], LANES), jnp.float32),
        in_specs=[pl.BlockSpec(memory_space=pltpu.VMEM)],
        out_specs=pl.BlockSpec(memory_space=pltpu.VMEM),
        compiler_params=pltpu.CompilerParams(vmem_limit_bytes=32 * MIB),
        name="pack",
    )(x.reshape(groups, steps, x.shape[1], x.shape[2]))


def depth_kernel(groups, width, bins, scale, *refs):
    count = len(refs) - 9
    pieces = refs[:count]
    halo_ref, table_ref, s_ref, start_ref, total_ref, raw, sums, halves, sem = refs[count:]
    steps, depth = pieces[0].shape[-3], pieces[0].shape[-2]
    layers = depth * count
    colors = table_ref.shape[0]
    me = lax.axis_index("gz")
    copies = []
    for apart in range(count):
        source = me ^ apart
        place = pl.multiple_of(8 + source * depth, 8)
        origin = pieces[apart].at[me] if apart == 0 else pieces[apart]
        copies.append(pltpu.make_async_copy(
            origin, raw.at[pl.ds(1, steps), pl.ds(place, depth), :], sem.at[apart]))
    for copy in copies:
        copy.start()
    zeros = jnp.zeros((steps + 2, 8, LANES), jnp.float32)
    raw[:, 0:8, :] = zeros
    raw[:, 8 + layers:16 + layers, :] = zeros
    for copy in copies:
        copy.wait()
    lane = group_ids((layers, LANES), width)
    halo = halo_ref[...].reshape(layers, LANES)
    low = pltpu.roll(raw[steps, 8:8 + layers, :], width, 1)
    high = pltpu.roll(raw[1, 8:8 + layers, :], LANES - width, 1)
    raw[0, 8:8 + layers, :] = jnp.where(lane == 0, halo, low)
    raw[steps + 1, 8:8 + layers, :] = jnp.where(lane == groups - 1, halo, high)

    def smooth(step, carry):
        v = raw[step] + 2.0 * raw[step + 1] + raw[step + 2]
        size = v.shape[0]
        before = pltpu.roll(v, 1, 0)
        after = pltpu.roll(v, size - 1, 0)
        total = before + 2.0 * v + after
        s_ref[step] = total[8:8 + layers] * (scale / 64.0)
        return carry

    lax.fori_loop(0, steps, smooth, 0)
    edge = lax.broadcasted_iota(jnp.int32, (bins, LANES), 0).astype(jnp.float32) - 1.0
    rows = steps // 2

    def count_layer(z, carry):
        for half in range(2):
            acc = jnp.zeros((bins, LANES), jnp.float32)
            for step in range(rows):
                row = jnp.broadcast_to(s_ref[half * rows + step, pl.ds(z, 1), :], (bins, LANES))
                acc = acc + jnp.minimum(jnp.maximum(row, edge), edge + 1.0)
            sums[half, z] = acc - edge * rows
        return carry

    lax.fori_loop(0, layers, count_layer, 0)
    table = table_ref[...]
    at_once = 4

    def products(chunk, carry):
        for half in range(2):
            wide = jnp.concatenate(
                [sums[half, chunk * at_once + k] for k in range(at_once)], axis=1)
            out = jnp.dot(table, wide, precision=lax.Precision.HIGHEST,
                          preferred_element_type=jnp.float32)
            for k in range(at_once):
                halves[half, chunk * at_once + k] = out[:, k * LANES:(k + 1) * LANES]
        return carry

    lax.fori_loop(0, layers // at_once, products, 0)
    group = group_ids((colors, LANES), width)

    def scan_groups(chunk, carry):
        packed = jnp.zeros((colors, LANES), jnp.float32)
        for k in range(groups):
            z = chunk * groups + k
            first = halves[0, z]
            both = first + halves[1, z]
            inclusive = both
            everything = both
            shift = 1
            while shift < groups:
                moved = pltpu.roll(inclusive, shift * width, 1)
                inclusive = inclusive + jnp.where(group >= shift, moved, 0.0)
                everything = everything + pltpu.roll(everything, shift * width, 1)
                shift *= 2
            begin = inclusive - both
            start_ref[0, z] = begin
            start_ref[1, z] = begin + first
            packed = jnp.where(group == k, everything, packed)
        total_ref[chunk] = packed
        return carry

    lax.fori_loop(0, layers // groups, scan_groups, 0)


def depths(own, received, halo, table, groups, width, bins):
    count, steps, depth, _ = own.shape
    layers = count * depth
    colors = table.shape[0]
    return pl.pallas_call(
        functools.partial(depth_kernel, groups, width, bins, float(bins - 1)),
        out_shape=(
            jax.ShapeDtypeStruct((steps, layers, LANES), jnp.float32),
            jax.ShapeDtypeStruct((2, layers, colors, LANES), jnp.float32),
            jax.ShapeDtypeStruct((layers // groups, colors, LANES), jnp.float32),
        ),
        in_specs=[pl.BlockSpec(memory_space=pl.ANY)] * count
        + [pl.BlockSpec(memory_space=pltpu.VMEM)] * 2,
        out_specs=[pl.BlockSpec(memory_space=pltpu.VMEM)] * 3,
        scratch_shapes=[
            pltpu.VMEM((steps + 2, layers + 16, LANES), jnp.float32),
            pltpu.VMEM((2, layers, bins, LANES), jnp.float32),
            pltpu.VMEM((2, layers, colors, LANES), jnp.float32),
            pltpu.SemaphoreType.DMA((count,)),
        ],
        compiler_params=pltpu.CompilerParams(vmem_limit_bytes=48 * MIB),
        name="depths",
    )(own, *received, halo, table)


def render_kernel(groups, width, bins, ratio, turn, s_ref, start_ref, table_ref, ambient_ref,
                  backdrop_ref, *refs):
    *before_refs, image_ref, depth = refs
    steps, layers, _ = s_ref.shape
    rows = steps // 2
    colors = ambient_ref.shape[0]
    half = (lax.axis_index("gz") + turn) % 2
    group = group_ids((colors, LANES), width)

    def begin(chunk, carry):
        packed = before_refs[0][chunk]
        for ref in before_refs[1:]:
            packed = packed + ref[chunk]
        for k in range(groups):
            z = chunk * groups + k
            value = jnp.where(group == k, packed, 0.0)
            shift = 1
            while shift < groups:
                value = value + pltpu.roll(value, shift * width, 1)
                shift *= 2
            depth[z] = start_ref[half, z] + value
        return carry

    lax.fori_loop(0, layers // groups, begin, 0)
    ambient = ambient_ref[...]
    table = table_ref[...]
    edge = (lax.broadcasted_iota(jnp.int32, (bins, LANES), 0).astype(jnp.float32) - 1.0).astype(
        jnp.bfloat16)
    zero = jnp.zeros((bins, LANES), jnp.bfloat16)
    one = jnp.ones((bins, LANES), jnp.bfloat16)
    block = 8

    def advance(step, carry):
        row = half * rows + step

        def layer_block(chunk, state):
            through, partial = state
            place = pl.multiple_of(chunk * block, block)
            s = s_ref[row, pl.ds(place, block), :]
            lower = jnp.floor(s)
            frac = s - lower
            coarse = frac.astype(jnp.bfloat16).astype(jnp.float32)
            fine = frac - coarse

            def wide(value, r):
                return jnp.broadcast_to(value[r:r + 1], (bins, LANES)).astype(jnp.bfloat16)

            columns = []
            for r in range(block):
                away = wide(lower, r) - edge
                main = jnp.minimum(jnp.maximum(away + wide(coarse, r), zero), one)
                rest = jnp.where(away == zero, wide(fine, r), zero)
                columns.append(jnp.concatenate([main, main, rest], axis=0))
            weights = jnp.concatenate(columns, axis=1)
            props = jnp.dot(table, weights, preferred_element_type=jnp.float32)
            for r in range(block):
                part = props[:, r * LANES:(r + 1) * LANES]
                sigma, color = part[:colors], part[colors:]
                later = through * jnp.exp2(sigma)
                z = place + r
                above = depth[z]
                shade = color * (ambient + jnp.exp2(above))
                partial = partial + (through - later) * shade
                depth[z] = above + sigma * ratio
                through = later
            return through, partial

        state = (jnp.ones((colors, LANES), jnp.float32), jnp.zeros((colors, LANES), jnp.float32))
        through, partial = lax.fori_loop(0, layers // block, layer_block, state, unroll=True)
        image_ref[step] = partial + through * backdrop_ref[...]
        return carry

    lax.fori_loop(0, rows, advance, 0)


def pack_image_kernel(groups, width, x_ref, out_ref):
    for chunk in range(x_ref.shape[0] // groups):
        tiles = swap_groups([x_ref[chunk * groups + k] for k in range(groups)], groups, width)
        for part in range(groups):
            out_ref[part, chunk] = tiles[part]


def pack_image(image, groups, width):
    rows, colors, _ = image.shape
    return pl.pallas_call(
        functools.partial(pack_image_kernel, groups, width),
        out_shape=jax.ShapeDtypeStruct((groups, rows // groups, colors, LANES), jnp.float32),
        in_specs=[pl.BlockSpec(memory_space=pltpu.VMEM)],
        out_specs=pl.BlockSpec(memory_space=pltpu.VMEM),
        name="pack_image",
    )(image)


def render(s, start, table, ambient, backdrop, before, groups, width, bins, ratio, turn):
    steps, layers, _ = s.shape
    colors = ambient.shape[0]
    return pl.pallas_call(
        functools.partial(render_kernel, groups, width, bins, ratio, turn),
        out_shape=jax.ShapeDtypeStruct((steps // 2, colors, LANES), jnp.float32),
        in_specs=[pl.BlockSpec(memory_space=pltpu.VMEM)] * (5 + len(before)),
        out_specs=pl.BlockSpec(memory_space=pltpu.VMEM),
        scratch_shapes=[pltpu.VMEM((layers, colors, LANES), jnp.float32)],
        compiler_params=pltpu.CompilerParams(vmem_limit_bytes=48 * MIB),
        name="render",
    )(s, start, table, ambient, backdrop, *before)


def unpack_kernel(groups, width, *refs):
    *pieces, out_ref = refs
    count = len(pieces)
    me = lax.axis_index("gz")
    chunks, colors, _ = pieces[0].shape
    for tile in range(count // groups):
        for chunk in range(chunks):
            values = []
            for part in range(groups):
                values.append(pieces[tile * groups + part][chunk])
            tiles = swap_groups(values, groups, width)
            for part in range(groups):
                out_ref[chunk * groups + part, :, tile * LANES:(tile + 1) * LANES] = tiles[part]


def unpack(pieces, groups, width):
    count, chunks, colors, _ = pieces.shape
    return pl.pallas_call(
        lambda x_ref, out_ref: unpack_kernel(
            groups, width, *[x_ref.at[k] for k in range(count)], out_ref),
        out_shape=jax.ShapeDtypeStruct((chunks * groups, colors, count * width), jnp.float32),
        in_specs=[pl.BlockSpec(memory_space=pltpu.VMEM)],
        out_specs=pl.BlockSpec(memory_space=pltpu.VMEM),
        name="unpack",
    )(pieces)


def exchange(value, axis, apart):
    pairs = [(source, source ^ apart) for source in range(lax.axis_size(axis))]
    return lax.ppermute(value, axis, pairs)


def local(density, bin_rows, tf_extinction, tf_color, extinction_scale, ambient, backdrop):
    rows_x, depth, width_y = density.shape
    colors = tf_color.shape[1]
    bins = bin_rows.shape[0]
    count = lax.axis_size("gz")
    size_x = lax.axis_size("gx")
    me = lax.axis_index("gz")
    width = width_y // count
    groups = LANES // width
    steps = rows_x // groups
    step_x = 1.0 / (rows_x * size_x)
    step_z = 1.0 / (depth * count)

    up = [(i, i + 1) for i in range(size_x - 1)]
    down = [(j, i) for i, j in up]
    before = lax.ppermute(density[rows_x - 1:], "gx", up)
    after = lax.ppermute(density[:1], "gx", down)

    packed = pack(density, groups, width)
    received = []
    for apart in range(count - 1, 0, -1):
        give = lax.dynamic_index_in_dim(packed, me ^ apart, 0, keepdims=False)
        received.insert(0, exchange(give, "gz", apart))
    middle = jnp.zeros((groups - 2,) + density.shape[1:], jnp.float32)
    halo = pack(jnp.concatenate([before, middle, after], axis=0), groups, width)
    halo = lax.all_to_all(halo[:, 0], "gz", 0, 0)

    both = jnp.concatenate([tf_extinction, tf_color], axis=1)
    onehot = (bin_rows[:, None] == jnp.arange(both.shape[0], dtype=jnp.int32)[None, :]).astype(
        jnp.float32)
    table = jnp.dot(onehot, both, precision=lax.Precision.HIGHEST,
                    preferred_element_type=jnp.float32)
    rises = jnp.concatenate([table[:1], table[1:] - table[:-1]], axis=0).T
    rise_sigma = rises[:colors] * extinction_scale[:, None]
    rise_all = jnp.concatenate([rise_sigma * (-step_z * LOG2E), rises[colors:]], axis=0)
    coarse = lax.reduce_precision(rise_all, 8, 7)
    fine = rise_all - coarse
    split = jnp.concatenate([coarse, fine, coarse], axis=1).astype(jnp.bfloat16)

    s, start, total = depths(
        packed, received, halo, rise_sigma * (-step_x * LOG2E), groups, width, bins)
    sums = []
    for hop in range(1, size_x):
        sums.append(lax.ppermute(total, "gx", [(i, i + hop) for i in range(size_x - hop)]))

    ambient = jnp.broadcast_to(ambient[:, None], (colors, LANES))
    backdrop = jnp.broadcast_to(backdrop[:, None], (colors, LANES))
    halves = [
        render(s, start, split, ambient, backdrop, sums, groups, width, bins, step_x / step_z, turn)
        for turn in range(2)
    ]
    share = steps // 2
    if share % groups == 0:
        parts = [pack_image(half, groups, width) for half in halves]
        got = []
        for apart in range(count):
            give = lax.dynamic_index_in_dim(
                parts[apart % 2], (me ^ apart) // 2, 0, keepdims=False)
            got.append(exchange(give, "gz", apart) if apart else give)
        pieces = jnp.stack(got)[jnp.arange(count) ^ me]
        return unpack(pieces, groups, width)
    even = me % 2 == 0
    image = jnp.stack([jnp.where(even, halves[0], halves[1]),
                       jnp.where(even, halves[1], halves[0])])
    image = image.reshape(2, share, colors, groups, width).transpose(3, 0, 1, 2, 4)
    image = lax.all_to_all(image.reshape(count, share, colors, width), "gz", 0, 0)
    return image.transpose(1, 2, 0, 3).reshape(share, colors, width_y)


def solution(mesh):
    in_specs = (P("gx", "gz", None), P(), P(), P(), P(), P(), P())
    out_specs = P(("gx", "gz"), None, None)
    return jax.shard_map(local, mesh=mesh, in_specs=in_specs, out_specs=out_specs, check_vma=False)
```

```python
import functools

import jax
import jax.numpy as jnp
from jax import lax
from jax.experimental import pallas as pl
from jax.experimental.pallas import tpu as pltpu
from jax.sharding import PartitionSpec as P

LANES = 128
LOG2E = 1.4426950408889634
MIB = 1 << 20


def group_ids(shape, width):
    return lax.broadcasted_iota(jnp.int32, shape, len(shape) - 1) // width


def swap_groups(tiles, groups, width):
    tiles = list(tiles)
    lane = group_ids(tiles[0].shape, width)
    bit = 1
    while bit < groups:
        upper = (lane & bit) != 0
        shift = bit * width
        for first in range(groups):
            if first & bit:
                continue
            a, b = tiles[first], tiles[first | bit]
            axis = a.ndim - 1
            tiles[first] = jnp.where(upper, pltpu.roll(b, shift, axis), a)
            tiles[first | bit] = jnp.where(upper, b, pltpu.roll(a, LANES - shift, axis))
        bit *= 2
    return tiles


def blur_rows(parts, lane):
    out = []
    for tiles in parts:
        axis = tiles[0].ndim - 1
        up = [pltpu.roll(tile, 1, axis) for tile in tiles]
        down = [pltpu.roll(tile, LANES - 1, axis) for tile in tiles]
        row = []
        for t in range(len(tiles)):
            before = up[t - 1] if t > 0 else jnp.zeros_like(up[0])
            after = down[t + 1] if t + 1 < len(tiles) else jnp.zeros_like(up[0])
            low = jnp.where(lane == 0, before, up[t])
            high = jnp.where(lane == LANES - 1, after, down[t])
            row.append(low + 2.0 * tiles[t] + high)
        out.append(row)
    return out


def pack_kernel(groups, width, x_ref, out_ref):
    tile_count = x_ref.shape[3] // LANES
    steps, depth = x_ref.shape[1], x_ref.shape[2]
    size = 4
    lane = lax.broadcasted_iota(jnp.int32, (size, depth, LANES), 2)

    def body(chunk, carry):
        place = pl.ds(chunk * size, size)
        wide = blur_rows(
            [[x_ref[part, place, :, t * LANES:(t + 1) * LANES] for t in range(tile_count)]
             for part in range(groups)], lane)
        for t in range(tile_count):
            swapped = swap_groups([wide[part][t] for part in range(groups)], groups, width)
            for part in range(groups):
                out_ref[t * groups + part, place] = swapped[part]
        return carry

    lax.fori_loop(0, steps // size, body, 0)


def pack(x, groups, width):
    steps = x.shape[0] // groups
    blocks = x.shape[2] // width
    return pl.pallas_call(
        functools.partial(pack_kernel, groups, width),
        out_shape=jax.ShapeDtypeStruct((blocks, steps, x.shape[1], LANES), jnp.float32),
        in_specs=[pl.BlockSpec(memory_space=pltpu.VMEM)],
        out_specs=pl.BlockSpec(memory_space=pltpu.VMEM),
        compiler_params=pltpu.CompilerParams(vmem_limit_bytes=8 * MIB),
        name="pack",
    )(x.reshape(groups, steps, x.shape[1], x.shape[2]))


def address_kernel(groups, width, packed_ref, before_ref, after_ref, *refs):
    out_refs, halo = refs[:-1], refs[-1]
    count, steps, depth, _ = packed_ref.shape
    me = lax.axis_index("gz")
    tile_count = before_ref.shape[2] // LANES
    lane = lax.broadcasted_iota(jnp.int32, (depth, LANES), 1)
    ends = blur_rows(
        [[ref[0, :, t * LANES:(t + 1) * LANES] for t in range(tile_count)]
         for ref in (before_ref, after_ref)], lane)
    for t in range(tile_count):
        tiles = [ends[0][t]] * (groups - 1) + [ends[1][t]]
        swapped = swap_groups(tiles, groups, width)
        for part in range(groups):
            halo[t * groups + part] = swapped[part]
    for apart in range(count):
        out_refs[apart][0:steps] = packed_ref[me ^ apart]
        out_refs[apart][steps] = halo[me ^ apart]


def address(packed, before, after, groups, width):
    count, steps, depth, _ = packed.shape
    shape = jax.ShapeDtypeStruct((steps + 1, depth, LANES), jnp.float32)
    return pl.pallas_call(
        functools.partial(address_kernel, groups, width),
        out_shape=[shape] * count,
        in_specs=[pl.BlockSpec(memory_space=pltpu.VMEM)] * 3,
        out_specs=[pl.BlockSpec(memory_space=pltpu.VMEM)] * count,
        scratch_shapes=[pltpu.VMEM((count, depth, LANES), jnp.float32)],
        compiler_params=pltpu.CompilerParams(vmem_limit_bytes=8 * MIB),
        name="address",
    )(packed, before, after)


def split_sum(table, wide):
    coarse = wide.astype(jnp.bfloat16)
    fine = (wide - coarse.astype(jnp.float32)).astype(jnp.bfloat16)
    weights = jnp.concatenate([coarse, coarse, fine], axis=0)
    return jnp.dot(table, weights, preferred_element_type=jnp.float32)


def depth_kernel(groups, width, bins, scale, *refs):
    count = len(refs) - 7
    pieces = refs[:count]
    table_ref, s_ref, start_ref, total_ref, raw, sums, halves = refs[count:]
    steps, depth = pieces[0].shape[-3] - 1, pieces[0].shape[-2]
    layers = depth * count
    colors = table_ref.shape[0]
    me = lax.axis_index("gz")
    zeros = jnp.zeros((steps + 2, 8, LANES), jnp.float32)
    raw[:, 0:8, :] = zeros
    raw[:, 8 + layers:16 + layers, :] = zeros
    lane = group_ids((depth, LANES), width)
    for apart in range(count):
        piece = pieces[apart]
        place = pl.ds(pl.multiple_of(8 + (me ^ apart) * depth, 8), depth)
        raw[1:steps + 1, place, :] = piece[0:steps]
        halo = piece[steps]
        low = pltpu.roll(piece[steps - 1], width, 1)
        high = pltpu.roll(piece[0], LANES - width, 1)
        raw[0, place, :] = jnp.where(lane == 0, halo, low)
        raw[steps + 1, place, :] = jnp.where(lane == groups - 1, halo, high)

    def smooth(step, carry):
        v = raw[step] + 2.0 * raw[step + 1] + raw[step + 2]
        size = v.shape[0]
        before = pltpu.roll(v, 1, 0)
        after = pltpu.roll(v, size - 1, 0)
        total = before + 2.0 * v + after
        s_ref[step] = total[8:8 + layers] * (scale / 64.0)
        return carry

    lax.fori_loop(0, steps, smooth, 0, unroll=2)
    edge = lax.broadcasted_iota(jnp.int32, (bins, LANES), 0).astype(jnp.float32) - 1.0
    rows = steps // 2

    def count_layer(z, carry):
        for half in range(2):
            acc = jnp.zeros((bins, LANES), jnp.float32)
            for step in range(rows):
                row = jnp.broadcast_to(s_ref[half * rows + step, pl.ds(z, 1), :], (bins, LANES))
                acc = acc + jnp.minimum(jnp.maximum(row, edge), edge + 1.0)
            sums[half, z] = acc - edge * rows
        return carry

    lax.fori_loop(0, layers, count_layer, 0, unroll=2)
    table = table_ref[...]
    at_once = 8

    def products(chunk, carry):
        wide = [sums[half, chunk * at_once + k] for half in range(2) for k in range(at_once)]
        out = split_sum(table, jnp.concatenate(wide, axis=1))
        for half in range(2):
            for k in range(at_once):
                place = (half * at_once + k) * LANES
                halves[half, chunk * at_once + k] = out[:, place:place + LANES]
        return carry

    lax.fori_loop(0, layers // at_once, products, 0, unroll=2)
    group = group_ids((colors, LANES), width)

    def scan_groups(chunk, carry):
        packed = jnp.zeros((colors, LANES), jnp.float32)
        for k in range(groups):
            z = chunk * groups + k
            first = halves[0, z]
            both = first + halves[1, z]
            inclusive = both
            everything = both
            shift = 1
            while shift < groups:
                moved = pltpu.roll(inclusive, shift * width, 1)
                inclusive = inclusive + jnp.where(group >= shift, moved, 0.0)
                everything = everything + pltpu.roll(everything, shift * width, 1)
                shift *= 2
            begin = inclusive - both
            start_ref[0, z] = begin
            start_ref[1, z] = begin + first
            packed = jnp.where(group == k, everything, packed)
        total_ref[chunk] = packed
        return carry

    lax.fori_loop(0, layers // groups, scan_groups, 0, unroll=4)


def depths(pieces, table, groups, width, bins):
    count = len(pieces)
    steps, depth = pieces[0].shape[0] - 1, pieces[0].shape[1]
    layers = count * depth
    colors = table.shape[0]
    return pl.pallas_call(
        functools.partial(depth_kernel, groups, width, bins, float(bins - 1)),
        out_shape=(
            jax.ShapeDtypeStruct((steps, layers, LANES), jnp.float32),
            jax.ShapeDtypeStruct((2, layers, colors, LANES), jnp.float32),
            jax.ShapeDtypeStruct((layers // groups, colors, LANES), jnp.float32),
        ),
        in_specs=[pl.BlockSpec(memory_space=pltpu.VMEM)] * (count + 1),
        out_specs=[pl.BlockSpec(memory_space=pltpu.VMEM)] * 3,
        scratch_shapes=[
            pltpu.VMEM((steps + 2, layers + 16, LANES), jnp.float32),
            pltpu.VMEM((2, layers, bins, LANES), jnp.float32),
            pltpu.VMEM((2, layers, colors, LANES), jnp.float32),
        ],
        compiler_params=pltpu.CompilerParams(
            vmem_limit_bytes=8 * MIB + layers * (LANES * 4 * 2) * (bins + 2 * colors)),
        name="depths",
    )(*pieces, table)


def render_kernel(groups, width, bins, ratio, turn, sums_count, s_ref, start_ref, table_ref,
                  columns_ref, *refs):
    before_refs = refs[:sums_count]
    out_refs, image, depth = refs[sums_count:-2], refs[-2], refs[-1]
    steps, layers, _ = s_ref.shape
    rows = steps // 2
    colors = columns_ref.shape[1]
    me = lax.axis_index("gz")
    half = (me + turn) % 2
    group = group_ids((colors, LANES), width)

    def begin(chunk, carry):
        packed = before_refs[0][chunk]
        for ref in before_refs[1:]:
            packed = packed + ref[chunk]
        for k in range(groups):
            z = chunk * groups + k
            value = jnp.where(group == k, packed, 0.0)
            shift = 1
            while shift < groups:
                value = value + pltpu.roll(value, shift * width, 1)
                shift *= 2
            depth[z] = start_ref[half, z] + value
        return carry

    lax.fori_loop(0, layers // groups, begin, 0, unroll=4)
    ambient = columns_ref[1]
    table = table_ref[...]
    edge = (lax.broadcasted_iota(jnp.int32, (bins, LANES), 0).astype(jnp.float32) - 1.0).astype(
        jnp.bfloat16)
    zero = jnp.zeros((bins, LANES), jnp.bfloat16)
    one = jnp.ones((bins, LANES), jnp.bfloat16)
    block = 8

    def advance(step, carry):
        row = half * rows + step

        def layer_block(chunk, state):
            through, partial = state
            place = pl.multiple_of(chunk * block, block)
            s = s_ref[row, pl.ds(place, block), :]
            lower = jnp.floor(s)
            frac = s - lower
            coarse = frac.astype(jnp.bfloat16).astype(jnp.float32)
            fine = frac - coarse

            def wide(value, r):
                return jnp.broadcast_to(value[r:r + 1], (bins, LANES)).astype(jnp.bfloat16)

            columns = []
            for r in range(block):
                away = wide(lower, r) - edge
                main = jnp.minimum(jnp.maximum(away + wide(coarse, r), zero), one)
                rest = jnp.where(away == zero, wide(fine, r), zero)
                columns.append(jnp.concatenate([main, main, rest], axis=0))
            weights = jnp.concatenate(columns, axis=1)
            props = jnp.dot(table, weights, preferred_element_type=jnp.float32)
            for r in range(block):
                part = props[:, r * LANES:(r + 1) * LANES]
                sigma, color = part[:colors], part[colors:]
                later = through * jnp.exp2(sigma)
                z = place + r
                above = depth[z]
                shade = color * (ambient + jnp.exp2(above))
                partial = partial + (through - later) * shade
                depth[z] = above + sigma * ratio
                through = later
            return through, partial

        state = (jnp.ones((colors, LANES), jnp.float32), jnp.zeros((colors, LANES), jnp.float32))
        through, partial = lax.fori_loop(0, layers // block, layer_block, state, unroll=True)
        image[step] = partial + through * columns_ref[2]
        return carry

    lax.fori_loop(0, rows, advance, 0)
    if len(out_refs) == 1:
        out_refs[0][...] = image[...]
        return
    for chunk in range(rows // groups):
        place = pl.ds(chunk * groups, groups)
        tiles = swap_groups([image[chunk * groups + k] for k in range(groups)], groups, width)
        for part in range(groups):
            image[chunk * groups + part] = tiles[part]
    for slot in range(groups):
        part = slot ^ (me // 2)
        for chunk in range(rows // groups):
            out_refs[slot][chunk] = image[chunk * groups + part]


def render(s, start, table, columns, before, groups, width, bins, ratio, turn):
    steps, layers, _ = s.shape
    colors = columns.shape[1]
    share = steps // 2
    if share % groups == 0:
        shapes = [jax.ShapeDtypeStruct((share // groups, colors, LANES), jnp.float32)] * groups
    else:
        shapes = [jax.ShapeDtypeStruct((share, colors, LANES), jnp.float32)]
    return pl.pallas_call(
        functools.partial(render_kernel, groups, width, bins, ratio, turn, len(before)),
        out_shape=shapes,
        in_specs=[pl.BlockSpec(memory_space=pltpu.VMEM)] * (4 + len(before)),
        out_specs=[pl.BlockSpec(memory_space=pltpu.VMEM)] * len(shapes),
        scratch_shapes=[
            pltpu.VMEM((share, colors, LANES), jnp.float32),
            pltpu.VMEM((layers, colors, LANES), jnp.float32),
        ],
        compiler_params=pltpu.CompilerParams(vmem_limit_bytes=8 * MIB + layers * colors * 512 * 4),
        name="render",
    )(s, start, table, columns, *before)


def unpack_kernel(groups, width, *refs):
    arrived, out_ref, pieces = refs[:-2], refs[-2], refs[-1]
    count = len(arrived)
    me = lax.axis_index("gz")
    for apart in range(count):
        pieces[me ^ apart] = arrived[apart][...]
    for tile in range(count // groups):
        for chunk in range(arrived[0].shape[0]):
            tiles = swap_groups(
                [pieces[tile * groups + part, chunk] for part in range(groups)], groups, width)
            for part in range(groups):
                out_ref[chunk * groups + part, :, tile * LANES:(tile + 1) * LANES] = tiles[part]


def unpack(arrived, groups, width):
    count = len(arrived)
    chunks, colors, _ = arrived[0].shape
    return pl.pallas_call(
        functools.partial(unpack_kernel, groups, width),
        out_shape=jax.ShapeDtypeStruct((chunks * groups, colors, count * width), jnp.float32),
        in_specs=[pl.BlockSpec(memory_space=pltpu.VMEM)] * count,
        out_specs=pl.BlockSpec(memory_space=pltpu.VMEM),
        scratch_shapes=[pltpu.VMEM((count, chunks, colors, LANES), jnp.float32)],
        compiler_params=pltpu.CompilerParams(vmem_limit_bytes=8 * MIB),
        name="unpack",
    )(*arrived)


def table_kernel(step_x, step_z, bins_ref, extinction_ref, color_ref, columns_ref, sum_ref,
                 split_ref):
    rows, bins = extinction_ref.shape[1], bins_ref.shape[1]
    colors = extinction_ref.shape[0]
    row = lax.broadcasted_iota(jnp.int32, (rows, bins), 0)
    bin_id = lax.broadcasted_iota(jnp.int32, (rows, bins), 1)
    here = (row == bins_ref[0:1, :]).astype(jnp.float32)
    below = ((row == bins_ref[1:2, :]) & (bin_id > 0)).astype(jnp.float32)

    def rise(ref):
        now = jnp.dot(ref[...], here, precision=lax.Precision.HIGHEST,
                      preferred_element_type=jnp.float32)
        then = jnp.dot(ref[...], below, precision=lax.Precision.HIGHEST,
                       preferred_element_type=jnp.float32)
        return now - then

    def split(value):
        coarse = value.astype(jnp.bfloat16)
        fine = (value - coarse.astype(jnp.float32)).astype(jnp.bfloat16)
        return jnp.concatenate([coarse, fine, coarse], axis=1)

    sigma = rise(extinction_ref) * columns_ref[0, :, 0:bins]
    sum_ref[...] = split(sigma * (-step_x * LOG2E))
    split_ref[0:colors] = split(sigma * (-step_z * LOG2E))
    split_ref[colors:2 * colors] = split(rise(color_ref))


def tables(bin_rows, tf_extinction, tf_color, columns, step_x, step_z):
    bins = bin_rows.shape[0]
    colors = tf_color.shape[1]
    shifted = jnp.stack([bin_rows, jnp.roll(bin_rows, 1)])
    return pl.pallas_call(
        functools.partial(table_kernel, step_x, step_z),
        out_shape=(
            jax.ShapeDtypeStruct((colors, 3 * bins), jnp.bfloat16),
            jax.ShapeDtypeStruct((2 * colors, 3 * bins), jnp.bfloat16),
        ),
        in_specs=[pl.BlockSpec(memory_space=pltpu.VMEM)] * 4,
        out_specs=[pl.BlockSpec(memory_space=pltpu.VMEM)] * 2,
        compiler_params=pltpu.CompilerParams(vmem_limit_bytes=4 * MIB),
        name="tables",
    )(shifted, tf_extinction.T, tf_color.T, columns)


def exchange(value, axis, apart):
    pairs = [(source, source ^ apart) for source in range(lax.axis_size(axis))]
    return lax.ppermute(value, axis, pairs)


def local(density, bin_rows, tf_extinction, tf_color, extinction_scale, ambient, backdrop):
    rows_x, depth, width_y = density.shape
    colors = tf_color.shape[1]
    bins = bin_rows.shape[0]
    count = lax.axis_size("gz")
    size_x = lax.axis_size("gx")
    me = lax.axis_index("gz")
    width = width_y // count
    groups = LANES // width
    steps = rows_x // groups
    step_x = 1.0 / (rows_x * size_x)
    step_z = 1.0 / (depth * count)

    up = [(i, i + 1) for i in range(size_x - 1)]
    down = [(j, i) for i, j in up]
    before = lax.ppermute(density[rows_x - 1:], "gx", up)
    after = lax.ppermute(density[:1], "gx", down)

    packed = pack(density, groups, width)
    pieces = list(address(packed, before, after, groups, width))
    for apart in range(count - 1, 0, -1):
        pieces[apart] = exchange(pieces[apart], "gz", apart)
    columns = jnp.broadcast_to(
        jnp.stack([extinction_scale, ambient, backdrop])[:, :, None], (3, colors, LANES))
    sum_table, table = tables(bin_rows, tf_extinction, tf_color, columns, step_x, step_z)

    s, start, total = depths(pieces, sum_table, groups, width, bins)
    sums = []
    for hop in range(1, size_x):
        sums.append(lax.ppermute(total, "gx", [(i, i + hop) for i in range(size_x - hop)]))

    halves = [
        render(s, start, table, columns, sums, groups, width, bins, step_x / step_z, turn)
        for turn in range(2)
    ]
    share = steps // 2
    if share % groups == 0:
        arrived = []
        for apart in range(count):
            give = halves[apart % 2][apart // 2]
            arrived.append(exchange(give, "gz", apart) if apart else give)
        return unpack(arrived, groups, width)
    halves = [half[0] for half in halves]
    even = me % 2 == 0
    image = jnp.stack([jnp.where(even, halves[0], halves[1]),
                       jnp.where(even, halves[1], halves[0])])
    image = image.reshape(2, share, colors, groups, width).transpose(3, 0, 1, 2, 4)
    image = lax.all_to_all(image.reshape(count, share, colors, width), "gz", 0, 0)
    return image.transpose(1, 2, 0, 3).reshape(share, colors, width_y)


def solution(mesh):
    in_specs = (P("gx", "gz", None), P(), P(), P(), P(), P(), P())
    out_specs = P(("gx", "gz"), None, None)
    return jax.shard_map(local, mesh=mesh, in_specs=in_specs, out_specs=out_specs, check_vma=False)
```

```python
import functools

import jax
import jax.numpy as jnp
from jax import lax
from jax.experimental import pallas as pl
from jax.experimental.pallas import tpu as pltpu
from jax.sharding import PartitionSpec as P

LANES = 128
LOG2E = 1.4426950408889634
MIB = 1 << 20


def group_ids(shape, width):
    return lax.broadcasted_iota(jnp.int32, shape, len(shape) - 1) // width


def swap_groups(tiles, groups, width):
    tiles = list(tiles)
    lane = group_ids(tiles[0].shape, width)
    bit = 1
    while bit < groups:
        upper = (lane & bit) != 0
        shift = bit * width
        for first in range(groups):
            if first & bit:
                continue
            a, b = tiles[first], tiles[first | bit]
            axis = a.ndim - 1
            tiles[first] = jnp.where(upper, pltpu.roll(b, shift, axis), a)
            tiles[first | bit] = jnp.where(upper, b, pltpu.roll(a, LANES - shift, axis))
        bit *= 2
    return tiles


def blur_rows(parts, lane):
    out = []
    for tiles in parts:
        axis = tiles[0].ndim - 1
        up = [pltpu.roll(tile, 1, axis) for tile in tiles]
        down = [pltpu.roll(tile, LANES - 1, axis) for tile in tiles]
        row = []
        for t in range(len(tiles)):
            before = up[t - 1] if t > 0 else jnp.zeros_like(up[0])
            after = down[t + 1] if t + 1 < len(tiles) else jnp.zeros_like(up[0])
            low = jnp.where(lane == 0, before, up[t])
            high = jnp.where(lane == LANES - 1, after, down[t])
            row.append(low + 2.0 * tiles[t] + high)
        out.append(row)
    return out


def pack_kernel(groups, width, x_ref, out_ref):
    tile_count = x_ref.shape[3] // LANES
    steps, depth = x_ref.shape[1], x_ref.shape[2]
    size = 4
    lane = lax.broadcasted_iota(jnp.int32, (size, depth, LANES), 2)

    def body(chunk, carry):
        place = pl.ds(chunk * size, size)
        wide = blur_rows(
            [[x_ref[part, place, :, t * LANES:(t + 1) * LANES] for t in range(tile_count)]
             for part in range(groups)], lane)
        for t in range(tile_count):
            swapped = swap_groups([wide[part][t] for part in range(groups)], groups, width)
            for part in range(groups):
                out_ref[t * groups + part, place] = swapped[part]
        return carry

    lax.fori_loop(0, steps // size, body, 0)


def pack(x, groups, width):
    steps = x.shape[0] // groups
    blocks = x.shape[2] // width
    return pl.pallas_call(
        functools.partial(pack_kernel, groups, width),
        out_shape=jax.ShapeDtypeStruct((blocks, steps, x.shape[1], LANES), jnp.float32),
        in_specs=[pl.BlockSpec(memory_space=pltpu.VMEM)],
        out_specs=pl.BlockSpec(memory_space=pltpu.VMEM),
        compiler_params=pltpu.CompilerParams(vmem_limit_bytes=8 * MIB),
        name="pack",
    )(x.reshape(groups, steps, x.shape[1], x.shape[2]))


def address_kernel(groups, width, packed_ref, before_ref, after_ref, *refs):
    out_refs, halo = refs[:-1], refs[-1]
    count, steps, depth, _ = packed_ref.shape
    me = lax.axis_index("gz")
    tile_count = before_ref.shape[2] // LANES
    lane = lax.broadcasted_iota(jnp.int32, (depth, LANES), 1)
    ends = blur_rows(
        [[ref[0, :, t * LANES:(t + 1) * LANES] for t in range(tile_count)]
         for ref in (before_ref, after_ref)], lane)
    for t in range(tile_count):
        tiles = [ends[0][t]] * (groups - 1) + [ends[1][t]]
        swapped = swap_groups(tiles, groups, width)
        for part in range(groups):
            halo[t * groups + part] = swapped[part]
    for apart in range(count):
        out_refs[apart][0:steps] = packed_ref[me ^ apart]
        out_refs[apart][steps] = halo[me ^ apart]


def address(packed, before, after, groups, width):
    count, steps, depth, _ = packed.shape
    shape = jax.ShapeDtypeStruct((steps + 1, depth, LANES), jnp.float32)
    return pl.pallas_call(
        functools.partial(address_kernel, groups, width),
        out_shape=[shape] * count,
        in_specs=[pl.BlockSpec(memory_space=pltpu.VMEM)] * 3,
        out_specs=[pl.BlockSpec(memory_space=pltpu.VMEM)] * count,
        scratch_shapes=[pltpu.VMEM((count, depth, LANES), jnp.float32)],
        compiler_params=pltpu.CompilerParams(vmem_limit_bytes=8 * MIB),
        name="address",
    )(packed, before, after)


def split_sum(table, wide):
    coarse = wide.astype(jnp.bfloat16)
    fine = (wide - coarse.astype(jnp.float32)).astype(jnp.bfloat16)
    weights = jnp.concatenate([coarse, coarse, fine], axis=0)
    return jnp.dot(table, weights, preferred_element_type=jnp.float32)


def depth_kernel(groups, width, bins, scale, far, halves_count, count, *refs):
    pieces = refs[:-7]
    table_ref, s_ref, start_ref, total_ref, raw, sums, products_ref = refs[-7:]
    steps, depth = pieces[0].shape[-3] - 1, pieces[0].shape[-2]
    blocks = count // 2
    layers = depth * blocks
    slots = s_ref.shape[1]
    used = layers + 1 if far else layers
    colors = table_ref.shape[0]
    me = lax.axis_index("gz")
    lower = me < blocks
    lane = group_ids((depth, LANES), width)

    def place_piece(piece, row):
        place = pl.ds(row, depth)
        raw[1:steps + 1, place, :] = piece[0:steps]
        halo = piece[steps]
        low = pltpu.roll(piece[steps - 1], width, 1)
        high = pltpu.roll(piece[0], LANES - width, 1)
        raw[0, place, :] = jnp.where(lane == 0, halo, low)
        raw[steps + 1, place, :] = jnp.where(lane == groups - 1, halo, high)

    zeros = jnp.zeros((steps + 2, depth, LANES), jnp.float32)
    raw[:, 0:depth, :] = zeros
    raw[:, depth + layers:2 * depth + layers, :] = zeros
    for apart in range(len(pieces)):
        block = (me ^ apart) % blocks
        if far and apart < blocks:
            @pl.when(block == jnp.where(lower, blocks - 1, 0))
            def _():
                row = jnp.where(lower, 0, depth + layers)
                place_piece(pieces[apart], pl.multiple_of(row, 8))
        else:
            place_piece(pieces[apart], pl.multiple_of(depth + block * depth, 8))
    slot = lax.broadcasted_iota(jnp.int32, (layers + depth, LANES), 0)
    if far:
        empty = slot > layers
        if slots > layers + depth:
            s_ref[:, layers + depth:slots, :] = jnp.full(
                (steps, slots - layers - depth, LANES), -1.0, jnp.float32)
    else:
        empty = (slot == jnp.where(lower, layers - 1, 0))[:layers]

    def smooth(step, carry):
        v = raw[step] + 2.0 * raw[step + 1] + raw[step + 2]
        size = v.shape[0]
        before = pltpu.roll(v, 1, 0)
        after = pltpu.roll(v, size - 1, 0)
        total = (before + 2.0 * v + after) * (scale / 64.0)
        if far:
            shifted = pltpu.roll(total, size - (depth - 1), 0)[:layers + depth]
            value = jnp.where(lower, shifted, total[depth:2 * depth + layers])
            s_ref[step, 0:layers + depth] = jnp.where(empty, -1.0, value)
        else:
            s_ref[step] = jnp.where(empty, -1.0, total[depth:depth + layers])
        return carry

    lax.fori_loop(0, steps, smooth, 0, unroll=2)
    edge = lax.broadcasted_iota(jnp.int32, (bins, LANES), 0).astype(jnp.float32) - 1.0
    rows = steps // halves_count

    def count_layer(z, carry):
        for half in range(halves_count):
            acc = jnp.zeros((bins, LANES), jnp.float32)
            for step in range(rows):
                row = jnp.broadcast_to(s_ref[half * rows + step, pl.ds(z, 1), :], (bins, LANES))
                acc = acc + jnp.minimum(jnp.maximum(row, edge), edge + 1.0)
            sums[half, z] = acc - edge * rows
        return carry

    lax.fori_loop(0, layers, count_layer, 0, unroll=2)
    for z in range(layers, slots):
        if z < used:
            count_layer(z, 0)
        else:
            for half in range(halves_count):
                sums[half, z] = jnp.zeros((bins, LANES), jnp.float32)
    table = table_ref[...]
    at_once = 8

    def products(chunk, carry):
        wide = [sums[half, chunk * at_once + k]
                for half in range(halves_count) for k in range(at_once)]
        out = split_sum(table, jnp.concatenate(wide, axis=1))
        for half in range(halves_count):
            for k in range(at_once):
                place = (half * at_once + k) * LANES
                products_ref[half, chunk * at_once + k] = out[:, place:place + LANES]
        return carry

    lax.fori_loop(0, slots // at_once, products, 0, unroll=2)
    group = group_ids((colors, LANES), width)

    def scan_groups(chunk, carry):
        packed = jnp.zeros((colors, LANES), jnp.float32)
        for k in range(groups):
            z = chunk * groups + k
            first = products_ref[0, z]
            both = first
            for half in range(1, halves_count):
                both = both + products_ref[half, z]
            inclusive = both
            everything = both
            shift = 1
            while shift < groups:
                moved = pltpu.roll(inclusive, shift * width, 1)
                inclusive = inclusive + jnp.where(group >= shift, moved, 0.0)
                everything = everything + pltpu.roll(everything, shift * width, 1)
                shift *= 2
            begin = inclusive - both
            start_ref[0, z] = begin
            if halves_count > 1:
                start_ref[1, z] = begin + first
            packed = jnp.where(group == k, everything, packed)
        total_ref[chunk] = packed
        return carry

    lax.fori_loop(0, slots // groups, scan_groups, 0, unroll=4)


def depths(pieces, table, groups, width, bins, far, count):
    steps, depth = pieces[0].shape[0] - 1, pieces[0].shape[1]
    layers = depth * (count // 2)
    slots = layers + max(groups, depth) if far else layers
    halves = 2 if far else 1
    colors = table.shape[0]
    limit = 8 * MIB + slots * (LANES * 4 * halves) * (bins + 2 * colors)
    work = steps * slots * LANES * bins
    return pl.pallas_call(
        functools.partial(depth_kernel, groups, width, bins, float(bins - 1), far, halves, count),
        out_shape=(
            jax.ShapeDtypeStruct((steps, slots, LANES), jnp.float32),
            jax.ShapeDtypeStruct((halves, slots, colors, LANES), jnp.float32),
            jax.ShapeDtypeStruct((slots // groups, colors, LANES), jnp.float32),
        ),
        in_specs=[pl.BlockSpec(memory_space=pltpu.VMEM)] * (len(pieces) + 1),
        out_specs=[pl.BlockSpec(memory_space=pltpu.VMEM)] * 3,
        scratch_shapes=[
            pltpu.VMEM((steps + 2, layers + 2 * depth, LANES), jnp.float32),
            pltpu.VMEM((halves, slots, bins, LANES), jnp.float32),
            pltpu.VMEM((halves, slots, colors, LANES), jnp.float32),
        ],
        compiler_params=pltpu.CompilerParams(vmem_limit_bytes=limit),
        cost_estimate=pl.CostEstimate(
            flops=4 * work, bytes_accessed=8 * steps * slots * LANES, transcendentals=0),
        name="depths_far" if far else "depths_near",
    )(*pieces, table)


def render_kernel(groups, width, bins, ratio, turn, near, blocks, sums_count, s_ref, start_ref,
                  table_ref, columns_ref, *refs):
    before_refs = refs[:sums_count]
    near_refs, refs = refs[sums_count:sums_count + near], refs[sums_count + near:]
    out_refs, image, depth = refs[:-2], refs[-2], refs[-1]
    rows, slots = image.shape[0], s_ref.shape[1]
    colors = columns_ref.shape[1]
    block = 8
    me = lax.axis_index("gz")
    lower = me < blocks
    half = 0 if turn is None else (me + turn) % 2
    group = group_ids((colors, LANES), width)

    def begin(chunk, carry):
        packed = before_refs[0][chunk]
        for ref in before_refs[1:]:
            packed = packed + ref[chunk]
        for k in range(groups):
            z = chunk * groups + k
            value = jnp.where(group == k, packed, 0.0)
            shift = 1
            while shift < groups:
                value = value + pltpu.roll(value, shift * width, 1)
                shift *= 2
            depth[z] = start_ref[half, z] + value
        return carry

    lax.fori_loop(0, slots // groups, begin, 0, unroll=4)
    ambient = columns_ref[1]
    table = table_ref[...]
    edge = (lax.broadcasted_iota(jnp.int32, (bins, LANES), 0).astype(jnp.float32) - 1.0).astype(
        jnp.bfloat16)
    zero = jnp.zeros((bins, LANES), jnp.bfloat16)
    one = jnp.ones((bins, LANES), jnp.bfloat16)
    layers = blocks * block

    def advance(step, carry):
        row = half * rows + step

        def layer_block(place, size, state):
            through, partial = state
            s = s_ref[row, pl.ds(place, block), :]
            lower_bin = jnp.floor(s)
            frac = s - lower_bin
            coarse = frac.astype(jnp.bfloat16).astype(jnp.float32)
            fine = frac - coarse

            def wide(value, r):
                return jnp.broadcast_to(value[r:r + 1], (bins, LANES)).astype(jnp.bfloat16)

            columns = []
            for r in range(size):
                away = wide(lower_bin, r) - edge
                main = jnp.minimum(jnp.maximum(away + wide(coarse, r), zero), one)
                rest = jnp.where(away == zero, wide(fine, r), zero)
                columns.append(jnp.concatenate([main, main, rest], axis=0))
            weights = jnp.concatenate(columns, axis=1)
            props = jnp.dot(table, weights, preferred_element_type=jnp.float32)
            for r in range(size):
                part = props[:, r * LANES:(r + 1) * LANES]
                sigma, color = part[:colors], part[colors:]
                later = through * jnp.exp2(sigma)
                z = place + r
                above = depth[z]
                shade = color * (ambient + jnp.exp2(above))
                partial = partial + (through - later) * shade
                depth[z] = above + sigma * ratio
                through = later
            return through, partial

        state = (jnp.ones((colors, LANES), jnp.float32), jnp.zeros((colors, LANES), jnp.float32))
        for chunk in range(blocks):
            state = layer_block(chunk * block, block, state)
        if turn is None:
            out_refs[0][step], out_refs[1][step] = state[1], state[0]
            return carry
        through, partial = layer_block(layers, 1, state)
        near_partial, near_through = near_refs[0][row], near_refs[1][row]
        front = jnp.where(lower, near_partial, partial)
        back = jnp.where(lower, partial, near_partial)
        passed = jnp.where(lower, near_through, through)
        image[step] = front + passed * back + through * near_through * columns_ref[2]
        return carry

    lax.fori_loop(0, rows, advance, 0)
    if turn is None:
        return
    if len(out_refs) == 1:
        out_refs[0][...] = image[...]
        return
    for chunk in range(rows // groups):
        tiles = swap_groups([image[chunk * groups + k] for k in range(groups)], groups, width)
        for part in range(groups):
            image[chunk * groups + part] = tiles[part]
    for slot in range(groups):
        part = slot ^ (me // 2)
        for chunk in range(rows // groups):
            out_refs[slot][chunk] = image[chunk * groups + part]


def render(s, start, table, columns, before, near, groups, width, bins, ratio, turn, blocks):
    steps, slots, _ = s.shape
    colors = columns.shape[1]
    share = steps // 2
    if turn is None:
        share = steps
        shapes = [jax.ShapeDtypeStruct((steps, colors, LANES), jnp.float32)] * 2
    elif share % groups == 0:
        shapes = [jax.ShapeDtypeStruct((share // groups, colors, LANES), jnp.float32)] * groups
    else:
        shapes = [jax.ShapeDtypeStruct((share, colors, LANES), jnp.float32)]
    work = share * slots * LANES
    return pl.pallas_call(
        functools.partial(render_kernel, groups, width, bins, ratio, turn, len(near), blocks,
                          len(before)),
        out_shape=shapes,
        in_specs=[pl.BlockSpec(memory_space=pltpu.VMEM)] * (4 + len(before) + len(near)),
        out_specs=[pl.BlockSpec(memory_space=pltpu.VMEM)] * len(shapes),
        scratch_shapes=[
            pltpu.VMEM((share, colors, LANES), jnp.float32),
            pltpu.VMEM((slots, colors, LANES), jnp.float32),
        ],
        compiler_params=pltpu.CompilerParams(vmem_limit_bytes=8 * MIB + slots * colors * 512 * 4),
        cost_estimate=pl.CostEstimate(
            flops=work * bins * colors * 12, bytes_accessed=4 * work,
            transcendentals=2 * work * colors),
        name="render_near" if turn is None else "render_far",
    )(s, start, table, columns, *before, *near)


def unpack_kernel(groups, width, *refs):
    arrived, out_ref, pieces = refs[:-2], refs[-2], refs[-1]
    count = len(arrived)
    me = lax.axis_index("gz")
    for apart in range(count):
        pieces[me ^ apart] = arrived[apart][...]
    for tile in range(count // groups):
        for chunk in range(arrived[0].shape[0]):
            tiles = swap_groups(
                [pieces[tile * groups + part, chunk] for part in range(groups)], groups, width)
            for part in range(groups):
                out_ref[chunk * groups + part, :, tile * LANES:(tile + 1) * LANES] = tiles[part]


def unpack(arrived, groups, width):
    count = len(arrived)
    chunks, colors, _ = arrived[0].shape
    return pl.pallas_call(
        functools.partial(unpack_kernel, groups, width),
        out_shape=jax.ShapeDtypeStruct((chunks * groups, colors, count * width), jnp.float32),
        in_specs=[pl.BlockSpec(memory_space=pltpu.VMEM)] * count,
        out_specs=pl.BlockSpec(memory_space=pltpu.VMEM),
        scratch_shapes=[pltpu.VMEM((count, chunks, colors, LANES), jnp.float32)],
        compiler_params=pltpu.CompilerParams(vmem_limit_bytes=8 * MIB),
        name="unpack",
    )(*arrived)


def table_kernel(step_x, step_z, bins_ref, extinction_ref, color_ref, columns_ref, sum_ref,
                 split_ref):
    rows, bins = extinction_ref.shape[1], bins_ref.shape[1]
    colors = extinction_ref.shape[0]
    row = lax.broadcasted_iota(jnp.int32, (rows, bins), 0)
    bin_id = lax.broadcasted_iota(jnp.int32, (rows, bins), 1)
    here = (row == bins_ref[0:1, :]).astype(jnp.float32)
    below = ((row == bins_ref[1:2, :]) & (bin_id > 0)).astype(jnp.float32)

    def rise(ref):
        now = jnp.dot(ref[...], here, precision=lax.Precision.HIGHEST,
                      preferred_element_type=jnp.float32)
        then = jnp.dot(ref[...], below, precision=lax.Precision.HIGHEST,
                       preferred_element_type=jnp.float32)
        return now - then

    def split(value):
        coarse = value.astype(jnp.bfloat16)
        fine = (value - coarse.astype(jnp.float32)).astype(jnp.bfloat16)
        return jnp.concatenate([coarse, fine, coarse], axis=1)

    sigma = rise(extinction_ref) * columns_ref[0, :, 0:bins]
    sum_ref[...] = split(sigma * (-step_x * LOG2E))
    split_ref[0:colors] = split(sigma * (-step_z * LOG2E))
    split_ref[colors:2 * colors] = split(rise(color_ref))


def tables(bin_rows, tf_extinction, tf_color, columns, step_x, step_z):
    bins = bin_rows.shape[0]
    colors = tf_color.shape[1]
    shifted = jnp.stack([bin_rows, jnp.roll(bin_rows, 1)])
    return pl.pallas_call(
        functools.partial(table_kernel, step_x, step_z),
        out_shape=(
            jax.ShapeDtypeStruct((colors, 3 * bins), jnp.bfloat16),
            jax.ShapeDtypeStruct((2 * colors, 3 * bins), jnp.bfloat16),
        ),
        in_specs=[pl.BlockSpec(memory_space=pltpu.VMEM)] * 4,
        out_specs=[pl.BlockSpec(memory_space=pltpu.VMEM)] * 2,
        compiler_params=pltpu.CompilerParams(vmem_limit_bytes=4 * MIB),
        name="tables",
    )(shifted, tf_extinction.T, tf_color.T, columns)


def exchange(value, axis, apart):
    pairs = [(source, source ^ apart) for source in range(lax.axis_size(axis))]
    return lax.ppermute(value, axis, pairs)


def local(density, bin_rows, tf_extinction, tf_color, extinction_scale, ambient, backdrop):
    rows_x, depth, width_y = density.shape
    colors = tf_color.shape[1]
    bins = bin_rows.shape[0]
    count = lax.axis_size("gz")
    size_x = lax.axis_size("gx")
    me = lax.axis_index("gz")
    width = width_y // count
    groups = LANES // width
    steps = rows_x // groups
    step_x = 1.0 / (rows_x * size_x)
    step_z = 1.0 / (depth * count)

    up = [(i, i + 1) for i in range(size_x - 1)]
    down = [(j, i) for i, j in up]
    before = lax.ppermute(density[rows_x - 1:], "gx", up)
    after = lax.ppermute(density[:1], "gx", down)

    packed = pack(density, groups, width)
    pieces = list(address(packed, before, after, groups, width))
    for apart in range(1, count):
        pieces[apart] = exchange(pieces[apart], "gz", apart)
    columns = jnp.broadcast_to(
        jnp.stack([extinction_scale, ambient, backdrop])[:, :, None], (3, colors, LANES))
    sum_table, table = tables(bin_rows, tf_extinction, tf_color, columns, step_x, step_z)

    def prefixes(total):
        return [lax.ppermute(total, "gx", [(i, i + hop) for i in range(size_x - hop)])
                for hop in range(1, size_x)]

    blocks = count // 2
    ratio = step_x / step_z
    s, start, total = depths(pieces[:blocks], sum_table, groups, width, bins, False, count)
    near = render(s, start, table, columns, prefixes(total), [], groups, width, bins, ratio,
                  None, blocks)
    s, start, total = depths(pieces, sum_table, groups, width, bins, True, count)
    sums = prefixes(total)
    halves = [
        render(s, start, table, columns, sums, near, groups, width, bins, ratio, turn, blocks)
        for turn in range(2)
    ]
    share = steps // 2
    if share % groups == 0:
        arrived = []
        for apart in range(count):
            give = halves[apart % 2][apart // 2]
            arrived.append(exchange(give, "gz", apart) if apart else give)
        return unpack(arrived, groups, width)
    halves = [half[0] for half in halves]
    even = me % 2 == 0
    image = jnp.stack([jnp.where(even, halves[0], halves[1]),
                       jnp.where(even, halves[1], halves[0])])
    image = image.reshape(2, share, colors, groups, width).transpose(3, 0, 1, 2, 4)
    image = lax.all_to_all(image.reshape(count, share, colors, width), "gz", 0, 0)
    return image.transpose(1, 2, 0, 3).reshape(share, colors, width_y)


def solution(mesh):
    in_specs = (P("gx", "gz", None), P(), P(), P(), P(), P(), P())
    out_specs = P(("gx", "gz"), None, None)
    return jax.shard_map(local, mesh=mesh, in_specs=in_specs, out_specs=out_specs, check_vma=False)
```

```python
import functools

import jax
import jax.numpy as jnp
from jax import lax
from jax.experimental import pallas as pl
from jax.experimental.pallas import tpu as pltpu
from jax.sharding import PartitionSpec as P

LANES = 128
LOG2E = 1.4426950408889634
MIB = 1 << 20


def group_ids(shape, width):
    return lax.broadcasted_iota(jnp.int32, shape, len(shape) - 1) // width


def swap_groups(tiles, groups, width):
    tiles = list(tiles)
    lane = group_ids(tiles[0].shape, width)
    bit = 1
    while bit < groups:
        upper = (lane & bit) != 0
        shift = bit * width
        for first in range(groups):
            if first & bit:
                continue
            a, b = tiles[first], tiles[first | bit]
            axis = a.ndim - 1
            tiles[first] = jnp.where(upper, pltpu.roll(b, shift, axis), a)
            tiles[first | bit] = jnp.where(upper, b, pltpu.roll(a, LANES - shift, axis))
        bit *= 2
    return tiles


def blur_rows(parts, lane):
    out = []
    for tiles in parts:
        axis = tiles[0].ndim - 1
        up = [pltpu.roll(tile, 1, axis) for tile in tiles]
        down = [pltpu.roll(tile, LANES - 1, axis) for tile in tiles]
        row = []
        for t in range(len(tiles)):
            before = up[t - 1] if t > 0 else jnp.zeros_like(up[0])
            after = down[t + 1] if t + 1 < len(tiles) else jnp.zeros_like(up[0])
            low = jnp.where(lane == 0, before, up[t])
            high = jnp.where(lane == LANES - 1, after, down[t])
            row.append(low + 2.0 * tiles[t] + high)
        out.append(row)
    return out


def pack_kernel(groups, width, x_ref, out_ref):
    tile_count = x_ref.shape[3] // LANES
    lane = lax.broadcasted_iota(jnp.int32, x_ref.shape[1:3] + (LANES,), 2)
    wide = blur_rows(
        [[x_ref[part, :, :, t * LANES:(t + 1) * LANES] for t in range(tile_count)]
         for part in range(groups)], lane)
    for t in range(tile_count):
        swapped = swap_groups([wide[part][t] for part in range(groups)], groups, width)
        for part in range(groups):
            out_ref[t * groups + part] = swapped[part]


def pack(x, groups, width):
    steps = x.shape[0] // groups
    blocks = x.shape[2] // width
    depth, width_y = x.shape[1:]
    size = 4
    return pl.pallas_call(
        functools.partial(pack_kernel, groups, width),
        grid=(steps // size,),
        out_shape=jax.ShapeDtypeStruct((blocks, steps, depth, LANES), jnp.float32),
        in_specs=[pl.BlockSpec((groups, size, depth, width_y), lambda i: (0, i, 0, 0))],
        out_specs=pl.BlockSpec((blocks, size, depth, LANES), lambda i: (0, i, 0, 0)),
        compiler_params=pltpu.CompilerParams(vmem_limit_bytes=8 * MIB),
        name="pack",
    )(x.reshape(groups, steps, x.shape[1], x.shape[2]))


def address_kernel(groups, width, packed_ref, before_ref, after_ref, *refs):
    out_refs, halo = refs[:-1], refs[-1]
    count, steps, depth, _ = packed_ref.shape
    me = lax.axis_index("gz")
    tile_count = before_ref.shape[2] // LANES
    lane = lax.broadcasted_iota(jnp.int32, (depth, LANES), 1)
    position = lax.axis_index("gx")
    inside = (position > 0, position < lax.axis_size("gx") - 1)
    ends = blur_rows(
        [[jnp.where(there, ref[0, :, t * LANES:(t + 1) * LANES], 0.0) for t in range(tile_count)]
         for ref, there in zip((before_ref, after_ref), inside)], lane)
    for t in range(tile_count):
        tiles = [ends[0][t]] * (groups - 1) + [ends[1][t]]
        swapped = swap_groups(tiles, groups, width)
        for part in range(groups):
            halo[t * groups + part] = swapped[part]
    for apart in range(count):
        out_refs[apart][0:steps] = packed_ref[me ^ apart]
        out_refs[apart][steps] = halo[me ^ apart]


def address(packed, before, after, groups, width):
    count, steps, depth, _ = packed.shape
    shape = jax.ShapeDtypeStruct((steps + 1, depth, LANES), jnp.float32)
    return pl.pallas_call(
        functools.partial(address_kernel, groups, width),
        out_shape=[shape] * count,
        in_specs=[pl.BlockSpec(memory_space=pltpu.VMEM)] * 3,
        out_specs=[pl.BlockSpec(memory_space=pltpu.VMEM)] * count,
        scratch_shapes=[pltpu.VMEM((count, depth, LANES), jnp.float32)],
        compiler_params=pltpu.CompilerParams(vmem_limit_bytes=8 * MIB),
        name="address",
    )(packed, before, after)


def split_sum(table, wide):
    coarse = wide.astype(jnp.bfloat16)
    fine = (wide - coarse.astype(jnp.float32)).astype(jnp.bfloat16)
    weights = jnp.concatenate([coarse, coarse, fine], axis=0)
    return jnp.dot(table, weights, preferred_element_type=jnp.float32)


def depth_kernel(groups, width, bins, scale, far, halves_count, count, *refs):
    pieces = refs[:-8] if far else refs[:-7]
    table_ref, s_ref, start_ref, total_ref, raw, sums, products_ref = refs[-7:]
    steps, depth = pieces[0].shape[-3] - 1, pieces[0].shape[-2]
    blocks = count // 2
    layers = depth * blocks
    slots = s_ref.shape[1]
    used = layers + 1 if far else layers
    colors = table_ref.shape[0]
    me = lax.axis_index("gz")
    lower = me < blocks
    lane = group_ids((depth, LANES), width)

    def place_piece(piece, row):
        place = pl.ds(row, depth)
        raw[1:steps + 1, place, :] = piece[0:steps]
        halo = piece[steps]
        low = pltpu.roll(piece[steps - 1], width, 1)
        high = pltpu.roll(piece[0], LANES - width, 1)
        raw[0, place, :] = jnp.where(lane == 0, halo, low)
        raw[steps + 1, place, :] = jnp.where(lane == groups - 1, halo, high)

    zeros = jnp.zeros((steps + 2, depth, LANES), jnp.float32)
    raw[:, 0:depth, :] = zeros
    raw[:, depth + layers:2 * depth + layers, :] = zeros
    for apart in range(len(pieces)):
        block = (me ^ apart) % blocks
        if far and apart < blocks:
            @pl.when(block == jnp.where(lower, blocks - 1, 0))
            def _():
                row = jnp.where(lower, 0, depth + layers)
                place_piece(pieces[apart], pl.multiple_of(row, 8))
        else:
            place_piece(pieces[apart], pl.multiple_of(depth + block * depth, 8))
    slot = lax.broadcasted_iota(jnp.int32, (layers + depth, LANES), 0)
    if far:
        empty = slot > layers
        if slots > layers + depth:
            s_ref[:, layers + depth:slots, :] = jnp.full(
                (steps, slots - layers - depth, LANES), -1.0, jnp.float32)
    else:
        empty = (slot == jnp.where(lower, layers - 1, 0))[:layers]

    def smooth(step, carry):
        v = raw[step] + 2.0 * raw[step + 1] + raw[step + 2]
        size = v.shape[0]
        before = pltpu.roll(v, 1, 0)
        after = pltpu.roll(v, size - 1, 0)
        total = (before + 2.0 * v + after) * (scale / 64.0)
        if far:
            shifted = pltpu.roll(total, size - (depth - 1), 0)[:layers + depth]
            value = jnp.where(lower, shifted, total[depth:2 * depth + layers])
            s_ref[step, 0:layers + depth] = jnp.where(empty, -1.0, value)
        else:
            s_ref[step] = jnp.where(empty, -1.0, total[depth:depth + layers])
        return carry

    lax.fori_loop(0, steps, smooth, 0, unroll=2)
    edge = lax.broadcasted_iota(jnp.int32, (bins, LANES), 0).astype(jnp.float32) - 1.0
    rows = steps // halves_count

    def count_layer(z, carry):
        for half in range(halves_count):
            acc = jnp.zeros((bins, LANES), jnp.float32)
            for step in range(rows):
                row = jnp.broadcast_to(s_ref[half * rows + step, pl.ds(z, 1), :], (bins, LANES))
                acc = acc + jnp.minimum(jnp.maximum(row, edge), edge + 1.0)
            sums[half, z] = acc - edge * rows
        return carry

    lax.fori_loop(0, layers, count_layer, 0, unroll=2)
    for z in range(layers, slots):
        if z < used:
            count_layer(z, 0)
        else:
            for half in range(halves_count):
                sums[half, z] = jnp.zeros((bins, LANES), jnp.float32)
    table = table_ref[...]
    at_once = 8

    def products(chunk, carry):
        wide = [sums[half, chunk * at_once + k]
                for half in range(halves_count) for k in range(at_once)]
        out = split_sum(table, jnp.concatenate(wide, axis=1))
        for half in range(halves_count):
            for k in range(at_once):
                place = (half * at_once + k) * LANES
                products_ref[half, chunk * at_once + k] = out[:, place:place + LANES]
        return carry

    lax.fori_loop(0, slots // at_once, products, 0, unroll=2)
    group = group_ids((colors, LANES), width)

    def scan_groups(chunk, carry):
        packed = jnp.zeros((colors, LANES), jnp.float32)
        for k in range(groups):
            z = chunk * groups + k
            first = products_ref[0, z]
            both = first
            for half in range(1, halves_count):
                both = both + products_ref[half, z]
            inclusive = both
            everything = both
            shift = 1
            while shift < groups:
                moved = pltpu.roll(inclusive, shift * width, 1)
                inclusive = inclusive + jnp.where(group >= shift, moved, 0.0)
                everything = everything + pltpu.roll(everything, shift * width, 1)
                shift *= 2
            begin = inclusive - both
            start_ref[0, z] = begin
            if halves_count > 1:
                start_ref[1, z] = begin + first
            packed = jnp.where(group == k, everything, packed)
        total_ref[chunk] = packed
        return carry

    lax.fori_loop(0, slots // groups, scan_groups, 0, unroll=4)


def depths(pieces, table, groups, width, bins, far, count, after=()):
    steps, depth = pieces[0].shape[0] - 1, pieces[0].shape[1]
    layers = depth * (count // 2)
    slots = layers + max(groups, depth) if far else layers
    halves = 2 if far else 1
    colors = table.shape[0]
    limit = 8 * MIB + slots * (LANES * 4 * halves) * (bins + 2 * colors)
    return pl.pallas_call(
        functools.partial(depth_kernel, groups, width, bins, float(bins - 1), far, halves, count),
        out_shape=(
            jax.ShapeDtypeStruct((steps, slots, LANES), jnp.float32),
            jax.ShapeDtypeStruct((halves, slots, colors, LANES), jnp.float32),
            jax.ShapeDtypeStruct((slots // groups, colors, LANES), jnp.float32),
        ),
        in_specs=[pl.BlockSpec(memory_space=pltpu.VMEM)] * (len(pieces) + len(after) + 1),
        out_specs=[pl.BlockSpec(memory_space=pltpu.VMEM)] * 3,
        scratch_shapes=[
            pltpu.VMEM((steps + 2, layers + 2 * depth, LANES), jnp.float32),
            pltpu.VMEM((halves, slots, bins, LANES), jnp.float32),
            pltpu.VMEM((halves, slots, colors, LANES), jnp.float32),
        ],
        compiler_params=pltpu.CompilerParams(vmem_limit_bytes=limit),
        cost_estimate=pl.CostEstimate(flops=0, bytes_accessed=0, transcendentals=0),
        name="depths_far" if far else "depths_near",
    )(*pieces, *after, table)


def render_kernel(groups, width, bins, ratio, turn, near, blocks, sums_count, s_ref, start_ref,
                  table_ref, columns_ref, *refs):
    before_refs = refs[:sums_count]
    near_refs, refs = refs[sums_count:sums_count + near], refs[sums_count + near:]
    out_refs, image, depth = refs[:-2], refs[-2], refs[-1]
    rows, slots = image.shape[0], s_ref.shape[1]
    colors = columns_ref.shape[1]
    block = 8
    me = lax.axis_index("gz")
    lower = me < blocks
    half = 0 if turn is None else (me + turn) % 2
    position = lax.axis_index("gx")
    group = group_ids((colors, LANES), width)

    def begin(chunk, carry):
        packed = jnp.zeros((colors, LANES), jnp.float32)
        for hop, ref in enumerate(before_refs, 1):
            packed = packed + jnp.where(position >= hop, ref[chunk], 0.0)
        for k in range(groups):
            z = chunk * groups + k
            value = jnp.where(group == k, packed, 0.0)
            shift = 1
            while shift < groups:
                value = value + pltpu.roll(value, shift * width, 1)
                shift *= 2
            depth[z] = start_ref[half, z] + value
        return carry

    lax.fori_loop(0, slots // groups, begin, 0, unroll=4)
    ambient = columns_ref[1]
    table = table_ref[...]
    edge = (lax.broadcasted_iota(jnp.int32, (bins, LANES), 0).astype(jnp.float32) - 1.0).astype(
        jnp.bfloat16)
    zero = jnp.zeros((bins, LANES), jnp.bfloat16)
    one = jnp.ones((bins, LANES), jnp.bfloat16)
    layers = blocks * block

    def advance(step, carry):
        row = half * rows + step

        def layer_block(place, size, state):
            through, partial = state
            s = s_ref[row, pl.ds(place, block), :]
            lower_bin = jnp.floor(s)
            frac = s - lower_bin
            coarse = frac.astype(jnp.bfloat16).astype(jnp.float32)
            fine = frac - coarse

            def wide(value, r):
                return jnp.broadcast_to(value[r:r + 1], (bins, LANES)).astype(jnp.bfloat16)

            columns = []
            for r in range(size):
                away = wide(lower_bin, r) - edge
                main = jnp.minimum(jnp.maximum(away + wide(coarse, r), zero), one)
                rest = jnp.where(away == zero, wide(fine, r), zero)
                columns.append(jnp.concatenate([main, main, rest], axis=0))
            weights = jnp.concatenate(columns, axis=1)
            props = jnp.dot(table, weights, preferred_element_type=jnp.float32)
            for r in range(size):
                part = props[:, r * LANES:(r + 1) * LANES]
                sigma, color = part[:colors], part[colors:]
                later = through * jnp.exp2(sigma)
                z = place + r
                above = depth[z]
                shade = color * (ambient + jnp.exp2(above))
                partial = partial + (through - later) * shade
                depth[z] = above + sigma * ratio
                through = later
            return through, partial

        state = (jnp.ones((colors, LANES), jnp.float32), jnp.zeros((colors, LANES), jnp.float32))
        for chunk in range(blocks):
            state = layer_block(chunk * block, block, state)
        if turn is None:
            out_refs[0][step], out_refs[1][step] = state[1], state[0]
            return carry
        through, partial = layer_block(layers, 1, state)
        near_partial, near_through = near_refs[0][row], near_refs[1][row]
        front = jnp.where(lower, near_partial, partial)
        back = jnp.where(lower, partial, near_partial)
        passed = jnp.where(lower, near_through, through)
        image[step] = front + passed * back + through * near_through * columns_ref[2]
        return carry

    lax.fori_loop(0, rows, advance, 0, unroll=4 if turn is None else 2)
    if turn is None:
        out_refs[2][...] = jnp.zeros((8, LANES), jnp.float32)
        return
    if len(out_refs) == 1:
        out_refs[0][...] = image[...]
        return
    for chunk in range(rows // groups):
        tiles = swap_groups([image[chunk * groups + k] for k in range(groups)], groups, width)
        for part in range(groups):
            image[chunk * groups + part] = tiles[part]
    for slot in range(groups):
        part = slot ^ (me // 2)
        for chunk in range(rows // groups):
            out_refs[slot][chunk] = image[chunk * groups + part]


def render(s, start, table, columns, before, near, groups, width, bins, ratio, turn, blocks):
    steps, slots, _ = s.shape
    colors = columns.shape[1]
    share = steps // 2
    if turn is None:
        share = steps
        shapes = [jax.ShapeDtypeStruct((steps, colors, LANES), jnp.float32)] * 2
        shapes.append(jax.ShapeDtypeStruct((8, LANES), jnp.float32))
    elif share % groups == 0:
        shapes = [jax.ShapeDtypeStruct((share // groups, colors, LANES), jnp.float32)] * groups
    else:
        shapes = [jax.ShapeDtypeStruct((share, colors, LANES), jnp.float32)]
    return pl.pallas_call(
        functools.partial(render_kernel, groups, width, bins, ratio, turn, len(near), blocks,
                          len(before)),
        out_shape=shapes,
        in_specs=[pl.BlockSpec(memory_space=pltpu.VMEM)] * (4 + len(before) + len(near)),
        out_specs=[pl.BlockSpec(memory_space=pltpu.VMEM)] * len(shapes),
        scratch_shapes=[
            pltpu.VMEM((share, colors, LANES), jnp.float32),
            pltpu.VMEM((slots, colors, LANES), jnp.float32),
        ],
        compiler_params=pltpu.CompilerParams(vmem_limit_bytes=8 * MIB + slots * colors * 512 * 4),
        cost_estimate=pl.CostEstimate(flops=0, bytes_accessed=0, transcendentals=0),
        name="render_near" if turn is None else "render_far",
    )(s, start, table, columns, *before, *near)


def unpack_kernel(groups, width, *refs):
    arrived, out_ref, pieces = refs[:-2], refs[-2], refs[-1]
    count = len(arrived)
    me = lax.axis_index("gz")
    for apart in range(count):
        pieces[me ^ apart] = arrived[apart][...]
    for tile in range(count // groups):
        for chunk in range(arrived[0].shape[0]):
            tiles = swap_groups(
                [pieces[tile * groups + part, chunk] for part in range(groups)], groups, width)
            for part in range(groups):
                out_ref[chunk * groups + part, :, tile * LANES:(tile + 1) * LANES] = tiles[part]


def unpack(arrived, groups, width):
    count = len(arrived)
    chunks, colors, _ = arrived[0].shape
    return pl.pallas_call(
        functools.partial(unpack_kernel, groups, width),
        out_shape=jax.ShapeDtypeStruct((chunks * groups, colors, count * width), jnp.float32),
        in_specs=[pl.BlockSpec(memory_space=pltpu.VMEM)] * count,
        out_specs=pl.BlockSpec(memory_space=pltpu.VMEM),
        scratch_shapes=[pltpu.VMEM((count, chunks, colors, LANES), jnp.float32)],
        compiler_params=pltpu.CompilerParams(vmem_limit_bytes=8 * MIB),
        name="unpack",
    )(*arrived)


def table_kernel(step_x, step_z, bins_ref, extinction_ref, color_ref, columns_ref, sum_ref,
                 split_ref):
    rows, bins = extinction_ref.shape[1], bins_ref.shape[1]
    colors = extinction_ref.shape[0]
    row = lax.broadcasted_iota(jnp.int32, (rows, bins), 0)
    bin_id = lax.broadcasted_iota(jnp.int32, (rows, bins), 1)
    here = (row == bins_ref[0:1, :]).astype(jnp.float32)
    below = ((row == bins_ref[1:2, :]) & (bin_id > 0)).astype(jnp.float32)

    def rise(ref):
        now = jnp.dot(ref[...], here, precision=lax.Precision.HIGHEST,
                      preferred_element_type=jnp.float32)
        then = jnp.dot(ref[...], below, precision=lax.Precision.HIGHEST,
                       preferred_element_type=jnp.float32)
        return now - then

    def split(value):
        coarse = value.astype(jnp.bfloat16)
        fine = (value - coarse.astype(jnp.float32)).astype(jnp.bfloat16)
        return jnp.concatenate([coarse, fine, coarse], axis=1)

    sigma = rise(extinction_ref) * columns_ref[0, :, 0:bins]
    sum_ref[...] = split(sigma * (-step_x * LOG2E))
    split_ref[0:colors] = split(sigma * (-step_z * LOG2E))
    split_ref[colors:2 * colors] = split(rise(color_ref))


def tables(bin_rows, tf_extinction, tf_color, columns, step_x, step_z):
    bins = bin_rows.shape[0]
    colors = tf_color.shape[1]
    shifted = jnp.stack([bin_rows, jnp.roll(bin_rows, 1)])
    return pl.pallas_call(
        functools.partial(table_kernel, step_x, step_z),
        out_shape=(
            jax.ShapeDtypeStruct((colors, 3 * bins), jnp.bfloat16),
            jax.ShapeDtypeStruct((2 * colors, 3 * bins), jnp.bfloat16),
        ),
        in_specs=[pl.BlockSpec(memory_space=pltpu.VMEM)] * 4,
        out_specs=[pl.BlockSpec(memory_space=pltpu.VMEM)] * 2,
        compiler_params=pltpu.CompilerParams(vmem_limit_bytes=4 * MIB),
        name="tables",
    )(shifted, tf_extinction.T, tf_color.T, columns)


def exchange(value, axis, apart):
    pairs = [(source, source ^ apart) for source in range(lax.axis_size(axis))]
    return lax.ppermute(value, axis, pairs)


def local(density, bin_rows, tf_extinction, tf_color, extinction_scale, ambient, backdrop):
    rows_x, depth, width_y = density.shape
    colors = tf_color.shape[1]
    bins = bin_rows.shape[0]
    count = lax.axis_size("gz")
    size_x = lax.axis_size("gx")
    me = lax.axis_index("gz")
    width = width_y // count
    groups = LANES // width
    steps = rows_x // groups
    step_x = 1.0 / (rows_x * size_x)
    step_z = 1.0 / (depth * count)

    up = [(i, (i + 1) % size_x) for i in range(size_x)]
    down = [(j, i) for i, j in up]
    before = lax.ppermute(density[rows_x - 1:], "gx", up)
    after = lax.ppermute(density[:1], "gx", down)

    packed = pack(density, groups, width)
    pieces = list(address(packed, before, after, groups, width))
    for apart in range(1, count):
        give = pieces[apart]
        if apart >= count * 3 // 4:
            give, _ = lax.optimization_barrier((give, pieces[apart - count // 4]))
        pieces[apart] = exchange(give, "gz", apart)
    columns = jnp.broadcast_to(
        jnp.stack([extinction_scale, ambient, backdrop])[:, :, None], (3, colors, LANES))
    sum_table, table = tables(bin_rows, tf_extinction, tf_color, columns, step_x, step_z)

    def prefixes(total):
        return [lax.ppermute(total, "gx", [(i, (i + hop) % size_x) for i in range(size_x)])
                for hop in range(1, size_x)]

    blocks = count // 2
    ratio = step_x / step_z
    s, start, total = depths(pieces[:blocks], sum_table, groups, width, bins, False, count)
    *near, done = render(s, start, table, columns, prefixes(total), [], groups, width, bins, ratio,
                         None, blocks)
    s, start, total = depths(pieces, sum_table, groups, width, bins, True, count, [done])
    sums = prefixes(total)
    halves = [
        render(s, start, table, columns, sums, near, groups, width, bins, ratio, turn, blocks)
        for turn in range(2)
    ]
    share = steps // 2
    if share % groups == 0:
        arrived = []
        for apart in range(count):
            give = halves[apart % 2][apart // 2]
            arrived.append(exchange(give, "gz", apart) if apart else give)
        return unpack(arrived, groups, width)
    halves = [half[0] for half in halves]
    even = me % 2 == 0
    image = jnp.stack([jnp.where(even, halves[0], halves[1]),
                       jnp.where(even, halves[1], halves[0])])
    image = image.reshape(2, share, colors, groups, width).transpose(3, 0, 1, 2, 4)
    image = lax.all_to_all(image.reshape(count, share, colors, width), "gz", 0, 0)
    return image.transpose(1, 2, 0, 3).reshape(share, colors, width_y)


def solution(mesh):
    in_specs = (P("gx", "gz", None), P(), P(), P(), P(), P(), P())
    out_specs = P(("gx", "gz"), None, None)
    return jax.shard_map(local, mesh=mesh, in_specs=in_specs, out_specs=out_specs, check_vma=False)
```

```python
import functools

import jax
import jax.numpy as jnp
from jax import lax
from jax.experimental import pallas as pl
from jax.experimental.pallas import tpu as pltpu
from jax.sharding import PartitionSpec as P

LANES = 128
LOG2E = 1.4426950408889634
MIB = 1 << 20


def group_ids(shape, width):
    return lax.broadcasted_iota(jnp.int32, shape, len(shape) - 1) // width


def swap_groups(tiles, groups, width):
    tiles = list(tiles)
    lane = group_ids(tiles[0].shape, width)
    bit = 1
    while bit < groups:
        upper = (lane & bit) != 0
        shift = bit * width
        for first in range(groups):
            if first & bit:
                continue
            a, b = tiles[first], tiles[first | bit]
            axis = a.ndim - 1
            tiles[first] = jnp.where(upper, pltpu.roll(b, shift, axis), a)
            tiles[first | bit] = jnp.where(upper, b, pltpu.roll(a, LANES - shift, axis))
        bit *= 2
    return tiles


def blur_rows(parts, lane):
    out = []
    for tiles in parts:
        axis = tiles[0].ndim - 1
        up = [pltpu.roll(tile, 1, axis) for tile in tiles]
        down = [pltpu.roll(tile, LANES - 1, axis) for tile in tiles]
        row = []
        for t in range(len(tiles)):
            before = up[t - 1] if t > 0 else jnp.zeros_like(up[0])
            after = down[t + 1] if t + 1 < len(tiles) else jnp.zeros_like(up[0])
            low = jnp.where(lane == 0, before, up[t])
            high = jnp.where(lane == LANES - 1, after, down[t])
            row.append(low + 2.0 * tiles[t] + high)
        out.append(row)
    return out


def pack_kernel(groups, width, x_ref, out_ref):
    tile_count = x_ref.shape[3] // LANES
    lane = lax.broadcasted_iota(jnp.int32, x_ref.shape[1:3] + (LANES,), 2)
    wide = blur_rows(
        [[x_ref[part, :, :, t * LANES:(t + 1) * LANES] for t in range(tile_count)]
         for part in range(groups)], lane)
    for t in range(tile_count):
        swapped = swap_groups([wide[part][t] for part in range(groups)], groups, width)
        for part in range(groups):
            out_ref[t * groups + part] = swapped[part]


def pack(x, groups, width):
    steps = x.shape[0] // groups
    blocks = x.shape[2] // width
    depth, width_y = x.shape[1:]
    size = 4
    return pl.pallas_call(
        functools.partial(pack_kernel, groups, width),
        grid=(steps // size,),
        out_shape=jax.ShapeDtypeStruct((blocks, steps, depth, LANES), jnp.float32),
        in_specs=[pl.BlockSpec((groups, size, depth, width_y), lambda i: (0, i, 0, 0))],
        out_specs=pl.BlockSpec((blocks, size, depth, LANES), lambda i: (0, i, 0, 0)),
        compiler_params=pltpu.CompilerParams(vmem_limit_bytes=8 * MIB),
        name="pack",
    )(x.reshape(groups, steps, x.shape[1], x.shape[2]))


def address_kernel(groups, width, packed_ref, before_ref, after_ref, *refs):
    out_refs, halo = refs[:-1], refs[-1]
    count, steps, depth, _ = packed_ref.shape
    me = lax.axis_index("gz")
    tile_count = before_ref.shape[2] // LANES
    lane = lax.broadcasted_iota(jnp.int32, (depth, LANES), 1)
    position = lax.axis_index("gx")
    inside = (position > 0, position < lax.axis_size("gx") - 1)
    ends = blur_rows(
        [[jnp.where(there, ref[0, :, t * LANES:(t + 1) * LANES], 0.0) for t in range(tile_count)]
         for ref, there in zip((before_ref, after_ref), inside)], lane)
    for t in range(tile_count):
        tiles = [ends[0][t]] * (groups - 1) + [ends[1][t]]
        swapped = swap_groups(tiles, groups, width)
        for part in range(groups):
            halo[t * groups + part] = swapped[part]
    for apart in range(count):
        out_refs[apart][0:steps] = packed_ref[me ^ apart]
        out_refs[apart][steps] = halo[me ^ apart]


def address(packed, before, after, groups, width):
    count, steps, depth, _ = packed.shape
    shape = jax.ShapeDtypeStruct((steps + 1, depth, LANES), jnp.float32)
    return pl.pallas_call(
        functools.partial(address_kernel, groups, width),
        out_shape=[shape] * count,
        in_specs=[pl.BlockSpec(memory_space=pltpu.VMEM)] * 3,
        out_specs=[pl.BlockSpec(memory_space=pltpu.VMEM)] * count,
        scratch_shapes=[pltpu.VMEM((count, depth, LANES), jnp.float32)],
        compiler_params=pltpu.CompilerParams(vmem_limit_bytes=8 * MIB),
        name="address",
    )(packed, before, after)


def split_sum(table, wide):
    coarse = wide.astype(jnp.bfloat16)
    fine = (wide - coarse.astype(jnp.float32)).astype(jnp.bfloat16)
    weights = jnp.concatenate([coarse, coarse, fine], axis=0)
    return jnp.dot(table, weights, preferred_element_type=jnp.float32)


def depth_kernel(groups, width, bins, scale, far, halves_count, count, *refs):
    pieces = refs[:-8] if far else refs[:-7]
    table_ref, s_ref, start_ref, total_ref, raw, sums, products_ref = refs[-7:]
    steps, depth = pieces[0].shape[-3] - 1, pieces[0].shape[-2]
    blocks = count // 2
    layers = depth * blocks
    slots = s_ref.shape[1]
    used = layers + 1 if far else layers
    colors = table_ref.shape[0]
    me = lax.axis_index("gz")
    lower = me < blocks
    lane = group_ids((depth, LANES), width)

    def place_piece(piece, row):
        place = pl.ds(row, depth)
        raw[1:steps + 1, place, :] = piece[0:steps]
        halo = piece[steps]
        low = pltpu.roll(piece[steps - 1], width, 1)
        high = pltpu.roll(piece[0], LANES - width, 1)
        raw[0, place, :] = jnp.where(lane == 0, halo, low)
        raw[steps + 1, place, :] = jnp.where(lane == groups - 1, halo, high)

    zeros = jnp.zeros((steps + 2, depth, LANES), jnp.float32)
    raw[:, 0:depth, :] = zeros
    raw[:, depth + layers:2 * depth + layers, :] = zeros
    for apart in range(len(pieces)):
        block = (me ^ apart) % blocks
        if far and apart < blocks:
            @pl.when(block == jnp.where(lower, blocks - 1, 0))
            def _():
                row = jnp.where(lower, 0, depth + layers)
                place_piece(pieces[apart], pl.multiple_of(row, 8))
        else:
            place_piece(pieces[apart], pl.multiple_of(depth + block * depth, 8))
    slot = lax.broadcasted_iota(jnp.int32, (layers + depth, LANES), 0)
    if far:
        empty = slot > layers
        if slots > layers + depth:
            s_ref[:, layers + depth:slots, :] = jnp.full(
                (steps, slots - layers - depth, LANES), -1.0, jnp.float32)
    else:
        empty = (slot == jnp.where(lower, layers - 1, 0))[:layers]

    def smooth(step, carry):
        v = raw[step] + 2.0 * raw[step + 1] + raw[step + 2]
        size = v.shape[0]
        before = pltpu.roll(v, 1, 0)
        after = pltpu.roll(v, size - 1, 0)
        total = (before + 2.0 * v + after) * (scale / 64.0)
        if far:
            shifted = pltpu.roll(total, size - (depth - 1), 0)[:layers + depth]
            value = jnp.where(lower, shifted, total[depth:2 * depth + layers])
            s_ref[step, 0:layers + depth] = jnp.where(empty, -1.0, value)
        else:
            s_ref[step] = jnp.where(empty, -1.0, total[depth:depth + layers])
        return carry

    lax.fori_loop(0, steps, smooth, 0, unroll=2)
    edge = lax.broadcasted_iota(jnp.int32, (bins, LANES), 0).astype(jnp.float32) - 1.0
    rows = steps // halves_count

    def count_layer(z, carry):
        for half in range(halves_count):
            acc = jnp.zeros((bins, LANES), jnp.float32)
            for step in range(rows):
                row = jnp.broadcast_to(s_ref[half * rows + step, pl.ds(z, 1), :], (bins, LANES))
                acc = acc + jnp.minimum(jnp.maximum(row, edge), edge + 1.0)
            sums[half, z] = acc - edge * rows
        return carry

    lax.fori_loop(0, layers, count_layer, 0, unroll=2)
    for z in range(layers, slots):
        if z < used:
            count_layer(z, 0)
        else:
            for half in range(halves_count):
                sums[half, z] = jnp.zeros((bins, LANES), jnp.float32)
    table = table_ref[...]
    at_once = 8

    def products(chunk, carry):
        wide = [sums[half, chunk * at_once + k]
                for half in range(halves_count) for k in range(at_once)]
        out = split_sum(table, jnp.concatenate(wide, axis=1))
        for half in range(halves_count):
            for k in range(at_once):
                place = (half * at_once + k) * LANES
                products_ref[half, chunk * at_once + k] = out[:, place:place + LANES]
        return carry

    lax.fori_loop(0, slots // at_once, products, 0, unroll=2)
    group = group_ids((colors, LANES), width)

    def scan_groups(chunk, carry):
        packed = jnp.zeros((colors, LANES), jnp.float32)
        for k in range(groups):
            z = chunk * groups + k
            first = products_ref[0, z]
            both = first
            for half in range(1, halves_count):
                both = both + products_ref[half, z]
            inclusive = both
            everything = both
            shift = 1
            while shift < groups:
                moved = pltpu.roll(inclusive, shift * width, 1)
                inclusive = inclusive + jnp.where(group >= shift, moved, 0.0)
                everything = everything + pltpu.roll(everything, shift * width, 1)
                shift *= 2
            begin = inclusive - both
            start_ref[0, z] = begin
            if halves_count > 1:
                start_ref[1, z] = begin + first
            packed = jnp.where(group == k, everything, packed)
        total_ref[chunk] = packed
        return carry

    lax.fori_loop(0, slots // groups, scan_groups, 0, unroll=4)


def depths(pieces, table, groups, width, bins, far, count, after=()):
    steps, depth = pieces[0].shape[0] - 1, pieces[0].shape[1]
    layers = depth * (count // 2)
    slots = layers + max(groups, depth) if far else layers
    halves = 2 if far else 1
    colors = table.shape[0]
    limit = 8 * MIB + slots * (LANES * 4 * halves) * (bins + 2 * colors)
    return pl.pallas_call(
        functools.partial(depth_kernel, groups, width, bins, float(bins - 1), far, halves, count),
        out_shape=(
            jax.ShapeDtypeStruct((steps, slots, LANES), jnp.float32),
            jax.ShapeDtypeStruct((halves, slots, colors, LANES), jnp.float32),
            jax.ShapeDtypeStruct((slots // groups, colors, LANES), jnp.float32),
        ),
        in_specs=[pl.BlockSpec(memory_space=pltpu.VMEM)] * (len(pieces) + len(after) + 1),
        out_specs=[pl.BlockSpec(memory_space=pltpu.VMEM)] * 3,
        scratch_shapes=[
            pltpu.VMEM((steps + 2, layers + 2 * depth, LANES), jnp.float32),
            pltpu.VMEM((halves, slots, bins, LANES), jnp.float32),
            pltpu.VMEM((halves, slots, colors, LANES), jnp.float32),
        ],
        compiler_params=pltpu.CompilerParams(vmem_limit_bytes=limit),
        cost_estimate=pl.CostEstimate(flops=0, bytes_accessed=0, transcendentals=0),
        name="depths_far" if far else "depths_near",
    )(*pieces, *after, table)


def render_kernel(groups, width, bins, ratio, turn, near, blocks, sums_count, s_ref, start_ref,
                  table_ref, columns_ref, *refs):
    before_refs = refs[:sums_count]
    near_refs, refs = refs[sums_count:sums_count + near], refs[sums_count + near:]
    out_refs, image, depth = refs[:-2], refs[-2], refs[-1]
    rows, slots = image.shape[0], s_ref.shape[1]
    colors = columns_ref.shape[1]
    block = 8
    me = lax.axis_index("gz")
    lower = me < blocks
    half = 0 if turn is None else (me + turn) % 2
    position = lax.axis_index("gx")
    group = group_ids((colors, LANES), width)

    def begin(chunk, carry):
        packed = jnp.zeros((colors, LANES), jnp.float32)
        for hop, ref in enumerate(before_refs, 1):
            packed = packed + jnp.where(position >= hop, ref[chunk], 0.0)
        for k in range(groups):
            z = chunk * groups + k
            value = jnp.where(group == k, packed, 0.0)
            shift = 1
            while shift < groups:
                value = value + pltpu.roll(value, shift * width, 1)
                shift *= 2
            depth[z] = start_ref[half, z] + value
        return carry

    lax.fori_loop(0, slots // groups, begin, 0, unroll=4)
    ambient = columns_ref[1]
    table = table_ref[...]
    edge = (lax.broadcasted_iota(jnp.int32, (bins, LANES), 0).astype(jnp.float32) - 1.0).astype(
        jnp.bfloat16)
    zero = jnp.zeros((bins, LANES), jnp.bfloat16)
    one = jnp.ones((bins, LANES), jnp.bfloat16)
    layers = blocks * block

    def advance(step, carry):
        row = half * rows + step

        def layer_block(place, size, state):
            through, partial = state
            s = s_ref[row, pl.ds(place, block), :]
            lower_bin = jnp.floor(s)
            frac = s - lower_bin
            coarse = frac.astype(jnp.bfloat16).astype(jnp.float32)
            fine = frac - coarse

            def wide(value, r):
                return jnp.broadcast_to(value[r:r + 1], (bins, LANES)).astype(jnp.bfloat16)

            columns = []
            for r in range(size):
                away = wide(lower_bin, r) - edge
                main = jnp.minimum(jnp.maximum(away + wide(coarse, r), zero), one)
                rest = jnp.where(away == zero, wide(fine, r), zero)
                columns.append(jnp.concatenate([main, main, rest], axis=0))
            weights = jnp.concatenate(columns, axis=1)
            props = jnp.dot(table, weights, preferred_element_type=jnp.float32)
            for r in range(size):
                part = props[:, r * LANES:(r + 1) * LANES]
                sigma, color = part[:colors], part[colors:]
                later = through * jnp.exp2(sigma)
                z = place + r
                above = depth[z]
                shade = color * (ambient + jnp.exp2(above))
                partial = partial + (through - later) * shade
                depth[z] = above + sigma * ratio
                through = later
            return through, partial

        state = (jnp.ones((colors, LANES), jnp.float32), jnp.zeros((colors, LANES), jnp.float32))
        for chunk in range(blocks):
            state = layer_block(chunk * block, block, state)
        if turn is None:
            out_refs[0][step], out_refs[1][step] = state[1], state[0]
            return carry
        through, partial = layer_block(layers, 1, state)
        near_partial, near_through = near_refs[0][row], near_refs[1][row]
        front = jnp.where(lower, near_partial, partial)
        back = jnp.where(lower, partial, near_partial)
        passed = jnp.where(lower, near_through, through)
        image[step] = front + passed * back + through * near_through * columns_ref[2]
        return carry

    lax.fori_loop(0, rows, advance, 0, unroll=4 if turn is None else 2)
    if turn is None:
        out_refs[2][...] = jnp.zeros((8, LANES), jnp.float32)
        return
    if len(out_refs) == 1:
        out_refs[0][...] = image[...]
        return
    for chunk in range(rows // groups):
        tiles = swap_groups([image[chunk * groups + k] for k in range(groups)], groups, width)
        for part in range(groups):
            image[chunk * groups + part] = tiles[part]
    for slot in range(groups):
        part = slot ^ (me // 2)
        for chunk in range(rows // groups):
            out_refs[slot][chunk] = image[chunk * groups + part]


def render(s, start, table, columns, before, near, groups, width, bins, ratio, turn, blocks):
    steps, slots, _ = s.shape
    colors = columns.shape[1]
    share = steps // 2
    if turn is None:
        share = steps
        shapes = [jax.ShapeDtypeStruct((steps, colors, LANES), jnp.float32)] * 2
        shapes.append(jax.ShapeDtypeStruct((8, LANES), jnp.float32))
    elif share % groups == 0:
        shapes = [jax.ShapeDtypeStruct((share // groups, colors, LANES), jnp.float32)] * groups
    else:
        shapes = [jax.ShapeDtypeStruct((share, colors, LANES), jnp.float32)]
    return pl.pallas_call(
        functools.partial(render_kernel, groups, width, bins, ratio, turn, len(near), blocks,
                          len(before)),
        out_shape=shapes,
        in_specs=[pl.BlockSpec(memory_space=pltpu.VMEM)] * (4 + len(before) + len(near)),
        out_specs=[pl.BlockSpec(memory_space=pltpu.VMEM)] * len(shapes),
        scratch_shapes=[
            pltpu.VMEM((share, colors, LANES), jnp.float32),
            pltpu.VMEM((slots, colors, LANES), jnp.float32),
        ],
        compiler_params=pltpu.CompilerParams(vmem_limit_bytes=8 * MIB + slots * colors * 512 * 4),
        cost_estimate=pl.CostEstimate(flops=0, bytes_accessed=0, transcendentals=0),
        name="render_near" if turn is None else "render_far",
    )(s, start, table, columns, *before, *near)


def unpack_kernel(groups, width, *refs):
    arrived, out_ref, pieces = refs[:-2], refs[-2], refs[-1]
    count = len(arrived)
    me = lax.axis_index("gz")
    for apart in range(count):
        pieces[me ^ apart] = arrived[apart][...]
    for tile in range(count // groups):
        for chunk in range(arrived[0].shape[0]):
            tiles = swap_groups(
                [pieces[tile * groups + part, chunk] for part in range(groups)], groups, width)
            for part in range(groups):
                out_ref[chunk * groups + part, :, tile * LANES:(tile + 1) * LANES] = tiles[part]


def unpack(arrived, groups, width):
    count = len(arrived)
    chunks, colors, _ = arrived[0].shape
    return pl.pallas_call(
        functools.partial(unpack_kernel, groups, width),
        out_shape=jax.ShapeDtypeStruct((chunks * groups, colors, count * width), jnp.float32),
        in_specs=[pl.BlockSpec(memory_space=pltpu.VMEM)] * count,
        out_specs=pl.BlockSpec(memory_space=pltpu.VMEM),
        scratch_shapes=[pltpu.VMEM((count, chunks, colors, LANES), jnp.float32)],
        compiler_params=pltpu.CompilerParams(vmem_limit_bytes=8 * MIB),
        name="unpack",
    )(*arrived)


def table_kernel(step_x, step_z, bins_ref, extinction_ref, color_ref, columns_ref, sum_ref,
                 split_ref):
    rows, bins = extinction_ref.shape[1], bins_ref.shape[1]
    colors = extinction_ref.shape[0]
    row = lax.broadcasted_iota(jnp.int32, (rows, bins), 0)
    bin_id = lax.broadcasted_iota(jnp.int32, (rows, bins), 1)
    here = (row == bins_ref[0:1, :]).astype(jnp.float32)
    below = ((row == bins_ref[1:2, :]) & (bin_id > 0)).astype(jnp.float32)

    def rise(ref):
        now = jnp.dot(ref[...], here, precision=lax.Precision.HIGHEST,
                      preferred_element_type=jnp.float32)
        then = jnp.dot(ref[...], below, precision=lax.Precision.HIGHEST,
                       preferred_element_type=jnp.float32)
        return now - then

    def split(value):
        coarse = value.astype(jnp.bfloat16)
        fine = (value - coarse.astype(jnp.float32)).astype(jnp.bfloat16)
        return jnp.concatenate([coarse, fine, coarse], axis=1)

    sigma = rise(extinction_ref) * columns_ref[0, :, 0:bins]
    sum_ref[...] = split(sigma * (-step_x * LOG2E))
    split_ref[0:colors] = split(sigma * (-step_z * LOG2E))
    split_ref[colors:2 * colors] = split(rise(color_ref))


def tables(bin_rows, tf_extinction, tf_color, columns, step_x, step_z):
    bins = bin_rows.shape[0]
    colors = tf_color.shape[1]
    shifted = jnp.stack([bin_rows, jnp.roll(bin_rows, 1)])
    return pl.pallas_call(
        functools.partial(table_kernel, step_x, step_z),
        out_shape=(
            jax.ShapeDtypeStruct((colors, 3 * bins), jnp.bfloat16),
            jax.ShapeDtypeStruct((2 * colors, 3 * bins), jnp.bfloat16),
        ),
        in_specs=[pl.BlockSpec(memory_space=pltpu.VMEM)] * 4,
        out_specs=[pl.BlockSpec(memory_space=pltpu.VMEM)] * 2,
        compiler_params=pltpu.CompilerParams(vmem_limit_bytes=4 * MIB),
        name="tables",
    )(shifted, tf_extinction.T, tf_color.T, columns)


def exchange(value, axis, apart):
    pairs = [(source, source ^ apart) for source in range(lax.axis_size(axis))]
    return lax.ppermute(value, axis, pairs)


def local(density, bin_rows, tf_extinction, tf_color, extinction_scale, ambient, backdrop):
    rows_x, depth, width_y = density.shape
    colors = tf_color.shape[1]
    bins = bin_rows.shape[0]
    count = lax.axis_size("gz")
    size_x = lax.axis_size("gx")
    me = lax.axis_index("gz")
    width = width_y // count
    groups = LANES // width
    steps = rows_x // groups
    step_x = 1.0 / (rows_x * size_x)
    step_z = 1.0 / (depth * count)

    up = [(i, (i + 1) % size_x) for i in range(size_x)]
    down = [(j, i) for i, j in up]
    before = lax.ppermute(density[rows_x - 1:], "gx", up)
    after = lax.ppermute(density[:1], "gx", down)

    packed = pack(density, groups, width)
    pieces = list(address(packed, before, after, groups, width))
    for apart in range(1, count):
        give = pieces[apart]
        if apart > count // 2:
            ahead = apart - count // 2 + 1
            give, _ = lax.optimization_barrier((give, pieces[ahead]))
        pieces[apart] = exchange(give, "gz", apart)
    columns = jnp.broadcast_to(
        jnp.stack([extinction_scale, ambient, backdrop])[:, :, None], (3, colors, LANES))
    sum_table, table = tables(bin_rows, tf_extinction, tf_color, columns, step_x, step_z)

    def prefixes(total):
        return [lax.ppermute(total, "gx", [(i, (i + hop) % size_x) for i in range(size_x)])
                for hop in range(1, size_x)]

    blocks = count // 2
    ratio = step_x / step_z
    s, start, total = depths(pieces[:blocks], sum_table, groups, width, bins, False, count)
    *near, done = render(s, start, table, columns, prefixes(total), [], groups, width, bins, ratio,
                         None, blocks)
    s, start, total = depths(pieces, sum_table, groups, width, bins, True, count, [done])
    sums = prefixes(total)
    halves = [
        render(s, start, table, columns, sums, near, groups, width, bins, ratio, turn, blocks)
        for turn in range(2)
    ]
    share = steps // 2
    if share % groups == 0:
        arrived = []
        for apart in range(count):
            give = halves[apart % 2][apart // 2]
            arrived.append(exchange(give, "gz", apart) if apart else give)
        return unpack(arrived, groups, width)
    halves = [half[0] for half in halves]
    even = me % 2 == 0
    image = jnp.stack([jnp.where(even, halves[0], halves[1]),
                       jnp.where(even, halves[1], halves[0])])
    image = image.reshape(2, share, colors, groups, width).transpose(3, 0, 1, 2, 4)
    image = lax.all_to_all(image.reshape(count, share, colors, width), "gz", 0, 0)
    return image.transpose(1, 2, 0, 3).reshape(share, colors, width_y)


def solution(mesh):
    in_specs = (P("gx", "gz", None), P(), P(), P(), P(), P(), P())
    out_specs = P(("gx", "gz"), None, None)
    return jax.shard_map(local, mesh=mesh, in_specs=in_specs, out_specs=out_specs, check_vma=False)
```

```python
import functools

import jax
import jax.numpy as jnp
from jax import lax
from jax.experimental import pallas as pl
from jax.experimental.pallas import tpu as pltpu
from jax.sharding import PartitionSpec as P

LANES = 128
LOG2E = 1.4426950408889634
MIB = 1 << 20


def group_ids(shape, width):
    return lax.broadcasted_iota(jnp.int32, shape, len(shape) - 1) // width


def swap_groups(tiles, groups, width):
    tiles = list(tiles)
    lane = group_ids(tiles[0].shape, width)
    bit = 1
    while bit < groups:
        upper = (lane & bit) != 0
        shift = bit * width
        for first in range(groups):
            if first & bit:
                continue
            a, b = tiles[first], tiles[first | bit]
            axis = a.ndim - 1
            tiles[first] = jnp.where(upper, pltpu.roll(b, shift, axis), a)
            tiles[first | bit] = jnp.where(upper, b, pltpu.roll(a, LANES - shift, axis))
        bit *= 2
    return tiles


def blur_rows(parts, lane):
    out = []
    for tiles in parts:
        axis = tiles[0].ndim - 1
        up = [pltpu.roll(tile, 1, axis) for tile in tiles]
        down = [pltpu.roll(tile, LANES - 1, axis) for tile in tiles]
        row = []
        for t in range(len(tiles)):
            before = up[t - 1] if t > 0 else jnp.zeros_like(up[0])
            after = down[t + 1] if t + 1 < len(tiles) else jnp.zeros_like(up[0])
            low = jnp.where(lane == 0, before, up[t])
            high = jnp.where(lane == LANES - 1, after, down[t])
            row.append(low + 2.0 * tiles[t] + high)
        out.append(row)
    return out


def pack_kernel(groups, width, x_ref, out_ref):
    tile_count = x_ref.shape[3] // LANES
    lane = lax.broadcasted_iota(jnp.int32, x_ref.shape[1:3] + (LANES,), 2)
    wide = blur_rows(
        [[x_ref[part, :, :, t * LANES:(t + 1) * LANES] for t in range(tile_count)]
         for part in range(groups)], lane)
    for t in range(tile_count):
        swapped = swap_groups([wide[part][t] for part in range(groups)], groups, width)
        for part in range(groups):
            out_ref[t * groups + part] = swapped[part]


def pack(x, groups, width):
    steps = x.shape[0] // groups
    blocks = x.shape[2] // width
    depth, width_y = x.shape[1:]
    size = 4
    return pl.pallas_call(
        functools.partial(pack_kernel, groups, width),
        grid=(steps // size,),
        out_shape=jax.ShapeDtypeStruct((blocks, steps, depth, LANES), jnp.float32),
        in_specs=[pl.BlockSpec((groups, size, depth, width_y), lambda i: (0, i, 0, 0))],
        out_specs=pl.BlockSpec((blocks, size, depth, LANES), lambda i: (0, i, 0, 0)),
        compiler_params=pltpu.CompilerParams(vmem_limit_bytes=8 * MIB),
        name="pack",
    )(x.reshape(groups, steps, x.shape[1], x.shape[2]))


def address_kernel(groups, width, packed_ref, before_ref, after_ref, *refs):
    out_refs, halo = refs[:-1], refs[-1]
    count, steps, depth, _ = packed_ref.shape
    me = lax.axis_index("gz")
    tile_count = before_ref.shape[2] // LANES
    lane = lax.broadcasted_iota(jnp.int32, (depth, LANES), 1)
    position = lax.axis_index("gx")
    inside = (position > 0, position < lax.axis_size("gx") - 1)
    ends = blur_rows(
        [[jnp.where(there, ref[0, :, t * LANES:(t + 1) * LANES], 0.0) for t in range(tile_count)]
         for ref, there in zip((before_ref, after_ref), inside)], lane)
    for t in range(tile_count):
        tiles = [ends[0][t]] * (groups - 1) + [ends[1][t]]
        swapped = swap_groups(tiles, groups, width)
        for part in range(groups):
            halo[t * groups + part] = swapped[part]
    for apart in range(count):
        out_refs[apart][0:steps] = packed_ref[me ^ apart]
        out_refs[apart][steps] = halo[me ^ apart]


def address(packed, before, after, groups, width):
    count, steps, depth, _ = packed.shape
    shape = jax.ShapeDtypeStruct((steps + 1, depth, LANES), jnp.float32)
    return pl.pallas_call(
        functools.partial(address_kernel, groups, width),
        out_shape=[shape] * count,
        in_specs=[pl.BlockSpec(memory_space=pltpu.VMEM)] * 3,
        out_specs=[pl.BlockSpec(memory_space=pltpu.VMEM)] * count,
        scratch_shapes=[pltpu.VMEM((count, depth, LANES), jnp.float32)],
        compiler_params=pltpu.CompilerParams(vmem_limit_bytes=8 * MIB),
        name="address",
    )(packed, before, after)


def split_sum(table, wide):
    coarse = wide.astype(jnp.bfloat16)
    fine = (wide - coarse.astype(jnp.float32)).astype(jnp.bfloat16)
    weights = jnp.concatenate([coarse, coarse, fine], axis=0)
    return jnp.dot(table, weights, preferred_element_type=jnp.float32)


def depth_kernel(groups, width, bins, scale, far, halves_count, count, *refs):
    pieces = refs[:-8] if far else refs[:-7]
    table_ref, s_ref, start_ref, total_ref, raw, sums, products_ref = refs[-7:]
    steps, depth = pieces[0].shape[-3] - 1, pieces[0].shape[-2]
    blocks = count // 2
    layers = depth * blocks
    slots = s_ref.shape[1]
    used = layers + 1 if far else layers
    colors = table_ref.shape[0]
    me = lax.axis_index("gz")
    lower = me < blocks
    lane = group_ids((depth, LANES), width)

    def place_piece(piece, row):
        place = pl.ds(row, depth)
        raw[1:steps + 1, place, :] = piece[0:steps]
        halo = piece[steps]
        low = pltpu.roll(piece[steps - 1], width, 1)
        high = pltpu.roll(piece[0], LANES - width, 1)
        raw[0, place, :] = jnp.where(lane == 0, halo, low)
        raw[steps + 1, place, :] = jnp.where(lane == groups - 1, halo, high)

    zeros = jnp.zeros((steps + 2, depth, LANES), jnp.float32)
    raw[:, 0:depth, :] = zeros
    raw[:, depth + layers:2 * depth + layers, :] = zeros
    for apart in range(len(pieces)):
        block = (me ^ apart) % blocks
        if far and apart < blocks:
            @pl.when(block == jnp.where(lower, blocks - 1, 0))
            def _():
                row = jnp.where(lower, 0, depth + layers)
                place_piece(pieces[apart], pl.multiple_of(row, 8))
        else:
            place_piece(pieces[apart], pl.multiple_of(depth + block * depth, 8))
    slot = lax.broadcasted_iota(jnp.int32, (layers + depth, LANES), 0)
    if far:
        empty = slot > layers
        if slots > layers + depth:
            s_ref[:, layers + depth:slots, :] = jnp.full(
                (steps, slots - layers - depth, LANES), -1.0, jnp.float32)
    else:
        empty = (slot == jnp.where(lower, layers - 1, 0))[:layers]

    def smooth(step, carry):
        v = raw[step] + 2.0 * raw[step + 1] + raw[step + 2]
        size = v.shape[0]
        before = pltpu.roll(v, 1, 0)
        after = pltpu.roll(v, size - 1, 0)
        total = (before + 2.0 * v + after) * (scale / 64.0)
        if far:
            shifted = pltpu.roll(total, size - (depth - 1), 0)[:layers + depth]
            value = jnp.where(lower, shifted, total[depth:2 * depth + layers])
            s_ref[step, 0:layers + depth] = jnp.where(empty, -1.0, value)
        else:
            s_ref[step] = jnp.where(empty, -1.0, total[depth:depth + layers])
        return carry

    lax.fori_loop(0, steps, smooth, 0, unroll=2)
    edge = lax.broadcasted_iota(jnp.int32, (bins, LANES), 0).astype(jnp.float32) - 1.0
    rows = steps // halves_count

    def count_layer(z, carry):
        for half in range(halves_count):
            acc = jnp.zeros((bins, LANES), jnp.float32)
            for step in range(rows):
                row = jnp.broadcast_to(s_ref[half * rows + step, pl.ds(z, 1), :], (bins, LANES))
                acc = acc + jnp.minimum(jnp.maximum(row, edge), edge + 1.0)
            sums[half, z] = acc - edge * rows
        return carry

    lax.fori_loop(0, layers, count_layer, 0, unroll=2)
    for z in range(layers, slots):
        if z < used:
            count_layer(z, 0)
        else:
            for half in range(halves_count):
                sums[half, z] = jnp.zeros((bins, LANES), jnp.float32)
    table = table_ref[...]
    at_once = 8

    def products(chunk, carry):
        wide = [sums[half, chunk * at_once + k]
                for half in range(halves_count) for k in range(at_once)]
        out = split_sum(table, jnp.concatenate(wide, axis=1))
        for half in range(halves_count):
            for k in range(at_once):
                place = (half * at_once + k) * LANES
                products_ref[half, chunk * at_once + k] = out[:, place:place + LANES]
        return carry

    lax.fori_loop(0, slots // at_once, products, 0, unroll=2)
    group = group_ids((colors, LANES), width)

    def scan_groups(chunk, carry):
        packed = jnp.zeros((colors, LANES), jnp.float32)
        for k in range(groups):
            z = chunk * groups + k
            first = products_ref[0, z]
            both = first
            for half in range(1, halves_count):
                both = both + products_ref[half, z]
            inclusive = both
            everything = both
            shift = 1
            while shift < groups:
                moved = pltpu.roll(inclusive, shift * width, 1)
                inclusive = inclusive + jnp.where(group >= shift, moved, 0.0)
                everything = everything + pltpu.roll(everything, shift * width, 1)
                shift *= 2
            begin = inclusive - both
            start_ref[0, z] = begin
            if halves_count > 1:
                start_ref[1, z] = begin + first
            packed = jnp.where(group == k, everything, packed)
        total_ref[chunk] = packed
        return carry

    lax.fori_loop(0, slots // groups, scan_groups, 0, unroll=4)


def depths(pieces, table, groups, width, bins, far, count, after=()):
    steps, depth = pieces[0].shape[0] - 1, pieces[0].shape[1]
    layers = depth * (count // 2)
    slots = layers + max(groups, depth) if far else layers
    halves = 2 if far else 1
    colors = table.shape[0]
    limit = 8 * MIB + slots * (LANES * 4 * halves) * (bins + 2 * colors)
    return pl.pallas_call(
        functools.partial(depth_kernel, groups, width, bins, float(bins - 1), far, halves, count),
        out_shape=(
            jax.ShapeDtypeStruct((steps, slots, LANES), jnp.float32),
            jax.ShapeDtypeStruct((halves, slots, colors, LANES), jnp.float32),
            jax.ShapeDtypeStruct((slots // groups, colors, LANES), jnp.float32),
        ),
        in_specs=[pl.BlockSpec(memory_space=pltpu.VMEM)] * (len(pieces) + len(after) + 1),
        out_specs=[pl.BlockSpec(memory_space=pltpu.VMEM)] * 3,
        scratch_shapes=[
            pltpu.VMEM((steps + 2, layers + 2 * depth, LANES), jnp.float32),
            pltpu.VMEM((halves, slots, bins, LANES), jnp.float32),
            pltpu.VMEM((halves, slots, colors, LANES), jnp.float32),
        ],
        compiler_params=pltpu.CompilerParams(vmem_limit_bytes=limit),
        cost_estimate=pl.CostEstimate(flops=0, bytes_accessed=0, transcendentals=0),
        name="depths_far" if far else "depths_near",
    )(*pieces, *after, table)


def render_kernel(groups, width, bins, ratio, turn, near, blocks, sums_count, s_ref, start_ref,
                  table_ref, columns_ref, *refs):
    before_refs = refs[:sums_count]
    near_refs, refs = refs[sums_count:sums_count + near], refs[sums_count + near:]
    out_refs, image, depth = refs[:-2], refs[-2], refs[-1]
    rows, slots = image.shape[0], s_ref.shape[1]
    colors = columns_ref.shape[1]
    block = 8
    me = lax.axis_index("gz")
    lower = me < blocks
    half = 0 if turn is None else (me + turn) % 2
    position = lax.axis_index("gx")
    group = group_ids((colors, LANES), width)

    def begin(chunk, carry):
        packed = jnp.zeros((colors, LANES), jnp.float32)
        for hop, ref in enumerate(before_refs, 1):
            packed = packed + jnp.where(position >= hop, ref[chunk], 0.0)
        for k in range(groups):
            z = chunk * groups + k
            value = jnp.where(group == k, packed, 0.0)
            shift = 1
            while shift < groups:
                value = value + pltpu.roll(value, shift * width, 1)
                shift *= 2
            depth[z] = start_ref[half, z] + value
        return carry

    lax.fori_loop(0, slots // groups, begin, 0, unroll=4)
    ambient = columns_ref[1]
    table = table_ref[...]
    edge = (lax.broadcasted_iota(jnp.int32, (bins, LANES), 0).astype(jnp.float32) - 1.0).astype(
        jnp.bfloat16)
    zero = jnp.zeros((bins, LANES), jnp.bfloat16)
    one = jnp.ones((bins, LANES), jnp.bfloat16)
    layers = blocks * block

    def advance(step, carry):
        row = half * rows + step

        def layer_block(place, size, state):
            through, partial = state
            s = s_ref[row, pl.ds(place, block), :]
            lower_bin = jnp.floor(s)
            frac = s - lower_bin
            coarse = frac.astype(jnp.bfloat16).astype(jnp.float32)
            fine = frac - coarse

            def wide(value, r):
                return jnp.broadcast_to(value[r:r + 1], (bins, LANES)).astype(jnp.bfloat16)

            columns = []
            for r in range(size):
                away = wide(lower_bin, r) - edge
                main = jnp.minimum(jnp.maximum(away + wide(coarse, r), zero), one)
                rest = jnp.where(away == zero, wide(fine, r), zero)
                columns.append(jnp.concatenate([main, main, rest], axis=0))
            weights = jnp.concatenate(columns, axis=1)
            props = jnp.dot(table, weights, preferred_element_type=jnp.float32)
            for r in range(size):
                part = props[:, r * LANES:(r + 1) * LANES]
                sigma, color = part[:colors], part[colors:]
                later = through * jnp.exp2(sigma)
                z = place + r
                above = depth[z]
                shade = color * (ambient + jnp.exp2(above))
                partial = partial + (through - later) * shade
                depth[z] = above + sigma * ratio
                through = later
            return through, partial

        state = (jnp.ones((colors, LANES), jnp.float32), jnp.zeros((colors, LANES), jnp.float32))
        for chunk in range(blocks):
            state = layer_block(chunk * block, block, state)
        if turn is None:
            out_refs[0][step], out_refs[1][step] = state[1], state[0]
            return carry
        through, partial = layer_block(layers, 1, state)
        near_partial, near_through = near_refs[0][row], near_refs[1][row]
        front = jnp.where(lower, near_partial, partial)
        back = jnp.where(lower, partial, near_partial)
        passed = jnp.where(lower, near_through, through)
        image[step] = front + passed * back + through * near_through * columns_ref[2]
        return carry

    lax.fori_loop(0, rows, advance, 0, unroll=4 if turn is None else 2)
    if turn is None:
        out_refs[2][...] = jnp.zeros((8, LANES), jnp.float32)
        return
    if len(out_refs) == 1:
        out_refs[0][...] = image[...]
        return
    for chunk in range(rows // groups):
        tiles = swap_groups([image[chunk * groups + k] for k in range(groups)], groups, width)
        for part in range(groups):
            image[chunk * groups + part] = tiles[part]
    for slot in range(groups):
        part = slot ^ (me // 2)
        for chunk in range(rows // groups):
            out_refs[slot][chunk] = image[chunk * groups + part]


def render(s, start, table, columns, before, near, groups, width, bins, ratio, turn, blocks):
    steps, slots, _ = s.shape
    colors = columns.shape[1]
    share = steps // 2
    if turn is None:
        share = steps
        shapes = [jax.ShapeDtypeStruct((steps, colors, LANES), jnp.float32)] * 2
        shapes.append(jax.ShapeDtypeStruct((8, LANES), jnp.float32))
    elif share % groups == 0:
        shapes = [jax.ShapeDtypeStruct((share // groups, colors, LANES), jnp.float32)] * groups
    else:
        shapes = [jax.ShapeDtypeStruct((share, colors, LANES), jnp.float32)]
    return pl.pallas_call(
        functools.partial(render_kernel, groups, width, bins, ratio, turn, len(near), blocks,
                          len(before)),
        out_shape=shapes,
        in_specs=[pl.BlockSpec(memory_space=pltpu.VMEM)] * (4 + len(before) + len(near)),
        out_specs=[pl.BlockSpec(memory_space=pltpu.VMEM)] * len(shapes),
        scratch_shapes=[
            pltpu.VMEM((share, colors, LANES), jnp.float32),
            pltpu.VMEM((slots, colors, LANES), jnp.float32),
        ],
        compiler_params=pltpu.CompilerParams(vmem_limit_bytes=8 * MIB + slots * colors * 512 * 4),
        cost_estimate=pl.CostEstimate(flops=0, bytes_accessed=0, transcendentals=0),
        name="render_near" if turn is None else "render_far",
    )(s, start, table, columns, *before, *near)


def unpack_kernel(groups, width, *refs):
    arrived, out_ref, pieces = refs[:-2], refs[-2], refs[-1]
    count = len(arrived)
    me = lax.axis_index("gz")
    for apart in range(count):
        pieces[me ^ apart] = arrived[apart][...]
    for tile in range(count // groups):
        for chunk in range(arrived[0].shape[0]):
            tiles = swap_groups(
                [pieces[tile * groups + part, chunk] for part in range(groups)], groups, width)
            for part in range(groups):
                out_ref[chunk * groups + part, :, tile * LANES:(tile + 1) * LANES] = tiles[part]


def unpack(arrived, groups, width):
    count = len(arrived)
    chunks, colors, _ = arrived[0].shape
    return pl.pallas_call(
        functools.partial(unpack_kernel, groups, width),
        out_shape=jax.ShapeDtypeStruct((chunks * groups, colors, count * width), jnp.float32),
        in_specs=[pl.BlockSpec(memory_space=pltpu.VMEM)] * count,
        out_specs=pl.BlockSpec(memory_space=pltpu.VMEM),
        scratch_shapes=[pltpu.VMEM((count, chunks, colors, LANES), jnp.float32)],
        compiler_params=pltpu.CompilerParams(vmem_limit_bytes=8 * MIB),
        name="unpack",
    )(*arrived)


def table_kernel(step_x, step_z, bins_ref, extinction_ref, color_ref, columns_ref, sum_ref,
                 split_ref):
    rows, bins = extinction_ref.shape[1], bins_ref.shape[1]
    colors = extinction_ref.shape[0]
    row = lax.broadcasted_iota(jnp.int32, (rows, bins), 0)
    bin_id = lax.broadcasted_iota(jnp.int32, (rows, bins), 1)
    here = (row == bins_ref[0:1, :]).astype(jnp.float32)
    below = ((row == bins_ref[1:2, :]) & (bin_id > 0)).astype(jnp.float32)

    def rise(ref):
        now = jnp.dot(ref[...], here, precision=lax.Precision.HIGHEST,
                      preferred_element_type=jnp.float32)
        then = jnp.dot(ref[...], below, precision=lax.Precision.HIGHEST,
                       preferred_element_type=jnp.float32)
        return now - then

    def split(value):
        coarse = value.astype(jnp.bfloat16)
        fine = (value - coarse.astype(jnp.float32)).astype(jnp.bfloat16)
        return jnp.concatenate([coarse, fine, coarse], axis=1)

    sigma = rise(extinction_ref) * columns_ref[0, :, 0:bins]
    sum_ref[...] = split(sigma * (-step_x * LOG2E))
    split_ref[0:colors] = split(sigma * (-step_z * LOG2E))
    split_ref[colors:2 * colors] = split(rise(color_ref))


def tables(bin_rows, tf_extinction, tf_color, columns, step_x, step_z):
    bins = bin_rows.shape[0]
    colors = tf_color.shape[1]
    shifted = jnp.stack([bin_rows, jnp.roll(bin_rows, 1)])
    return pl.pallas_call(
        functools.partial(table_kernel, step_x, step_z),
        out_shape=(
            jax.ShapeDtypeStruct((colors, 3 * bins), jnp.bfloat16),
            jax.ShapeDtypeStruct((2 * colors, 3 * bins), jnp.bfloat16),
        ),
        in_specs=[pl.BlockSpec(memory_space=pltpu.VMEM)] * 4,
        out_specs=[pl.BlockSpec(memory_space=pltpu.VMEM)] * 2,
        compiler_params=pltpu.CompilerParams(vmem_limit_bytes=4 * MIB),
        name="tables",
    )(shifted, tf_extinction.T, tf_color.T, columns)


def exchange(value, axis, apart):
    pairs = [(source, source ^ apart) for source in range(lax.axis_size(axis))]
    return lax.ppermute(value, axis, pairs)


def local(density, bin_rows, tf_extinction, tf_color, extinction_scale, ambient, backdrop):
    rows_x, depth, width_y = density.shape
    colors = tf_color.shape[1]
    bins = bin_rows.shape[0]
    count = lax.axis_size("gz")
    size_x = lax.axis_size("gx")
    me = lax.axis_index("gz")
    width = width_y // count
    groups = LANES // width
    steps = rows_x // groups
    step_x = 1.0 / (rows_x * size_x)
    step_z = 1.0 / (depth * count)

    up = [(i, (i + 1) % size_x) for i in range(size_x)]
    down = [(j, i) for i, j in up]
    before = lax.ppermute(density[rows_x - 1:], "gx", up)
    after = lax.ppermute(density[:1], "gx", down)

    packed = pack(density, groups, width)
    pieces = list(address(packed, before, after, groups, width))
    for apart in range(1, count):
        give = pieces[apart]
        if apart > count // 2:
            ahead = min(apart - count // 2 + 1, count // 2 - 1)
            give, _ = lax.optimization_barrier((give, pieces[ahead]))
        pieces[apart] = exchange(give, "gz", apart)
    columns = jnp.broadcast_to(
        jnp.stack([extinction_scale, ambient, backdrop])[:, :, None], (3, colors, LANES))
    sum_table, table = tables(bin_rows, tf_extinction, tf_color, columns, step_x, step_z)

    def prefixes(total):
        return [lax.ppermute(total, "gx", [(i, (i + hop) % size_x) for i in range(size_x)])
                for hop in range(1, size_x)]

    blocks = count // 2
    ratio = step_x / step_z
    s, start, total = depths(pieces[:blocks], sum_table, groups, width, bins, False, count)
    *near, done = render(s, start, table, columns, prefixes(total), [], groups, width, bins, ratio,
                         None, blocks)
    s, start, total = depths(pieces, sum_table, groups, width, bins, True, count, [done])
    sums = prefixes(total)
    halves = [
        render(s, start, table, columns, sums, near, groups, width, bins, ratio, turn, blocks)
        for turn in range(2)
    ]
    share = steps // 2
    if share % groups == 0:
        arrived = []
        for apart in range(count):
            give = halves[apart % 2][apart // 2]
            arrived.append(exchange(give, "gz", apart) if apart else give)
        return unpack(arrived, groups, width)
    halves = [half[0] for half in halves]
    even = me % 2 == 0
    image = jnp.stack([jnp.where(even, halves[0], halves[1]),
                       jnp.where(even, halves[1], halves[0])])
    image = image.reshape(2, share, colors, groups, width).transpose(3, 0, 1, 2, 4)
    image = lax.all_to_all(image.reshape(count, share, colors, width), "gz", 0, 0)
    return image.transpose(1, 2, 0, 3).reshape(share, colors, width_y)


def solution(mesh):
    in_specs = (P("gx", "gz", None), P(), P(), P(), P(), P(), P())
    out_specs = P(("gx", "gz"), None, None)
    return jax.shard_map(local, mesh=mesh, in_specs=in_specs, out_specs=out_specs, check_vma=False)
```

```python
import functools

import jax
import jax.numpy as jnp
from jax import lax
from jax.experimental import pallas as pl
from jax.experimental.pallas import tpu as pltpu
from jax.sharding import PartitionSpec as P

LANES = 128
LOG2E = 1.4426950408889634
MIB = 1 << 20


def group_ids(shape, width):
    return lax.broadcasted_iota(jnp.int32, shape, len(shape) - 1) // width


def swap_groups(tiles, groups, width):
    tiles = list(tiles)
    lane = group_ids(tiles[0].shape, width)
    bit = 1
    while bit < groups:
        upper = (lane & bit) != 0
        shift = bit * width
        for first in range(groups):
            if first & bit:
                continue
            a, b = tiles[first], tiles[first | bit]
            axis = a.ndim - 1
            tiles[first] = jnp.where(upper, pltpu.roll(b, shift, axis), a)
            tiles[first | bit] = jnp.where(upper, b, pltpu.roll(a, LANES - shift, axis))
        bit *= 2
    return tiles


def blur_rows(parts, lane):
    out = []
    for tiles in parts:
        axis = tiles[0].ndim - 1
        up = [pltpu.roll(tile, 1, axis) for tile in tiles]
        down = [pltpu.roll(tile, LANES - 1, axis) for tile in tiles]
        row = []
        for t in range(len(tiles)):
            before = up[t - 1] if t > 0 else jnp.zeros_like(up[0])
            after = down[t + 1] if t + 1 < len(tiles) else jnp.zeros_like(up[0])
            low = jnp.where(lane == 0, before, up[t])
            high = jnp.where(lane == LANES - 1, after, down[t])
            row.append(low + 2.0 * tiles[t] + high)
        out.append(row)
    return out


def pack_kernel(groups, width, x_ref, out_ref):
    tile_count = x_ref.shape[3] // LANES
    lane = lax.broadcasted_iota(jnp.int32, x_ref.shape[1:3] + (LANES,), 2)
    wide = blur_rows(
        [[x_ref[part, :, :, t * LANES:(t + 1) * LANES] for t in range(tile_count)]
         for part in range(groups)], lane)
    for t in range(tile_count):
        swapped = swap_groups([wide[part][t] for part in range(groups)], groups, width)
        for part in range(groups):
            out_ref[t * groups + part] = swapped[part]


def pack(x, groups, width):
    steps = x.shape[0] // groups
    blocks = x.shape[2] // width
    depth, width_y = x.shape[1:]
    size = 4
    return pl.pallas_call(
        functools.partial(pack_kernel, groups, width),
        grid=(steps // size,),
        out_shape=jax.ShapeDtypeStruct((blocks, steps, depth, LANES), jnp.float32),
        in_specs=[pl.BlockSpec((groups, size, depth, width_y), lambda i: (0, i, 0, 0))],
        out_specs=pl.BlockSpec((blocks, size, depth, LANES), lambda i: (0, i, 0, 0)),
        compiler_params=pltpu.CompilerParams(vmem_limit_bytes=8 * MIB),
        name="pack",
    )(x.reshape(groups, steps, x.shape[1], x.shape[2]))


def address_kernel(groups, width, packed_ref, before_ref, after_ref, *refs):
    out_refs, halo = refs[:-1], refs[-1]
    count, steps, depth, _ = packed_ref.shape
    me = lax.axis_index("gz")
    tile_count = before_ref.shape[2] // LANES
    lane = lax.broadcasted_iota(jnp.int32, (depth, LANES), 1)
    position = lax.axis_index("gx")
    inside = (position > 0, position < lax.axis_size("gx") - 1)
    ends = blur_rows(
        [[jnp.where(there, ref[0, :, t * LANES:(t + 1) * LANES], 0.0) for t in range(tile_count)]
         for ref, there in zip((before_ref, after_ref), inside)], lane)
    for t in range(tile_count):
        tiles = [ends[0][t]] * (groups - 1) + [ends[1][t]]
        swapped = swap_groups(tiles, groups, width)
        for part in range(groups):
            halo[t * groups + part] = swapped[part]
    for apart in range(count):
        out_refs[apart][0:steps] = packed_ref[me ^ apart]
        out_refs[apart][steps] = halo[me ^ apart]


def address(packed, before, after, groups, width):
    count, steps, depth, _ = packed.shape
    shape = jax.ShapeDtypeStruct((steps + 1, depth, LANES), jnp.float32)
    return pl.pallas_call(
        functools.partial(address_kernel, groups, width),
        out_shape=[shape] * count,
        in_specs=[pl.BlockSpec(memory_space=pltpu.VMEM)] * 3,
        out_specs=[pl.BlockSpec(memory_space=pltpu.VMEM)] * count,
        scratch_shapes=[pltpu.VMEM((count, depth, LANES), jnp.float32)],
        compiler_params=pltpu.CompilerParams(vmem_limit_bytes=8 * MIB),
        name="address",
    )(packed, before, after)


def split_sum(table, wide):
    coarse = wide.astype(jnp.bfloat16)
    fine = (wide - coarse.astype(jnp.float32)).astype(jnp.bfloat16)
    weights = jnp.concatenate([coarse, coarse, fine], axis=0)
    return jnp.dot(table, weights, preferred_element_type=jnp.float32)


def smooth_layers(groups, width, scale, far, count, pieces, s_ref, raw):
    steps, depth = pieces[0].shape[-3] - 1, pieces[0].shape[-2]
    blocks = count // 2
    layers = depth * blocks
    slots = s_ref.shape[1]
    me = lax.axis_index("gz")
    lower = me < blocks
    lane = group_ids((depth, LANES), width)

    def place_piece(piece, row):
        place = pl.ds(row, depth)
        raw[1:steps + 1, place, :] = piece[0:steps]
        halo = piece[steps]
        low = pltpu.roll(piece[steps - 1], width, 1)
        high = pltpu.roll(piece[0], LANES - width, 1)
        raw[0, place, :] = jnp.where(lane == 0, halo, low)
        raw[steps + 1, place, :] = jnp.where(lane == groups - 1, halo, high)

    zeros = jnp.zeros((steps + 2, depth, LANES), jnp.float32)
    raw[:, 0:depth, :] = zeros
    raw[:, depth + layers:2 * depth + layers, :] = zeros
    for apart in range(len(pieces)):
        block = (me ^ apart) % blocks
        if far and apart < blocks:
            @pl.when(block == jnp.where(lower, blocks - 1, 0))
            def _():
                row = jnp.where(lower, 0, depth + layers)
                place_piece(pieces[apart], pl.multiple_of(row, 8))
        else:
            place_piece(pieces[apart], pl.multiple_of(depth + block * depth, 8))
    slot = lax.broadcasted_iota(jnp.int32, (layers + depth, LANES), 0)
    if far:
        empty = slot > layers
        if slots > layers + depth:
            s_ref[:, layers + depth:slots, :] = jnp.full(
                (steps, slots - layers - depth, LANES), -1.0, jnp.float32)
    else:
        empty = (slot == jnp.where(lower, layers - 1, 0))[:layers]

    def smooth(step, carry):
        v = raw[step] + 2.0 * raw[step + 1] + raw[step + 2]
        size = v.shape[0]
        before = pltpu.roll(v, 1, 0)
        after = pltpu.roll(v, size - 1, 0)
        total = (before + 2.0 * v + after) * (scale / 64.0)
        if far:
            shifted = pltpu.roll(total, size - (depth - 1), 0)[:layers + depth]
            value = jnp.where(lower, shifted, total[depth:2 * depth + layers])
            s_ref[step, 0:layers + depth] = jnp.where(empty, -1.0, value)
        else:
            s_ref[step] = jnp.where(empty, -1.0, total[depth:depth + layers])
        return carry

    lax.fori_loop(0, steps, smooth, 0, unroll=2)


def scan_quarters(groups, width, first_ref, second_ref, start_ref, total_ref, offset):
    slots, colors = first_ref.shape[0], first_ref.shape[1]
    group = group_ids((colors, LANES), width)

    def scan_groups(chunk, carry):
        packed = jnp.zeros((colors, LANES), jnp.float32)
        for k in range(groups):
            z = chunk * groups + k
            first = first_ref[z]
            both = first if second_ref is None else first + second_ref[z]
            inclusive = both
            everything = both
            shift = 1
            while shift < groups:
                moved = pltpu.roll(inclusive, shift * width, 1)
                inclusive = inclusive + jnp.where(group >= shift, moved, 0.0)
                everything = everything + pltpu.roll(everything, shift * width, 1)
                shift *= 2
            begin = inclusive - both
            start_ref[0, z] = begin
            if second_ref is not None:
                start_ref[1, z] = begin + first
            packed = jnp.where(group == k, everything, packed)
        total_ref[offset + chunk] = packed
        return carry

    lax.fori_loop(0, slots // groups, scan_groups, 0, unroll=4)


def bin_edges(bins):
    return lax.broadcasted_iota(jnp.int32, (bins, LANES), 0).astype(jnp.float32) - 1.0


def properties(s, size, table, bins):
    edge = bin_edges(bins).astype(jnp.bfloat16)
    zero = jnp.zeros((bins, LANES), jnp.bfloat16)
    one = jnp.ones((bins, LANES), jnp.bfloat16)
    lower_bin = jnp.floor(s)
    frac = s - lower_bin
    coarse = frac.astype(jnp.bfloat16).astype(jnp.float32)
    fine = frac - coarse

    def wide(value, r):
        return jnp.broadcast_to(value[r:r + 1], (bins, LANES)).astype(jnp.bfloat16)

    columns = []
    for r in range(size):
        away = wide(lower_bin, r) - edge
        main = jnp.minimum(jnp.maximum(away + wide(coarse, r), zero), one)
        rest = jnp.where(away == zero, wide(fine, r), zero)
        columns.append(jnp.concatenate([main, main, rest], axis=0))
    return jnp.dot(table, jnp.concatenate(columns, axis=1), preferred_element_type=jnp.float32)


def near_kernel(groups, width, bins, ratio, count, *refs):
    pieces = refs[:count // 2]
    (table_ref, lit_ref, unlit_ref, through_ref, start_ref, total_ref, raw, s_ref,
     depth) = refs[count // 2:]
    steps, layers, colors, _ = lit_ref.shape
    smooth_layers(groups, width, float(bins - 1), False, count, pieces, s_ref, raw)
    depth[...] = jnp.zeros(depth.shape, jnp.float32)
    table = table_ref[...]
    block = 8

    def advance(step, carry):
        through = jnp.ones((colors, LANES), jnp.float32)
        unlit = jnp.zeros((colors, LANES), jnp.float32)
        for chunk in range(layers // block):
            place = chunk * block
            props = properties(s_ref[step, place:place + block, :], block, table, bins)
            for r in range(block):
                part = props[:, r * LANES:(r + 1) * LANES]
                sigma, color = part[:colors], part[colors:]
                later = through * jnp.exp2(sigma)
                seen = (through - later) * color
                above = depth[place + r]
                unlit = unlit + seen
                lit_ref[step, place + r] = seen * jnp.exp2(above)
                depth[place + r] = above + sigma * ratio
                through = later
        unlit_ref[step], through_ref[step] = unlit, through
        return carry

    lax.fori_loop(0, steps, advance, 0, unroll=4)
    scan_quarters(groups, width, depth, None, start_ref, total_ref, 0)


def render_near(pieces, table, colors, groups, width, bins, ratio, count):
    steps, depth = pieces[0].shape[0] - 1, pieces[0].shape[1]
    layers = depth * len(pieces)
    plane = jax.ShapeDtypeStruct((steps, colors, LANES), jnp.float32)
    return pl.pallas_call(
        functools.partial(near_kernel, groups, width, bins, ratio, count),
        out_shape=(
            jax.ShapeDtypeStruct((steps, layers, colors, LANES), jnp.float32),
            plane,
            plane,
            jax.ShapeDtypeStruct((1, layers, colors, LANES), jnp.float32),
            jax.ShapeDtypeStruct((layers // groups, colors, LANES), jnp.float32),
        ),
        in_specs=[pl.BlockSpec(memory_space=pltpu.VMEM)] * (len(pieces) + 1),
        out_specs=[pl.BlockSpec(memory_space=pltpu.VMEM)] * 5,
        scratch_shapes=[
            pltpu.VMEM((steps + 2, layers + 2 * depth, LANES), jnp.float32),
            pltpu.VMEM((steps, layers, LANES), jnp.float32),
            pltpu.VMEM((layers, colors, LANES), jnp.float32),
        ],
        compiler_params=pltpu.CompilerParams(vmem_limit_bytes=20 * MIB),
        cost_estimate=pl.CostEstimate(flops=0, bytes_accessed=0, transcendentals=0),
        name="render_near",
    )(*pieces, table)


def depth_kernel(groups, width, bins, count, *refs):
    pieces = refs[:count]
    near_ref, table_ref, s_ref, start_ref, total_ref, raw, sums, products_ref = refs[count:]
    steps, depth = pieces[0].shape[-3] - 1, pieces[0].shape[-2]
    layers = depth * (count // 2)
    slots = s_ref.shape[1]
    used = layers + 1
    smooth_layers(groups, width, float(bins - 1), True, count, pieces, s_ref, raw)
    edge = bin_edges(bins)
    rows = steps // 2

    def count_layer(z, carry):
        for half in range(2):
            acc = jnp.zeros((bins, LANES), jnp.float32)
            for step in range(rows):
                row = jnp.broadcast_to(s_ref[half * rows + step, pl.ds(z, 1), :], (bins, LANES))
                acc = acc + jnp.minimum(jnp.maximum(row, edge), edge + 1.0)
            sums[half, z] = acc - edge * rows
        return carry

    lax.fori_loop(0, layers, count_layer, 0, unroll=2)
    count_layer(layers, 0)
    for z in range(used, slots):
        for half in range(2):
            sums[half, z] = jnp.zeros((bins, LANES), jnp.float32)
    table = table_ref[...]
    at_once = 8

    def products(chunk, carry):
        wide = [sums[half, chunk * at_once + k] for half in range(2) for k in range(at_once)]
        out = split_sum(table, jnp.concatenate(wide, axis=1))
        for half in range(2):
            for k in range(at_once):
                place = (half * at_once + k) * LANES
                products_ref[half, chunk * at_once + k] = out[:, place:place + LANES]
        return carry

    lax.fori_loop(0, slots // at_once, products, 0, unroll=True)
    ahead = near_ref.shape[0]
    total_ref[0:ahead] = near_ref[...]
    scan_quarters(groups, width, products_ref.at[0], products_ref.at[1], start_ref, total_ref,
                  ahead)


def far_depths(pieces, near_total, table, groups, width, bins):
    count = len(pieces)
    steps, depth = pieces[0].shape[0] - 1, pieces[0].shape[1]
    layers = depth * (count // 2)
    slots = layers + max(groups, depth)
    colors = table.shape[0]
    limit = 8 * MIB + slots * (LANES * 4 * 2) * (bins + 2 * colors)
    return pl.pallas_call(
        functools.partial(depth_kernel, groups, width, bins, count),
        out_shape=(
            jax.ShapeDtypeStruct((steps, slots, LANES), jnp.float32),
            jax.ShapeDtypeStruct((2, slots, colors, LANES), jnp.float32),
            jax.ShapeDtypeStruct((near_total.shape[0] + slots // groups, colors, LANES),
                                 jnp.float32),
        ),
        in_specs=[pl.BlockSpec(memory_space=pltpu.VMEM)] * (count + 2),
        out_specs=[pl.BlockSpec(memory_space=pltpu.VMEM)] * 3,
        scratch_shapes=[
            pltpu.VMEM((steps + 2, layers + 2 * depth, LANES), jnp.float32),
            pltpu.VMEM((2, slots, bins, LANES), jnp.float32),
            pltpu.VMEM((2, slots, colors, LANES), jnp.float32),
        ],
        compiler_params=pltpu.CompilerParams(vmem_limit_bytes=limit),
        cost_estimate=pl.CostEstimate(flops=0, bytes_accessed=0, transcendentals=0),
        name="far_depths",
    )(*pieces, near_total, table)


def render_kernel(groups, width, bins, ratio, turn, blocks, hops, s_ref, start_ref, table_ref,
                  columns_ref, lit_ref, unlit_ref, near_through_ref, near_start_ref, *refs):
    before_refs, out_ref, image, depth, light = refs[:hops], *refs[hops:]
    rows, slots = image.shape[0], s_ref.shape[1]
    colors = columns_ref.shape[1]
    block = 8
    layers = blocks * block
    me = lax.axis_index("gz")
    lower = me < blocks
    half = (me + turn) % 2
    position = lax.axis_index("gx")
    group = group_ids((colors, LANES), width)
    ahead = layers // groups

    def before(chunk):
        packed = jnp.zeros((colors, LANES), jnp.float32)
        for hop, ref in enumerate(before_refs, 1):
            packed = packed + jnp.where(position >= hop, ref[chunk], 0.0)
        values = []
        for k in range(groups):
            value = jnp.where(group == k, packed, 0.0)
            shift = 1
            while shift < groups:
                value = value + pltpu.roll(value, shift * width, 1)
                shift *= 2
            values.append(value)
        return values

    def begin_near(chunk, carry):
        for k, value in enumerate(before(chunk)):
            z = chunk * groups + k
            light[z] = jnp.exp2(near_start_ref[0, z] + value)
        return carry

    def begin_far(chunk, carry):
        for k, value in enumerate(before(ahead + chunk)):
            z = chunk * groups + k
            depth[z] = start_ref[half, z] + value
        return carry

    lax.fori_loop(0, ahead, begin_near, 0, unroll=4)
    lax.fori_loop(0, slots // groups, begin_far, 0, unroll=4)
    ambient = columns_ref[1]
    table = table_ref[...]

    def advance(step, carry):
        row = half * rows + step
        through = jnp.ones((colors, LANES), jnp.float32)
        partial = jnp.zeros((colors, LANES), jnp.float32)
        for chunk in range(blocks + 1):
            place = chunk * block
            size = block if chunk < blocks else 1
            props = properties(s_ref[row, place:place + block, :], size, table, bins)
            for r in range(size):
                part = props[:, r * LANES:(r + 1) * LANES]
                sigma, color = part[:colors], part[colors:]
                later = through * jnp.exp2(sigma)
                above = depth[place + r]
                shade = color * (ambient + jnp.exp2(above))
                partial = partial + (through - later) * shade
                depth[place + r] = above + sigma * ratio
                through = later
        sums = [unlit_ref[row] * ambient] + [jnp.zeros((colors, LANES), jnp.float32)] * 3
        for z in range(layers):
            sums[z % 4] = sums[z % 4] + lit_ref[row, z] * light[z]
        near_partial = (sums[0] + sums[1]) + (sums[2] + sums[3])
        near_through = near_through_ref[row]
        front = jnp.where(lower, near_partial, partial)
        back = jnp.where(lower, partial, near_partial)
        passed = jnp.where(lower, near_through, through)
        image[step] = front + passed * back + through * near_through * columns_ref[2]
        return carry

    lax.fori_loop(0, rows, advance, 0, unroll=2)
    if len(out_ref.shape) == 3:
        out_ref[...] = image[...]
        return
    for chunk in range(rows // groups):
        tiles = swap_groups([image[chunk * groups + k] for k in range(groups)], groups, width)
        for part in range(groups):
            image[chunk * groups + part] = tiles[part]
    for slot in range(groups):
        part = slot ^ (me // 2)
        for chunk in range(rows // groups):
            out_ref[slot, chunk] = image[chunk * groups + part]


def render(s, start, table, columns, near, before, groups, width, bins, ratio, turn, blocks):
    steps, slots, _ = s.shape
    layers = near[0].shape[1]
    colors = columns.shape[1]
    share = steps // 2
    shape = (share, colors, LANES)
    if share % groups == 0:
        shape = (groups, share // groups, colors, LANES)
    operands = [s, start, table, columns, *near, *before]
    return pl.pallas_call(
        functools.partial(render_kernel, groups, width, bins, ratio, turn, blocks, len(before)),
        out_shape=jax.ShapeDtypeStruct(shape, jnp.float32),
        in_specs=[pl.BlockSpec(memory_space=pltpu.VMEM)] * len(operands),
        out_specs=pl.BlockSpec(memory_space=pltpu.VMEM),
        scratch_shapes=[
            pltpu.VMEM((share, colors, LANES), jnp.float32),
            pltpu.VMEM((slots, colors, LANES), jnp.float32),
            pltpu.VMEM((layers, colors, LANES), jnp.float32),
        ],
        compiler_params=pltpu.CompilerParams(vmem_limit_bytes=20 * MIB),
        cost_estimate=pl.CostEstimate(flops=0, bytes_accessed=0, transcendentals=0),
        name="render",
    )(*operands)


def unpack_kernel(groups, width, *refs):
    arrived, out_ref, pieces = refs[:-2], refs[-2], refs[-1]
    count = 2 * len(arrived)
    me = lax.axis_index("gz")
    for apart in range(count):
        pieces[me ^ apart] = arrived[apart // 2][apart % 2]
    for tile in range(count // groups):
        for chunk in range(arrived[0].shape[1]):
            tiles = swap_groups(
                [pieces[tile * groups + part, chunk] for part in range(groups)], groups, width)
            for part in range(groups):
                out_ref[chunk * groups + part, :, tile * LANES:(tile + 1) * LANES] = tiles[part]


def unpack(arrived, groups, width):
    count = 2 * len(arrived)
    _, chunks, colors, _ = arrived[0].shape
    return pl.pallas_call(
        functools.partial(unpack_kernel, groups, width),
        out_shape=jax.ShapeDtypeStruct((chunks * groups, colors, count * width), jnp.float32),
        in_specs=[pl.BlockSpec(memory_space=pltpu.VMEM)] * len(arrived),
        out_specs=pl.BlockSpec(memory_space=pltpu.VMEM),
        scratch_shapes=[pltpu.VMEM((count, chunks, colors, LANES), jnp.float32)],
        compiler_params=pltpu.CompilerParams(vmem_limit_bytes=8 * MIB),
        name="unpack",
    )(*arrived)


def table_kernel(step_x, step_z, bins_ref, extinction_ref, color_ref, columns_ref, sum_ref,
                 split_ref):
    rows, bins = extinction_ref.shape[1], bins_ref.shape[1]
    colors = extinction_ref.shape[0]
    row = lax.broadcasted_iota(jnp.int32, (rows, bins), 0)
    bin_id = lax.broadcasted_iota(jnp.int32, (rows, bins), 1)
    here = (row == bins_ref[0:1, :]).astype(jnp.float32)
    below = ((row == bins_ref[1:2, :]) & (bin_id > 0)).astype(jnp.float32)

    def rise(ref):
        now = jnp.dot(ref[...], here, precision=lax.Precision.HIGHEST,
                      preferred_element_type=jnp.float32)
        then = jnp.dot(ref[...], below, precision=lax.Precision.HIGHEST,
                       preferred_element_type=jnp.float32)
        return now - then

    def split(value):
        coarse = value.astype(jnp.bfloat16)
        fine = (value - coarse.astype(jnp.float32)).astype(jnp.bfloat16)
        return jnp.concatenate([coarse, fine, coarse], axis=1)

    sigma = rise(extinction_ref) * columns_ref[0, :, 0:bins]
    sum_ref[...] = split(sigma * (-step_x * LOG2E))
    split_ref[0:colors] = split(sigma * (-step_z * LOG2E))
    split_ref[colors:2 * colors] = split(rise(color_ref))


def tables(bin_rows, tf_extinction, tf_color, columns, step_x, step_z):
    bins = bin_rows.shape[0]
    colors = tf_color.shape[1]
    shifted = jnp.stack([bin_rows, jnp.roll(bin_rows, 1)])
    return pl.pallas_call(
        functools.partial(table_kernel, step_x, step_z),
        out_shape=(
            jax.ShapeDtypeStruct((colors, 3 * bins), jnp.bfloat16),
            jax.ShapeDtypeStruct((2 * colors, 3 * bins), jnp.bfloat16),
        ),
        in_specs=[pl.BlockSpec(memory_space=pltpu.VMEM)] * 4,
        out_specs=[pl.BlockSpec(memory_space=pltpu.VMEM)] * 2,
        compiler_params=pltpu.CompilerParams(vmem_limit_bytes=4 * MIB),
        name="tables",
    )(shifted, tf_extinction.T, tf_color.T, columns)


def exchange(value, axis, apart):
    pairs = [(source, source ^ apart) for source in range(lax.axis_size(axis))]
    return lax.ppermute(value, axis, pairs)


def local(density, bin_rows, tf_extinction, tf_color, extinction_scale, ambient, backdrop):
    rows_x, depth, width_y = density.shape
    colors = tf_color.shape[1]
    bins = bin_rows.shape[0]
    count = lax.axis_size("gz")
    size_x = lax.axis_size("gx")
    me = lax.axis_index("gz")
    width = width_y // count
    groups = LANES // width
    steps = rows_x // groups
    step_x = 1.0 / (rows_x * size_x)
    step_z = 1.0 / (depth * count)

    up = [(i, (i + 1) % size_x) for i in range(size_x)]
    down = [(j, i) for i, j in up]
    before = lax.ppermute(density[rows_x - 1:], "gx", up)
    after = lax.ppermute(density[:1], "gx", down)

    packed = pack(density, groups, width)
    pieces = list(address(packed, before, after, groups, width))
    for apart in range(1, count):
        give = pieces[apart]
        if apart > count // 2:
            ahead = min(apart - count // 2 + 1, count // 2 - 1)
            give, _ = lax.optimization_barrier((give, pieces[ahead]))
        pieces[apart] = exchange(give, "gz", apart)
    columns = jnp.broadcast_to(
        jnp.stack([extinction_scale, ambient, backdrop])[:, :, None], (3, colors, LANES))
    sum_table, table = tables(bin_rows, tf_extinction, tf_color, columns, step_x, step_z)

    blocks = count // 2
    ratio = step_x / step_z
    *near, near_total = render_near(
        pieces[:blocks], table, colors, groups, width, bins, ratio, count)
    s, start, total = far_depths(pieces, near_total, sum_table, groups, width, bins)
    sums = [lax.ppermute(total, "gx", [(i, (i + hop) % size_x) for i in range(size_x)])
            for hop in range(1, size_x)]

    def half_of(turn):
        return render(s, start, table, columns, near, sums, groups, width, bins, ratio, turn, blocks)

    share = steps // 2
    if share % groups == 0:
        joined = exchange(half_of(1), "gz", 1)
        both = jnp.stack([half_of(0), joined], axis=1)
        arrived = []
        for slot in range(count // 2):
            arrived.append(exchange(both[slot], "gz", 2 * slot) if slot else both[0])
        return unpack(arrived, groups, width)
    halves = [half_of(0), half_of(1)]
    even = me % 2 == 0
    image = jnp.stack([jnp.where(even, halves[0], halves[1]),
                       jnp.where(even, halves[1], halves[0])])
    image = image.reshape(2, share, colors, groups, width).transpose(3, 0, 1, 2, 4)
    image = lax.all_to_all(image.reshape(count, share, colors, width), "gz", 0, 0)
    return image.transpose(1, 2, 0, 3).reshape(share, colors, width_y)


def solution(mesh):
    in_specs = (P("gx", "gz", None), P(), P(), P(), P(), P(), P())
    out_specs = P(("gx", "gz"), None, None)
    return jax.shard_map(local, mesh=mesh, in_specs=in_specs, out_specs=out_specs, check_vma=False)
```

```python
import functools

import jax
import jax.numpy as jnp
from jax import lax
from jax.experimental import pallas as pl
from jax.experimental.pallas import tpu as pltpu
from jax.sharding import PartitionSpec as P

LANES = 128
LOG2E = 1.4426950408889634
MIB = 1 << 20


def group_ids(shape, width):
    return lax.broadcasted_iota(jnp.int32, shape, len(shape) - 1) // width


def swap_groups(tiles, groups, width):
    tiles = list(tiles)
    lane = group_ids(tiles[0].shape, width)
    bit = 1
    while bit < groups:
        upper = (lane & bit) != 0
        shift = bit * width
        for first in range(groups):
            if first & bit:
                continue
            a, b = tiles[first], tiles[first | bit]
            axis = a.ndim - 1
            tiles[first] = jnp.where(upper, pltpu.roll(b, shift, axis), a)
            tiles[first | bit] = jnp.where(upper, b, pltpu.roll(a, LANES - shift, axis))
        bit *= 2
    return tiles


def blur_rows(parts, lane):
    out = []
    for tiles in parts:
        axis = tiles[0].ndim - 1
        up = [pltpu.roll(tile, 1, axis) for tile in tiles]
        down = [pltpu.roll(tile, LANES - 1, axis) for tile in tiles]
        row = []
        for t in range(len(tiles)):
            before = up[t - 1] if t > 0 else jnp.zeros_like(up[0])
            after = down[t + 1] if t + 1 < len(tiles) else jnp.zeros_like(up[0])
            low = jnp.where(lane == 0, before, up[t])
            high = jnp.where(lane == LANES - 1, after, down[t])
            row.append(low + 2.0 * tiles[t] + high)
        out.append(row)
    return out


def pack_kernel(groups, width, x_ref, out_ref):
    tile_count = x_ref.shape[3] // LANES
    lane = lax.broadcasted_iota(jnp.int32, x_ref.shape[1:3] + (LANES,), 2)
    wide = blur_rows(
        [[x_ref[part, :, :, t * LANES:(t + 1) * LANES] for t in range(tile_count)]
         for part in range(groups)], lane)
    for t in range(tile_count):
        swapped = swap_groups([wide[part][t] for part in range(groups)], groups, width)
        for part in range(groups):
            out_ref[t * groups + part] = swapped[part]


def pack(x, groups, width):
    steps = x.shape[0] // groups
    blocks = x.shape[2] // width
    depth, width_y = x.shape[1:]
    size = 4
    return pl.pallas_call(
        functools.partial(pack_kernel, groups, width),
        grid=(steps // size,),
        out_shape=jax.ShapeDtypeStruct((blocks, steps, depth, LANES), jnp.float32),
        in_specs=[pl.BlockSpec((groups, size, depth, width_y), lambda i: (0, i, 0, 0))],
        out_specs=pl.BlockSpec((blocks, size, depth, LANES), lambda i: (0, i, 0, 0)),
        compiler_params=pltpu.CompilerParams(vmem_limit_bytes=8 * MIB),
        name="pack",
    )(x.reshape(groups, steps, x.shape[1], x.shape[2]))


def address_kernel(groups, width, packed_ref, before_ref, after_ref, *refs):
    out_refs, halo = refs[:-1], refs[-1]
    count, steps, depth, _ = packed_ref.shape
    me = lax.axis_index("gz")
    tile_count = before_ref.shape[2] // LANES
    lane = lax.broadcasted_iota(jnp.int32, (depth, LANES), 1)
    position = lax.axis_index("gx")
    inside = (position > 0, position < lax.axis_size("gx") - 1)
    ends = blur_rows(
        [[jnp.where(there, ref[0, :, t * LANES:(t + 1) * LANES], 0.0) for t in range(tile_count)]
         for ref, there in zip((before_ref, after_ref), inside)], lane)
    for t in range(tile_count):
        tiles = [ends[0][t]] * (groups - 1) + [ends[1][t]]
        swapped = swap_groups(tiles, groups, width)
        for part in range(groups):
            halo[t * groups + part] = swapped[part]
    for apart in range(count):
        out_refs[apart][0:steps] = packed_ref[me ^ apart]
        out_refs[apart][steps] = halo[me ^ apart]


def address(packed, before, after, groups, width):
    count, steps, depth, _ = packed.shape
    shape = jax.ShapeDtypeStruct((steps + 1, depth, LANES), jnp.float32)
    return pl.pallas_call(
        functools.partial(address_kernel, groups, width),
        out_shape=[shape] * count,
        in_specs=[pl.BlockSpec(memory_space=pltpu.VMEM)] * 3,
        out_specs=[pl.BlockSpec(memory_space=pltpu.VMEM)] * count,
        scratch_shapes=[pltpu.VMEM((count, depth, LANES), jnp.float32)],
        compiler_params=pltpu.CompilerParams(vmem_limit_bytes=8 * MIB),
        name="address",
    )(packed, before, after)


def split_sum(table, wide):
    coarse = wide.astype(jnp.bfloat16)
    fine = (wide - coarse.astype(jnp.float32)).astype(jnp.bfloat16)
    weights = jnp.concatenate([coarse, coarse, fine], axis=0)
    return jnp.dot(table, weights, preferred_element_type=jnp.float32)


def smooth_layers(groups, width, scale, far, count, pieces, s_ref, raw):
    steps, depth = pieces[0].shape[-3] - 1, pieces[0].shape[-2]
    blocks = count // 2
    layers = depth * blocks
    slots = s_ref.shape[1]
    me = lax.axis_index("gz")
    lower = me < blocks
    lane = group_ids((depth, LANES), width)

    def place_piece(piece, row):
        place = pl.ds(row, depth)
        raw[1:steps + 1, place, :] = piece[0:steps]
        halo = piece[steps]
        low = pltpu.roll(piece[steps - 1], width, 1)
        high = pltpu.roll(piece[0], LANES - width, 1)
        raw[0, place, :] = jnp.where(lane == 0, halo, low)
        raw[steps + 1, place, :] = jnp.where(lane == groups - 1, halo, high)

    zeros = jnp.zeros((steps + 2, depth, LANES), jnp.float32)
    raw[:, 0:depth, :] = zeros
    raw[:, depth + layers:2 * depth + layers, :] = zeros
    for apart in range(len(pieces)):
        block = (me ^ apart) % blocks
        if far and apart < blocks:
            @pl.when(block == jnp.where(lower, blocks - 1, 0))
            def _():
                row = jnp.where(lower, 0, depth + layers)
                place_piece(pieces[apart], pl.multiple_of(row, 8))
        else:
            place_piece(pieces[apart], pl.multiple_of(depth + block * depth, 8))
    slot = lax.broadcasted_iota(jnp.int32, (layers + depth, LANES), 0)
    if far:
        empty = slot > layers
        if slots > layers + depth:
            s_ref[:, layers + depth:slots, :] = jnp.full(
                (steps, slots - layers - depth, LANES), -1.0, jnp.float32)
    else:
        empty = (slot == jnp.where(lower, layers - 1, 0))[:layers]

    def smooth(step, carry):
        v = raw[step] + 2.0 * raw[step + 1] + raw[step + 2]
        size = v.shape[0]
        before = pltpu.roll(v, 1, 0)
        after = pltpu.roll(v, size - 1, 0)
        total = (before + 2.0 * v + after) * (scale / 64.0)
        if far:
            shifted = pltpu.roll(total, size - (depth - 1), 0)[:layers + depth]
            value = jnp.where(lower, shifted, total[depth:2 * depth + layers])
            s_ref[step, 0:layers + depth] = jnp.where(empty, -1.0, value)
        else:
            s_ref[step] = jnp.where(empty, -1.0, total[depth:depth + layers])
        return carry

    lax.fori_loop(0, steps, smooth, 0, unroll=2)


def scan_quarters(groups, width, sums_ref, start_ref, total_ref, offset):
    slots, colors = sums_ref.shape[0], sums_ref.shape[1]
    group = group_ids((colors, LANES), width)

    def scan_groups(chunk, carry):
        packed = jnp.zeros((colors, LANES), jnp.float32)
        for k in range(groups):
            z = chunk * groups + k
            both = sums_ref[z]
            inclusive = both
            everything = both
            shift = 1
            while shift < groups:
                moved = pltpu.roll(inclusive, shift * width, 1)
                inclusive = inclusive + jnp.where(group >= shift, moved, 0.0)
                everything = everything + pltpu.roll(everything, shift * width, 1)
                shift *= 2
            start_ref[z] = inclusive - both
            packed = jnp.where(group == k, everything, packed)
        total_ref[offset + chunk] = packed
        return carry

    lax.fori_loop(0, slots // groups, scan_groups, 0, unroll=4)


def bin_edges(bins):
    return lax.broadcasted_iota(jnp.int32, (bins, LANES), 0).astype(jnp.float32) - 1.0


def properties(s, size, table, bins):
    edge = bin_edges(bins).astype(jnp.bfloat16)
    zero = jnp.zeros((bins, LANES), jnp.bfloat16)
    one = jnp.ones((bins, LANES), jnp.bfloat16)
    lower_bin = jnp.floor(s)
    frac = s - lower_bin
    coarse = frac.astype(jnp.bfloat16).astype(jnp.float32)
    fine = frac - coarse

    def wide(value, r):
        return jnp.broadcast_to(value[r:r + 1], (bins, LANES)).astype(jnp.bfloat16)

    columns = []
    for r in range(size):
        away = wide(lower_bin, r) - edge
        main = jnp.minimum(jnp.maximum(away + wide(coarse, r), zero), one)
        rest = jnp.where(away == zero, wide(fine, r), zero)
        columns.append(jnp.concatenate([main, main, rest], axis=0))
    return jnp.dot(table, jnp.concatenate(columns, axis=1), preferred_element_type=jnp.float32)


def render_rows(bins, ratio, s_ref, table_ref, lit_ref, unlit_ref, through_ref, depth):
    steps, layers, colors, _ = lit_ref.shape
    depth[...] = jnp.zeros(depth.shape, jnp.float32)
    table = table_ref[...]
    block = 8

    def advance(step, carry):
        through = jnp.ones((colors, LANES), jnp.float32)
        unlit = jnp.zeros((colors, LANES), jnp.float32)
        for place in range(0, layers, block):
            size = min(block, layers - place)
            props = properties(s_ref[step, place:place + block, :], size, table, bins)
            for r in range(size):
                part = props[:, r * LANES:(r + 1) * LANES]
                sigma, color = part[:colors], part[colors:]
                later = through * jnp.exp2(sigma)
                seen = (through - later) * color
                above = depth[place + r]
                unlit = unlit + seen
                lit_ref[step, place + r] = seen * jnp.exp2(above)
                depth[place + r] = above + sigma * ratio
                through = later
        unlit_ref[step], through_ref[step] = unlit, through
        return carry

    lax.fori_loop(0, steps, advance, 0, unroll=4)


def near_kernel(groups, width, bins, ratio, count, *refs):
    pieces = refs[:count // 2]
    (table_ref, lit_ref, unlit_ref, through_ref, start_ref, total_ref, raw, s_ref,
     depth) = refs[count // 2:]
    smooth_layers(groups, width, float(bins - 1), False, count, pieces, s_ref, raw)
    render_rows(bins, ratio, s_ref, table_ref, lit_ref, unlit_ref, through_ref, depth)
    scan_quarters(groups, width, depth, start_ref, total_ref, 0)


def render_near(pieces, table, colors, groups, width, bins, ratio, count):
    steps, depth = pieces[0].shape[0] - 1, pieces[0].shape[1]
    layers = depth * len(pieces)
    plane = jax.ShapeDtypeStruct((steps, colors, LANES), jnp.float32)
    return pl.pallas_call(
        functools.partial(near_kernel, groups, width, bins, ratio, count),
        out_shape=(
            jax.ShapeDtypeStruct((steps, layers, colors, LANES), jnp.float32),
            plane,
            plane,
            jax.ShapeDtypeStruct((layers, colors, LANES), jnp.float32),
            jax.ShapeDtypeStruct((layers // groups, colors, LANES), jnp.float32),
        ),
        in_specs=[pl.BlockSpec(memory_space=pltpu.VMEM)] * (len(pieces) + 1),
        out_specs=[pl.BlockSpec(memory_space=pltpu.VMEM)] * 5,
        scratch_shapes=[
            pltpu.VMEM((steps + 2, layers + 2 * depth, LANES), jnp.float32),
            pltpu.VMEM((steps, layers, LANES), jnp.float32),
            pltpu.VMEM((layers, colors, LANES), jnp.float32),
        ],
        compiler_params=pltpu.CompilerParams(vmem_limit_bytes=20 * MIB),
        cost_estimate=pl.CostEstimate(flops=0, bytes_accessed=0, transcendentals=0),
        name="render_near",
    )(*pieces, table)


def depth_kernel(groups, width, bins, count, *refs):
    pieces = refs[:count]
    near_ref, table_ref, s_ref, start_ref, total_ref, raw, sums, products_ref = refs[count:]
    steps, depth = pieces[0].shape[-3] - 1, pieces[0].shape[-2]
    layers = depth * (count // 2)
    slots = s_ref.shape[1]
    smooth_layers(groups, width, float(bins - 1), True, count, pieces, s_ref, raw)
    edge = bin_edges(bins)

    def count_layer(z, carry):
        acc = jnp.zeros((bins, LANES), jnp.float32)
        for step in range(steps):
            row = jnp.broadcast_to(s_ref[step, pl.ds(z, 1), :], (bins, LANES))
            acc = acc + jnp.minimum(jnp.maximum(row, edge), edge + 1.0)
        sums[z] = acc - edge * steps
        return carry

    lax.fori_loop(0, layers, count_layer, 0, unroll=2)
    count_layer(layers, 0)
    for z in range(layers + 1, slots):
        sums[z] = jnp.zeros((bins, LANES), jnp.float32)
    table = table_ref[...]
    at_once = 8

    def products(chunk, carry):
        wide = [sums[chunk * at_once + k] for k in range(at_once)]
        out = split_sum(table, jnp.concatenate(wide, axis=1))
        for k in range(at_once):
            products_ref[chunk * at_once + k] = out[:, k * LANES:(k + 1) * LANES]
        return carry

    lax.fori_loop(0, slots // at_once, products, 0, unroll=True)
    ahead = near_ref.shape[0]
    total_ref[0:ahead] = near_ref[...]
    scan_quarters(groups, width, products_ref, start_ref, total_ref, ahead)


def far_depths(pieces, near_total, table, groups, width, bins):
    count = len(pieces)
    steps, depth = pieces[0].shape[0] - 1, pieces[0].shape[1]
    layers = depth * (count // 2)
    slots = layers + max(groups, depth)
    colors = table.shape[0]
    limit = 8 * MIB + slots * (LANES * 4) * (bins + 2 * colors)
    return pl.pallas_call(
        functools.partial(depth_kernel, groups, width, bins, count),
        out_shape=(
            jax.ShapeDtypeStruct((steps, slots, LANES), jnp.float32),
            jax.ShapeDtypeStruct((slots, colors, LANES), jnp.float32),
            jax.ShapeDtypeStruct((near_total.shape[0] + slots // groups, colors, LANES),
                                 jnp.float32),
        ),
        in_specs=[pl.BlockSpec(memory_space=pltpu.VMEM)] * (count + 2),
        out_specs=[pl.BlockSpec(memory_space=pltpu.VMEM)] * 3,
        scratch_shapes=[
            pltpu.VMEM((steps + 2, layers + 2 * depth, LANES), jnp.float32),
            pltpu.VMEM((slots, bins, LANES), jnp.float32),
            pltpu.VMEM((slots, colors, LANES), jnp.float32),
        ],
        compiler_params=pltpu.CompilerParams(vmem_limit_bytes=limit),
        cost_estimate=pl.CostEstimate(flops=0, bytes_accessed=0, transcendentals=0),
        name="far_depths",
    )(*pieces, near_total, table)


def render_far(s, table, colors, bins, ratio, layers):
    steps = s.shape[0]
    plane = jax.ShapeDtypeStruct((steps, colors, LANES), jnp.float32)
    return pl.pallas_call(
        functools.partial(render_rows, bins, ratio),
        out_shape=(jax.ShapeDtypeStruct((steps, layers, colors, LANES), jnp.float32), plane, plane),
        in_specs=[pl.BlockSpec(memory_space=pltpu.VMEM)] * 2,
        out_specs=[pl.BlockSpec(memory_space=pltpu.VMEM)] * 3,
        scratch_shapes=[pltpu.VMEM((layers, colors, LANES), jnp.float32)],
        compiler_params=pltpu.CompilerParams(vmem_limit_bytes=20 * MIB),
        cost_estimate=pl.CostEstimate(
            flops=10 ** 10, bytes_accessed=10 ** 7, transcendentals=10 ** 7),
        name="render_far",
    )(s, table)


def join_kernel(groups, width, turn, blocks, columns_ref, *refs):
    near_lit, near_unlit, near_through, near_start = refs[:4]
    far_lit, far_unlit, far_through, far_start = refs[4:8]
    before_refs, out_ref, image, near_light, far_light = refs[8:-4], *refs[-4:]
    rows, colors, _ = image.shape
    layers, far_layers = near_lit.shape[1], far_lit.shape[1]
    me = lax.axis_index("gz")
    lower = me < blocks
    half = (me + turn) % 2
    position = lax.axis_index("gx")
    group = group_ids((colors, LANES), width)
    ahead = layers // groups

    def begin(chunk, start_ref, offset, light):
        packed = jnp.zeros((colors, LANES), jnp.float32)
        for hop, ref in enumerate(before_refs, 1):
            packed = packed + jnp.where(position >= hop, ref[offset + chunk], 0.0)
        for k in range(groups):
            value = jnp.where(group == k, packed, 0.0)
            shift = 1
            while shift < groups:
                value = value + pltpu.roll(value, shift * width, 1)
                shift *= 2
            z = chunk * groups + k
            light[z] = jnp.exp2(start_ref[z] + value)

    def begin_near(chunk, carry):
        begin(chunk, near_start, 0, near_light)
        return carry

    def begin_far(chunk, carry):
        begin(chunk, far_start, ahead, far_light)
        return carry

    lax.fori_loop(0, ahead, begin_near, 0, unroll=4)
    lax.fori_loop(0, far_start.shape[0] // groups, begin_far, 0, unroll=4)
    ambient = columns_ref[1]
    backdrop = columns_ref[2]
    at_once = 2

    def light_rows(chunk, carry):
        place = [chunk * at_once + k for k in range(at_once)]

        def lit_sum(lit, unlit, light, count):
            sums = [[unlit[half * rows + row] * ambient, jnp.zeros((colors, LANES), jnp.float32)]
                    for row in place]
            for z in range(count):
                factor = light[z]
                for k, row in enumerate(place):
                    sums[k][z % 2] = sums[k][z % 2] + lit[half * rows + row, z] * factor
            return [a + b for a, b in sums]

        near = lit_sum(near_lit, near_unlit, near_light, layers)
        far = lit_sum(far_lit, far_unlit, far_light, far_layers)
        for k, row in enumerate(place):
            through = far_through[half * rows + row]
            passed = near_through[half * rows + row]
            front = jnp.where(lower, near[k], far[k])
            back = jnp.where(lower, far[k], near[k])
            image[row] = (front + jnp.where(lower, passed, through) * back
                          + through * passed * backdrop)
        return carry

    lax.fori_loop(0, rows // at_once, light_rows, 0, unroll=2)
    if len(out_ref.shape) == 3:
        out_ref[...] = image[...]
        return
    for chunk in range(rows // groups):
        tiles = swap_groups([image[chunk * groups + k] for k in range(groups)], groups, width)
        for part in range(groups):
            image[chunk * groups + part] = tiles[part]
    for slot in range(groups):
        part = slot ^ (me // 2)
        for chunk in range(rows // groups):
            out_ref[slot, chunk] = image[chunk * groups + part]


def join(columns, near, far, before, groups, width, turn, blocks):
    steps, layers, colors, _ = near[0].shape
    share = steps // 2
    shape = (share, colors, LANES)
    if share % groups == 0:
        shape = (groups, share // groups, colors, LANES)
    operands = [columns, *near, *far, *before]
    return pl.pallas_call(
        functools.partial(join_kernel, groups, width, turn, blocks),
        out_shape=jax.ShapeDtypeStruct(shape, jnp.float32),
        in_specs=[pl.BlockSpec(memory_space=pltpu.VMEM)] * len(operands),
        out_specs=pl.BlockSpec(memory_space=pltpu.VMEM),
        scratch_shapes=[
            pltpu.VMEM((share, colors, LANES), jnp.float32),
            pltpu.VMEM((layers, colors, LANES), jnp.float32),
            pltpu.VMEM((far[3].shape[0], colors, LANES), jnp.float32),
        ],
        compiler_params=pltpu.CompilerParams(vmem_limit_bytes=24 * MIB),
        cost_estimate=pl.CostEstimate(flops=0, bytes_accessed=0, transcendentals=0),
        name="join",
    )(*operands)


def unpack_kernel(groups, width, *refs):
    arrived, out_ref, pieces = refs[:-2], refs[-2], refs[-1]
    count = 2 * len(arrived)
    me = lax.axis_index("gz")
    for apart in range(count):
        pieces[me ^ apart] = arrived[apart // 2][apart % 2]
    for tile in range(count // groups):
        for chunk in range(arrived[0].shape[1]):
            tiles = swap_groups(
                [pieces[tile * groups + part, chunk] for part in range(groups)], groups, width)
            for part in range(groups):
                out_ref[chunk * groups + part, :, tile * LANES:(tile + 1) * LANES] = tiles[part]


def unpack(arrived, groups, width):
    count = 2 * len(arrived)
    _, chunks, colors, _ = arrived[0].shape
    return pl.pallas_call(
        functools.partial(unpack_kernel, groups, width),
        out_shape=jax.ShapeDtypeStruct((chunks * groups, colors, count * width), jnp.float32),
        in_specs=[pl.BlockSpec(memory_space=pltpu.VMEM)] * len(arrived),
        out_specs=pl.BlockSpec(memory_space=pltpu.VMEM),
        scratch_shapes=[pltpu.VMEM((count, chunks, colors, LANES), jnp.float32)],
        compiler_params=pltpu.CompilerParams(vmem_limit_bytes=8 * MIB),
        name="unpack",
    )(*arrived)


def table_kernel(step_x, step_z, bins_ref, extinction_ref, color_ref, columns_ref, sum_ref,
                 split_ref):
    rows, bins = extinction_ref.shape[1], bins_ref.shape[1]
    colors = extinction_ref.shape[0]
    row = lax.broadcasted_iota(jnp.int32, (rows, bins), 0)
    bin_id = lax.broadcasted_iota(jnp.int32, (rows, bins), 1)
    here = (row == bins_ref[0:1, :]).astype(jnp.float32)
    below = ((row == bins_ref[1:2, :]) & (bin_id > 0)).astype(jnp.float32)

    def rise(ref):
        now = jnp.dot(ref[...], here, precision=lax.Precision.HIGHEST,
                      preferred_element_type=jnp.float32)
        then = jnp.dot(ref[...], below, precision=lax.Precision.HIGHEST,
                       preferred_element_type=jnp.float32)
        return now - then

    def split(value):
        coarse = value.astype(jnp.bfloat16)
        fine = (value - coarse.astype(jnp.float32)).astype(jnp.bfloat16)
        return jnp.concatenate([coarse, fine, coarse], axis=1)

    sigma = rise(extinction_ref) * columns_ref[0, :, 0:bins]
    sum_ref[...] = split(sigma * (-step_x * LOG2E))
    split_ref[0:colors] = split(sigma * (-step_z * LOG2E))
    split_ref[colors:2 * colors] = split(rise(color_ref))


def tables(bin_rows, tf_extinction, tf_color, columns, step_x, step_z):
    bins = bin_rows.shape[0]
    colors = tf_color.shape[1]
    shifted = jnp.stack([bin_rows, jnp.roll(bin_rows, 1)])
    return pl.pallas_call(
        functools.partial(table_kernel, step_x, step_z),
        out_shape=(
            jax.ShapeDtypeStruct((colors, 3 * bins), jnp.bfloat16),
            jax.ShapeDtypeStruct((2 * colors, 3 * bins), jnp.bfloat16),
        ),
        in_specs=[pl.BlockSpec(memory_space=pltpu.VMEM)] * 4,
        out_specs=[pl.BlockSpec(memory_space=pltpu.VMEM)] * 2,
        compiler_params=pltpu.CompilerParams(vmem_limit_bytes=4 * MIB),
        name="tables",
    )(shifted, tf_extinction.T, tf_color.T, columns)


def exchange(value, axis, apart):
    pairs = [(source, source ^ apart) for source in range(lax.axis_size(axis))]
    return lax.ppermute(value, axis, pairs)


def local(density, bin_rows, tf_extinction, tf_color, extinction_scale, ambient, backdrop):
    rows_x, depth, width_y = density.shape
    colors = tf_color.shape[1]
    bins = bin_rows.shape[0]
    count = lax.axis_size("gz")
    size_x = lax.axis_size("gx")
    me = lax.axis_index("gz")
    width = width_y // count
    groups = LANES // width
    steps = rows_x // groups
    step_x = 1.0 / (rows_x * size_x)
    step_z = 1.0 / (depth * count)

    up = [(i, (i + 1) % size_x) for i in range(size_x)]
    down = [(j, i) for i, j in up]
    before = lax.ppermute(density[rows_x - 1:], "gx", up)
    after = lax.ppermute(density[:1], "gx", down)

    packed = pack(density, groups, width)
    pieces = list(address(packed, before, after, groups, width))
    for apart in range(1, count):
        give = pieces[apart]
        if apart > count // 2:
            ahead = min(apart - count // 2 + 1, count // 2 - 1)
            give, _ = lax.optimization_barrier((give, pieces[ahead]))
        pieces[apart] = exchange(give, "gz", apart)
    bin_rows, extinction_scale, ambient, backdrop, _ = lax.optimization_barrier(
        (bin_rows, extinction_scale, ambient, backdrop, pieces[2]))
    columns = jnp.broadcast_to(
        jnp.stack([extinction_scale, ambient, backdrop])[:, :, None], (3, colors, LANES))
    sum_table, table = tables(bin_rows, tf_extinction, tf_color, columns, step_x, step_z)

    blocks = count // 2
    ratio = step_x / step_z
    *near, near_total = render_near(
        pieces[:blocks], table, colors, groups, width, bins, ratio, count)
    s, start, total = far_depths(pieces, near_total, sum_table, groups, width, bins)
    sums = [lax.ppermute(total, "gx", [(i, (i + hop) % size_x) for i in range(size_x)])
            for hop in range(1, size_x)]

    layers = depth * blocks
    far = [*render_far(s, table, colors, bins, ratio, layers + 1), start]

    def half_of(turn):
        return join(columns, near, far, sums, groups, width, turn, blocks)

    share = steps // 2
    if share % groups == 0:
        joined = exchange(half_of(1), "gz", 1)
        both = jnp.stack([half_of(0), joined], axis=1)
        arrived = []
        for slot in range(count // 2):
            arrived.append(exchange(both[slot], "gz", 2 * slot) if slot else both[0])
        return unpack(arrived, groups, width)
    halves = [half_of(0), half_of(1)]
    even = me % 2 == 0
    image = jnp.stack([jnp.where(even, halves[0], halves[1]),
                       jnp.where(even, halves[1], halves[0])])
    image = image.reshape(2, share, colors, groups, width).transpose(3, 0, 1, 2, 4)
    image = lax.all_to_all(image.reshape(count, share, colors, width), "gz", 0, 0)
    return image.transpose(1, 2, 0, 3).reshape(share, colors, width_y)


def solution(mesh):
    in_specs = (P("gx", "gz", None), P(), P(), P(), P(), P(), P())
    out_specs = P(("gx", "gz"), None, None)
    return jax.shard_map(local, mesh=mesh, in_specs=in_specs, out_specs=out_specs, check_vma=False)
```

```python
import functools

import jax
import jax.numpy as jnp
from jax import lax
from jax.experimental import pallas as pl
from jax.experimental.pallas import tpu as pltpu
from jax.sharding import PartitionSpec as P

LANES = 128
LOG2E = 1.4426950408889634
MIB = 1 << 20


def group_ids(shape, width):
    return lax.broadcasted_iota(jnp.int32, shape, len(shape) - 1) // width


def swap_groups(tiles, groups, width):
    tiles = list(tiles)
    lane = group_ids(tiles[0].shape, width)
    bit = 1
    while bit < groups:
        upper = (lane & bit) != 0
        shift = bit * width
        for first in range(groups):
            if first & bit:
                continue
            a, b = tiles[first], tiles[first | bit]
            axis = a.ndim - 1
            tiles[first] = jnp.where(upper, pltpu.roll(b, shift, axis), a)
            tiles[first | bit] = jnp.where(upper, b, pltpu.roll(a, LANES - shift, axis))
        bit *= 2
    return tiles


def blur_rows(parts, lane):
    out = []
    for tiles in parts:
        axis = tiles[0].ndim - 1
        up = [pltpu.roll(tile, 1, axis) for tile in tiles]
        down = [pltpu.roll(tile, LANES - 1, axis) for tile in tiles]
        row = []
        for t in range(len(tiles)):
            before = up[t - 1] if t > 0 else jnp.zeros_like(up[0])
            after = down[t + 1] if t + 1 < len(tiles) else jnp.zeros_like(up[0])
            low = jnp.where(lane == 0, before, up[t])
            high = jnp.where(lane == LANES - 1, after, down[t])
            row.append(low + 2.0 * tiles[t] + high)
        out.append(row)
    return out


def pack_kernel(groups, width, x_ref, out_ref):
    tile_count = x_ref.shape[3] // LANES
    steps, depth = x_ref.shape[1], x_ref.shape[2]
    size = 4
    lane = lax.broadcasted_iota(jnp.int32, (size, depth, LANES), 2)
    for first in range(0, steps, size):
        place = pl.ds(first, size)
        wide = blur_rows(
            [[x_ref[group, place, :, t * LANES:(t + 1) * LANES] for t in range(tile_count)]
             for group in range(groups)], lane)
        for t in range(tile_count):
            swapped = swap_groups([wide[group][t] for group in range(groups)], groups, width)
            for group in range(groups):
                out_ref[t * groups + group, place] = swapped[group]


def pack(x, groups, width):
    steps = x.shape[0] // groups
    blocks = x.shape[2] // width
    depth, width_y = x.shape[1:]
    return pl.pallas_call(
        functools.partial(pack_kernel, groups, width),
        out_shape=jax.ShapeDtypeStruct((blocks, steps, depth, LANES), jnp.float32),
        in_specs=[pl.BlockSpec(memory_space=pltpu.VMEM)],
        out_specs=pl.BlockSpec(memory_space=pltpu.VMEM),
        compiler_params=pltpu.CompilerParams(vmem_limit_bytes=8 * MIB),
        name="pack",
    )(x.reshape(groups, steps, depth, width_y))


def address_kernel(groups, width, packed_ref, before_ref, after_ref, *refs):
    out_refs, halo = refs[:-1], refs[-1]
    count, steps, depth, _ = packed_ref.shape
    me = lax.axis_index("gz")
    tile_count = before_ref.shape[2] // LANES
    lane = lax.broadcasted_iota(jnp.int32, (depth, LANES), 1)
    position = lax.axis_index("gx")
    inside = (position > 0, position < lax.axis_size("gx") - 1)
    ends = blur_rows(
        [[jnp.where(there, ref[0, :, t * LANES:(t + 1) * LANES], 0.0) for t in range(tile_count)]
         for ref, there in zip((before_ref, after_ref), inside)], lane)
    for t in range(tile_count):
        tiles = [ends[0][t]] * (groups - 1) + [ends[1][t]]
        swapped = swap_groups(tiles, groups, width)
        for part in range(groups):
            halo[t * groups + part] = swapped[part]
    for apart in range(count):
        out_refs[apart][0:steps] = packed_ref[me ^ apart]
        out_refs[apart][steps] = halo[me ^ apart]


def address(packed, before, after, groups, width):
    count, steps, depth, _ = packed.shape
    shape = jax.ShapeDtypeStruct((steps + 1, depth, LANES), jnp.float32)
    return pl.pallas_call(
        functools.partial(address_kernel, groups, width),
        out_shape=[shape] * count,
        in_specs=[pl.BlockSpec(memory_space=pltpu.VMEM)] * 3,
        out_specs=[pl.BlockSpec(memory_space=pltpu.VMEM)] * count,
        scratch_shapes=[pltpu.VMEM((count, depth, LANES), jnp.float32)],
        compiler_params=pltpu.CompilerParams(vmem_limit_bytes=8 * MIB),
        name="address",
    )(packed, before, after)


def split_sum(table, wide):
    coarse = wide.astype(jnp.bfloat16)
    fine = (wide - coarse.astype(jnp.float32)).astype(jnp.bfloat16)
    weights = jnp.concatenate([coarse, coarse, fine], axis=0)
    return jnp.dot(table, weights, preferred_element_type=jnp.float32)


def smooth_layers(groups, width, scale, far, count, pieces, s_ref, raw):
    steps, depth = pieces[0].shape[-3] - 1, pieces[0].shape[-2]
    blocks = count // 2
    layers = depth * blocks
    slots = s_ref.shape[1]
    me = lax.axis_index("gz")
    lower = me < blocks
    lane = group_ids((depth, LANES), width)

    def place_piece(piece, row):
        place = pl.ds(row, depth)
        raw[1:steps + 1, place, :] = piece[0:steps]
        halo = piece[steps]
        low = pltpu.roll(piece[steps - 1], width, 1)
        high = pltpu.roll(piece[0], LANES - width, 1)
        raw[0, place, :] = jnp.where(lane == 0, halo, low)
        raw[steps + 1, place, :] = jnp.where(lane == groups - 1, halo, high)

    zeros = jnp.zeros((steps + 2, depth, LANES), jnp.float32)
    raw[:, 0:depth, :] = zeros
    raw[:, depth + layers:2 * depth + layers, :] = zeros
    for apart in range(len(pieces)):
        block = (me ^ apart) % blocks
        if far and apart < blocks:
            @pl.when(block == jnp.where(lower, blocks - 1, 0))
            def _():
                row = jnp.where(lower, 0, depth + layers)
                place_piece(pieces[apart], pl.multiple_of(row, 8))
        else:
            place_piece(pieces[apart], pl.multiple_of(depth + block * depth, 8))
    slot = lax.broadcasted_iota(jnp.int32, (layers + depth, LANES), 0)
    if far:
        empty = slot > layers
        if slots > layers + depth:
            s_ref[:, layers + depth:slots, :] = jnp.full(
                (steps, slots - layers - depth, LANES), -1.0, jnp.float32)
    else:
        empty = (slot == jnp.where(lower, layers - 1, 0))[:layers]

    def smooth(step, carry):
        v = raw[step] + 2.0 * raw[step + 1] + raw[step + 2]
        size = v.shape[0]
        before = pltpu.roll(v, 1, 0)
        after = pltpu.roll(v, size - 1, 0)
        total = (before + 2.0 * v + after) * (scale / 64.0)
        if far:
            shifted = pltpu.roll(total, size - (depth - 1), 0)[:layers + depth]
            value = jnp.where(lower, shifted, total[depth:2 * depth + layers])
            s_ref[step, 0:layers + depth] = jnp.where(empty, -1.0, value)
        else:
            s_ref[step] = jnp.where(empty, -1.0, total[depth:depth + layers])
        return carry

    lax.fori_loop(0, steps, smooth, 0, unroll=2)


def scan_quarters(groups, width, sums_ref, start_ref, total_ref, offset):
    slots, colors = sums_ref.shape[0], sums_ref.shape[1]
    group = group_ids((colors, LANES), width)

    def scan_groups(chunk, carry):
        packed = jnp.zeros((colors, LANES), jnp.float32)
        for k in range(groups):
            z = chunk * groups + k
            both = sums_ref[z]
            inclusive = both
            everything = both
            shift = 1
            while shift < groups:
                moved = pltpu.roll(inclusive, shift * width, 1)
                inclusive = inclusive + jnp.where(group >= shift, moved, 0.0)
                everything = everything + pltpu.roll(everything, shift * width, 1)
                shift *= 2
            start_ref[z] = inclusive - both
            packed = jnp.where(group == k, everything, packed)
        total_ref[offset + chunk] = packed
        return carry

    lax.fori_loop(0, slots // groups, scan_groups, 0, unroll=4)


def bin_edges(bins):
    return lax.broadcasted_iota(jnp.int32, (bins, LANES), 0).astype(jnp.float32) - 1.0


def properties(s, size, table, bins):
    edge = bin_edges(bins).astype(jnp.bfloat16)
    zero = jnp.zeros((bins, LANES), jnp.bfloat16)
    one = jnp.ones((bins, LANES), jnp.bfloat16)
    lower_bin = jnp.floor(s)
    frac = s - lower_bin
    coarse = frac.astype(jnp.bfloat16).astype(jnp.float32)
    fine = frac - coarse

    def wide(value, r):
        return jnp.broadcast_to(value[r:r + 1], (bins, LANES)).astype(jnp.bfloat16)

    columns = []
    for r in range(size):
        away = wide(lower_bin, r) - edge
        main = jnp.minimum(jnp.maximum(away + wide(coarse, r), zero), one)
        rest = jnp.where(away == zero, wide(fine, r), zero)
        columns.append(jnp.concatenate([main, main, rest], axis=0))
    return jnp.dot(table, jnp.concatenate(columns, axis=1), preferred_element_type=jnp.float32)


def render_rows(bins, ratio, s_ref, table_ref, lit_ref, unlit_ref, through_ref, depth):
    steps, layers, colors, _ = lit_ref.shape
    depth[...] = jnp.zeros(depth.shape, jnp.float32)
    table = table_ref[...]
    block = 8

    def advance(step, carry):
        through = jnp.ones((colors, LANES), jnp.float32)
        unlit = jnp.zeros((colors, LANES), jnp.float32)
        for place in range(0, layers, block):
            size = min(block, layers - place)
            props = properties(s_ref[step, place:place + block, :], size, table, bins)
            for r in range(size):
                part = props[:, r * LANES:(r + 1) * LANES]
                sigma, color = part[:colors], part[colors:]
                later = through * jnp.exp2(sigma)
                seen = (through - later) * color
                above = depth[place + r]
                unlit = unlit + seen
                lit_ref[step, place + r] = seen * jnp.exp2(above)
                depth[place + r] = above + sigma * ratio
                through = later
        unlit_ref[step], through_ref[step] = unlit, through
        return carry

    lax.fori_loop(0, steps, advance, 0, unroll=4)


def near_kernel(groups, width, bins, ratio, count, *refs):
    pieces = refs[:count // 2]
    (table_ref, lit_ref, unlit_ref, through_ref, start_ref, total_ref, raw, s_ref,
     depth) = refs[count // 2:]
    smooth_layers(groups, width, float(bins - 1), False, count, pieces, s_ref, raw)
    render_rows(bins, ratio, s_ref, table_ref, lit_ref, unlit_ref, through_ref, depth)
    scan_quarters(groups, width, depth, start_ref, total_ref, 0)


def render_near(pieces, table, colors, groups, width, bins, ratio, count):
    steps, depth = pieces[0].shape[0] - 1, pieces[0].shape[1]
    layers = depth * len(pieces)
    plane = jax.ShapeDtypeStruct((steps, colors, LANES), jnp.float32)
    return pl.pallas_call(
        functools.partial(near_kernel, groups, width, bins, ratio, count),
        out_shape=(
            jax.ShapeDtypeStruct((steps, layers, colors, LANES), jnp.float32),
            plane,
            plane,
            jax.ShapeDtypeStruct((layers, colors, LANES), jnp.float32),
            jax.ShapeDtypeStruct((layers // groups, colors, LANES), jnp.float32),
        ),
        in_specs=[pl.BlockSpec(memory_space=pltpu.VMEM)] * (len(pieces) + 1),
        out_specs=[pl.BlockSpec(memory_space=pltpu.VMEM)] * 5,
        scratch_shapes=[
            pltpu.VMEM((steps + 2, layers + 2 * depth, LANES), jnp.float32),
            pltpu.VMEM((steps, layers, LANES), jnp.float32),
            pltpu.VMEM((layers, colors, LANES), jnp.float32),
        ],
        compiler_params=pltpu.CompilerParams(vmem_limit_bytes=20 * MIB),
        cost_estimate=pl.CostEstimate(flops=0, bytes_accessed=0, transcendentals=0),
        name="render_near",
    )(*pieces, table)


def depth_kernel(groups, width, bins, count, *refs):
    pieces = refs[:count]
    near_ref, table_ref, s_ref, start_ref, total_ref, raw, sums, products_ref = refs[count:]
    steps, depth = pieces[0].shape[-3] - 1, pieces[0].shape[-2]
    layers = depth * (count // 2)
    slots = s_ref.shape[1]
    smooth_layers(groups, width, float(bins - 1), True, count, pieces, s_ref, raw)
    edge = bin_edges(bins) + 1.0
    first_bin = lax.broadcasted_iota(jnp.int32, (bins, LANES), 0) == 0

    def count_layer(z, carry):
        acc = [jnp.zeros((bins, LANES), jnp.float32)] * 2
        for step in range(steps):
            row = jnp.broadcast_to(s_ref[step, pl.ds(z, 1), :], (bins, LANES))
            acc[step % 2] = acc[step % 2] + jnp.minimum(row, edge)
        high = acc[0] + acc[1]
        low = jnp.where(first_bin, -1.0 * steps, pltpu.roll(high, 1, 0))
        sums[z] = high - low
        return carry

    lax.fori_loop(0, layers, count_layer, 0, unroll=2)
    count_layer(layers, 0)
    for z in range(layers + 1, slots):
        sums[z] = jnp.zeros((bins, LANES), jnp.float32)
    table = table_ref[...]
    at_once = 8

    def products(chunk, carry):
        wide = [sums[chunk * at_once + k] for k in range(at_once)]
        out = split_sum(table, jnp.concatenate(wide, axis=1))
        for k in range(at_once):
            products_ref[chunk * at_once + k] = out[:, k * LANES:(k + 1) * LANES]
        return carry

    lax.fori_loop(0, slots // at_once, products, 0, unroll=True)
    ahead = near_ref.shape[0]
    total_ref[0:ahead] = near_ref[...]
    scan_quarters(groups, width, products_ref, start_ref, total_ref, ahead)


def far_depths(pieces, near_total, table, groups, width, bins):
    count = len(pieces)
    steps, depth = pieces[0].shape[0] - 1, pieces[0].shape[1]
    layers = depth * (count // 2)
    slots = layers + max(groups, depth)
    colors = table.shape[0]
    limit = 8 * MIB + slots * (LANES * 4) * (bins + 2 * colors)
    return pl.pallas_call(
        functools.partial(depth_kernel, groups, width, bins, count),
        out_shape=(
            jax.ShapeDtypeStruct((steps, slots, LANES), jnp.float32),
            jax.ShapeDtypeStruct((slots, colors, LANES), jnp.float32),
            jax.ShapeDtypeStruct((near_total.shape[0] + slots // groups, colors, LANES),
                                 jnp.float32),
        ),
        in_specs=[pl.BlockSpec(memory_space=pltpu.VMEM)] * (count + 2),
        out_specs=[pl.BlockSpec(memory_space=pltpu.VMEM)] * 3,
        scratch_shapes=[
            pltpu.VMEM((steps + 2, layers + 2 * depth, LANES), jnp.float32),
            pltpu.VMEM((slots, bins, LANES), jnp.float32),
            pltpu.VMEM((slots, colors, LANES), jnp.float32),
        ],
        compiler_params=pltpu.CompilerParams(vmem_limit_bytes=limit),
        cost_estimate=pl.CostEstimate(flops=0, bytes_accessed=0, transcendentals=0),
        name="far_depths",
    )(*pieces, near_total, table)


def render_far(s, table, colors, bins, ratio, layers):
    steps = s.shape[0]
    plane = jax.ShapeDtypeStruct((steps, colors, LANES), jnp.float32)
    return pl.pallas_call(
        functools.partial(render_rows, bins, ratio),
        out_shape=(jax.ShapeDtypeStruct((steps, layers, colors, LANES), jnp.float32), plane, plane),
        in_specs=[pl.BlockSpec(memory_space=pltpu.VMEM)] * 2,
        out_specs=[pl.BlockSpec(memory_space=pltpu.VMEM)] * 3,
        scratch_shapes=[pltpu.VMEM((layers, colors, LANES), jnp.float32)],
        compiler_params=pltpu.CompilerParams(vmem_limit_bytes=20 * MIB),
        cost_estimate=pl.CostEstimate(
            flops=10 ** 10, bytes_accessed=10 ** 7, transcendentals=10 ** 7),
        name="render_far",
    )(s, table)


def join_kernel(groups, width, turn, blocks, columns_ref, *refs):
    near_lit, near_unlit, near_through, near_start = refs[:4]
    far_lit, far_unlit, far_through, far_start = refs[4:8]
    before_refs, out_ref, image, near_light, far_light = refs[8:-4], *refs[-4:]
    rows, colors, _ = image.shape
    layers, far_layers = near_lit.shape[1], far_lit.shape[1]
    me = lax.axis_index("gz")
    lower = me < blocks
    half = (me + turn) % 2
    position = lax.axis_index("gx")
    group = group_ids((colors, LANES), width)
    ahead = layers // groups

    def begin(chunk, start_ref, offset, light):
        packed = jnp.zeros((colors, LANES), jnp.float32)
        for hop, ref in enumerate(before_refs, 1):
            packed = packed + jnp.where(position >= hop, ref[offset + chunk], 0.0)
        for k in range(groups):
            value = jnp.where(group == k, packed, 0.0)
            shift = 1
            while shift < groups:
                value = value + pltpu.roll(value, shift * width, 1)
                shift *= 2
            z = chunk * groups + k
            light[z] = jnp.exp2(start_ref[z] + value)

    def begin_near(chunk, carry):
        begin(chunk, near_start, 0, near_light)
        return carry

    def begin_far(chunk, carry):
        begin(chunk, far_start, ahead, far_light)
        return carry

    lax.fori_loop(0, ahead, begin_near, 0, unroll=4)
    lax.fori_loop(0, far_start.shape[0] // groups, begin_far, 0, unroll=4)
    ambient = columns_ref[1]
    backdrop = columns_ref[2]
    at_once = 4 if rows % 4 == 0 else 2

    def light_rows(chunk, carry):
        place = [chunk * at_once + k for k in range(at_once)]

        def lit_sum(lit, unlit, light, count):
            sums = [unlit[half * rows + row] * ambient for row in place]
            for z in range(count):
                factor = light[z]
                for k, row in enumerate(place):
                    sums[k] = sums[k] + lit[half * rows + row, z] * factor
            return sums

        near = lit_sum(near_lit, near_unlit, near_light, layers)
        far = lit_sum(far_lit, far_unlit, far_light, far_layers)
        for k, row in enumerate(place):
            through = far_through[half * rows + row]
            passed = near_through[half * rows + row]
            front = jnp.where(lower, near[k], far[k])
            back = jnp.where(lower, far[k], near[k])
            image[row] = (front + jnp.where(lower, passed, through) * back
                          + through * passed * backdrop)
        return carry

    lax.fori_loop(0, rows // at_once, light_rows, 0, unroll=2)
    if len(out_ref.shape) == 3:
        out_ref[...] = image[...]
        return
    for chunk in range(rows // groups):
        tiles = swap_groups([image[chunk * groups + k] for k in range(groups)], groups, width)
        for part in range(groups):
            image[chunk * groups + part] = tiles[part]
    for slot in range(groups):
        part = slot ^ (me // 2)
        for chunk in range(rows // groups):
            out_ref[slot, chunk] = image[chunk * groups + part]


def join(columns, near, far, before, groups, width, turn, blocks):
    steps, layers, colors, _ = near[0].shape
    share = steps // 2
    shape = (share, colors, LANES)
    if share % groups == 0:
        shape = (groups, share // groups, colors, LANES)
    operands = [columns, *near, *far, *before]
    return pl.pallas_call(
        functools.partial(join_kernel, groups, width, turn, blocks),
        out_shape=jax.ShapeDtypeStruct(shape, jnp.float32),
        in_specs=[pl.BlockSpec(memory_space=pltpu.VMEM)] * len(operands),
        out_specs=pl.BlockSpec(memory_space=pltpu.VMEM),
        scratch_shapes=[
            pltpu.VMEM((share, colors, LANES), jnp.float32),
            pltpu.VMEM((layers, colors, LANES), jnp.float32),
            pltpu.VMEM((far[3].shape[0], colors, LANES), jnp.float32),
        ],
        compiler_params=pltpu.CompilerParams(vmem_limit_bytes=24 * MIB),
        cost_estimate=pl.CostEstimate(flops=0, bytes_accessed=0, transcendentals=0),
        name="join",
    )(*operands)


def unpack_kernel(groups, width, *refs):
    arrived, out_ref, pieces = refs[:-2], refs[-2], refs[-1]
    count = 2 * len(arrived)
    me = lax.axis_index("gz")
    for apart in range(count):
        pieces[me ^ apart] = arrived[apart // 2][apart % 2]
    for tile in range(count // groups):
        for chunk in range(arrived[0].shape[1]):
            tiles = swap_groups(
                [pieces[tile * groups + part, chunk] for part in range(groups)], groups, width)
            for part in range(groups):
                out_ref[chunk * groups + part, :, tile * LANES:(tile + 1) * LANES] = tiles[part]


def unpack(arrived, groups, width):
    count = 2 * len(arrived)
    _, chunks, colors, _ = arrived[0].shape
    return pl.pallas_call(
        functools.partial(unpack_kernel, groups, width),
        out_shape=jax.ShapeDtypeStruct((chunks * groups, colors, count * width), jnp.float32),
        in_specs=[pl.BlockSpec(memory_space=pltpu.VMEM)] * len(arrived),
        out_specs=pl.BlockSpec(memory_space=pltpu.VMEM),
        scratch_shapes=[pltpu.VMEM((count, chunks, colors, LANES), jnp.float32)],
        compiler_params=pltpu.CompilerParams(vmem_limit_bytes=8 * MIB),
        name="unpack",
    )(*arrived)


def table_kernel(step_x, step_z, bins_ref, extinction_ref, color_ref, columns_ref, sum_ref,
                 split_ref):
    rows, bins = extinction_ref.shape[1], bins_ref.shape[1]
    colors = extinction_ref.shape[0]
    row = lax.broadcasted_iota(jnp.int32, (rows, bins), 0)
    bin_id = lax.broadcasted_iota(jnp.int32, (rows, bins), 1)
    here = (row == bins_ref[0:1, :]).astype(jnp.float32)
    below = ((row == bins_ref[1:2, :]) & (bin_id > 0)).astype(jnp.float32)

    def rise(ref):
        now = jnp.dot(ref[...], here, precision=lax.Precision.HIGHEST,
                      preferred_element_type=jnp.float32)
        then = jnp.dot(ref[...], below, precision=lax.Precision.HIGHEST,
                       preferred_element_type=jnp.float32)
        return now - then

    def split(value):
        coarse = value.astype(jnp.bfloat16)
        fine = (value - coarse.astype(jnp.float32)).astype(jnp.bfloat16)
        return jnp.concatenate([coarse, fine, coarse], axis=1)

    sigma = rise(extinction_ref) * columns_ref[0, :, 0:bins]
    sum_ref[...] = split(sigma * (-step_x * LOG2E))
    split_ref[0:colors] = split(sigma * (-step_z * LOG2E))
    split_ref[colors:2 * colors] = split(rise(color_ref))


def tables(bin_rows, tf_extinction, tf_color, columns, step_x, step_z):
    bins = bin_rows.shape[0]
    colors = tf_color.shape[1]
    shifted = jnp.stack([bin_rows, jnp.roll(bin_rows, 1)])
    return pl.pallas_call(
        functools.partial(table_kernel, step_x, step_z),
        out_shape=(
            jax.ShapeDtypeStruct((colors, 3 * bins), jnp.bfloat16),
            jax.ShapeDtypeStruct((2 * colors, 3 * bins), jnp.bfloat16),
        ),
        in_specs=[pl.BlockSpec(memory_space=pltpu.VMEM)] * 4,
        out_specs=[pl.BlockSpec(memory_space=pltpu.VMEM)] * 2,
        compiler_params=pltpu.CompilerParams(vmem_limit_bytes=4 * MIB),
        name="tables",
    )(shifted, tf_extinction.T, tf_color.T, columns)


def exchange(value, axis, apart):
    pairs = [(source, source ^ apart) for source in range(lax.axis_size(axis))]
    return lax.ppermute(value, axis, pairs)


def local(density, bin_rows, tf_extinction, tf_color, extinction_scale, ambient, backdrop):
    rows_x, depth, width_y = density.shape
    colors = tf_color.shape[1]
    bins = bin_rows.shape[0]
    count = lax.axis_size("gz")
    size_x = lax.axis_size("gx")
    me = lax.axis_index("gz")
    width = width_y // count
    groups = LANES // width
    steps = rows_x // groups
    step_x = 1.0 / (rows_x * size_x)
    step_z = 1.0 / (depth * count)

    up = [(i, (i + 1) % size_x) for i in range(size_x)]
    down = [(j, i) for i, j in up]
    before = lax.ppermute(density[rows_x - 1:], "gx", up)
    after = lax.ppermute(density[:1], "gx", down)

    packed = pack(density, groups, width)
    pieces = list(address(packed, before, after, groups, width))
    for apart in range(1, count):
        give = pieces[apart]
        if apart > count // 2:
            ahead = min(apart - count // 2 + 1, count // 2 - 1)
            give, _ = lax.optimization_barrier((give, pieces[ahead]))
        pieces[apart] = exchange(give, "gz", apart)
    bin_rows, extinction_scale, ambient, backdrop, _ = lax.optimization_barrier(
        (bin_rows, extinction_scale, ambient, backdrop, pieces[2]))
    columns = jnp.broadcast_to(
        jnp.stack([extinction_scale, ambient, backdrop])[:, :, None], (3, colors, LANES))
    sum_table, table = tables(bin_rows, tf_extinction, tf_color, columns, step_x, step_z)

    blocks = count // 2
    ratio = step_x / step_z
    *near, near_total = render_near(
        pieces[:blocks], table, colors, groups, width, bins, ratio, count)
    s, start, total = far_depths(pieces, near_total, sum_table, groups, width, bins)
    sums = [lax.ppermute(total, "gx", [(i, (i + hop) % size_x) for i in range(size_x)])
            for hop in range(1, size_x)]

    layers = depth * blocks
    far = [*render_far(s, table, colors, bins, ratio, layers + 1), start]

    def half_of(turn):
        return join(columns, near, far, sums, groups, width, turn, blocks)

    share = steps // 2
    if share % groups == 0:
        joined = exchange(half_of(1), "gz", 1)
        both = jnp.stack([half_of(0), joined], axis=1)
        arrived = []
        for slot in range(count // 2):
            arrived.append(exchange(both[slot], "gz", 2 * slot) if slot else both[0])
        return unpack(arrived, groups, width)
    halves = [half_of(0), half_of(1)]
    even = me % 2 == 0
    image = jnp.stack([jnp.where(even, halves[0], halves[1]),
                       jnp.where(even, halves[1], halves[0])])
    image = image.reshape(2, share, colors, groups, width).transpose(3, 0, 1, 2, 4)
    image = lax.all_to_all(image.reshape(count, share, colors, width), "gz", 0, 0)
    return image.transpose(1, 2, 0, 3).reshape(share, colors, width_y)


def solution(mesh):
    in_specs = (P("gx", "gz", None), P(), P(), P(), P(), P(), P())
    out_specs = P(("gx", "gz"), None, None)
    return jax.shard_map(local, mesh=mesh, in_specs=in_specs, out_specs=out_specs, check_vma=False)
```

```python
import functools

import jax
import jax.numpy as jnp
from jax import lax
from jax.experimental import pallas as pl
from jax.experimental.pallas import tpu as pltpu
from jax.sharding import PartitionSpec as P

LANES = 128
LOG2E = 1.4426950408889634
MIB = 1 << 20


def group_ids(shape, width):
    return lax.broadcasted_iota(jnp.int32, shape, len(shape) - 1) // width


def swap_groups(tiles, groups, width):
    tiles = list(tiles)
    lane = group_ids(tiles[0].shape, width)
    bit = 1
    while bit < groups:
        upper = (lane & bit) != 0
        shift = bit * width
        for first in range(groups):
            if first & bit:
                continue
            a, b = tiles[first], tiles[first | bit]
            axis = a.ndim - 1
            tiles[first] = jnp.where(upper, pltpu.roll(b, shift, axis), a)
            tiles[first | bit] = jnp.where(upper, b, pltpu.roll(a, LANES - shift, axis))
        bit *= 2
    return tiles


def blur_rows(parts, lane):
    out = []
    for tiles in parts:
        axis = tiles[0].ndim - 1
        up = [pltpu.roll(tile, 1, axis) for tile in tiles]
        down = [pltpu.roll(tile, LANES - 1, axis) for tile in tiles]
        row = []
        for t in range(len(tiles)):
            before = up[t - 1] if t > 0 else jnp.zeros_like(up[0])
            after = down[t + 1] if t + 1 < len(tiles) else jnp.zeros_like(up[0])
            low = jnp.where(lane == 0, before, up[t])
            high = jnp.where(lane == LANES - 1, after, down[t])
            row.append(low + 2.0 * tiles[t] + high)
        out.append(row)
    return out


def pack_kernel(groups, width, x_ref, out_ref):
    tile_count = x_ref.shape[3] // LANES
    steps, depth = x_ref.shape[1], x_ref.shape[2]
    size = 4
    lane = lax.broadcasted_iota(jnp.int32, (size, depth, LANES), 2)
    for first in range(0, steps, size):
        place = pl.ds(first, size)
        wide = blur_rows(
            [[x_ref[group, place, :, t * LANES:(t + 1) * LANES] for t in range(tile_count)]
             for group in range(groups)], lane)
        for t in range(tile_count):
            swapped = swap_groups([wide[group][t] for group in range(groups)], groups, width)
            for group in range(groups):
                out_ref[t * groups + group, place] = swapped[group]


def pack(x, groups, width):
    steps = x.shape[0] // groups
    blocks = x.shape[2] // width
    depth, width_y = x.shape[1:]
    return pl.pallas_call(
        functools.partial(pack_kernel, groups, width),
        out_shape=jax.ShapeDtypeStruct((blocks, steps, depth, LANES), jnp.float32),
        in_specs=[pl.BlockSpec(memory_space=pltpu.VMEM)],
        out_specs=pl.BlockSpec(memory_space=pltpu.VMEM),
        compiler_params=pltpu.CompilerParams(vmem_limit_bytes=8 * MIB),
        name="pack",
    )(x.reshape(groups, steps, depth, width_y))


def address_kernel(groups, width, packed_ref, before_ref, after_ref, *refs):
    out_refs, halo = refs[:-1], refs[-1]
    count, steps, depth, _ = packed_ref.shape
    me = lax.axis_index("gz")
    tile_count = before_ref.shape[2] // LANES
    lane = lax.broadcasted_iota(jnp.int32, (depth, LANES), 1)
    position = lax.axis_index("gx")
    inside = (position > 0, position < lax.axis_size("gx") - 1)
    ends = blur_rows(
        [[jnp.where(there, ref[0, :, t * LANES:(t + 1) * LANES], 0.0) for t in range(tile_count)]
         for ref, there in zip((before_ref, after_ref), inside)], lane)
    for t in range(tile_count):
        tiles = [ends[0][t]] * (groups - 1) + [ends[1][t]]
        swapped = swap_groups(tiles, groups, width)
        for part in range(groups):
            halo[t * groups + part] = swapped[part]
    for apart, out_ref in enumerate(out_refs):
        out_ref[0:steps] = packed_ref[me ^ apart]
        out_ref[steps] = halo[me ^ apart]


def address(packed, before, after, groups, width):
    count, steps, depth, _ = packed.shape
    shape = jax.ShapeDtypeStruct((steps + 1, depth, LANES), jnp.float32)
    return pl.pallas_call(
        functools.partial(address_kernel, groups, width),
        out_shape=[shape] * count,
        in_specs=[pl.BlockSpec(memory_space=pltpu.VMEM)] * 3,
        out_specs=[pl.BlockSpec(memory_space=pltpu.VMEM)] * count,
        scratch_shapes=[pltpu.VMEM((count, depth, LANES), jnp.float32)],
        compiler_params=pltpu.CompilerParams(vmem_limit_bytes=8 * MIB),
        name="address",
    )(packed, before, after)


def split_sum(table, wide):
    coarse = wide.astype(jnp.bfloat16)
    fine = (wide - coarse.astype(jnp.float32)).astype(jnp.bfloat16)
    weights = jnp.concatenate([coarse, coarse, fine], axis=0)
    return jnp.dot(table, weights, preferred_element_type=jnp.float32)


def smooth_layers(groups, width, scale, far, count, pieces, s_ref, raw):
    steps, depth = pieces[0].shape[-3] - 1, pieces[0].shape[-2]
    blocks = count // 2
    layers = depth * blocks
    slots = s_ref.shape[1]
    me = lax.axis_index("gz")
    lower = me < blocks
    lane = group_ids((depth, LANES), width)

    def place_piece(piece, row):
        place = pl.ds(row, depth)
        raw[1:steps + 1, place, :] = piece[0:steps]
        halo = piece[steps]
        low = pltpu.roll(piece[steps - 1], width, 1)
        high = pltpu.roll(piece[0], LANES - width, 1)
        raw[0, place, :] = jnp.where(lane == 0, halo, low)
        raw[steps + 1, place, :] = jnp.where(lane == groups - 1, halo, high)

    zeros = jnp.zeros((steps + 2, depth, LANES), jnp.float32)
    raw[:, 0:depth, :] = zeros
    raw[:, depth + layers:2 * depth + layers, :] = zeros
    for apart in range(len(pieces)):
        block = (me ^ apart) % blocks
        if far and apart < blocks:
            @pl.when(block == jnp.where(lower, blocks - 1, 0))
            def _():
                row = jnp.where(lower, 0, depth + layers)
                place_piece(pieces[apart], pl.multiple_of(row, 8))
        else:
            place_piece(pieces[apart], pl.multiple_of(depth + block * depth, 8))
    slot = lax.broadcasted_iota(jnp.int32, (layers + depth, LANES), 0)
    if far:
        empty = slot > layers
        if slots > layers + depth:
            s_ref[:, layers + depth:slots, :] = jnp.full(
                (steps, slots - layers - depth, LANES), -1.0, jnp.float32)
    else:
        empty = (slot == jnp.where(lower, layers - 1, 0))[:layers]

    def smooth(step, carry):
        v = raw[step] + 2.0 * raw[step + 1] + raw[step + 2]
        size = v.shape[0]
        before = pltpu.roll(v, 1, 0)
        after = pltpu.roll(v, size - 1, 0)
        total = (before + 2.0 * v + after) * (scale / 64.0)
        if far:
            shifted = pltpu.roll(total, size - (depth - 1), 0)[:layers + depth]
            value = jnp.where(lower, shifted, total[depth:2 * depth + layers])
            s_ref[step, 0:layers + depth] = jnp.where(empty, -1.0, value)
        else:
            s_ref[step] = jnp.where(empty, -1.0, total[depth:depth + layers])
        return carry

    lax.fori_loop(0, steps, smooth, 0, unroll=2)


def scan_quarters(groups, width, sums_ref, start_ref, total_ref, offset):
    slots, colors = sums_ref.shape[0], sums_ref.shape[1]
    group = group_ids((colors, LANES), width)

    def scan_groups(chunk, carry):
        packed = jnp.zeros((colors, LANES), jnp.float32)
        for k in range(groups):
            z = chunk * groups + k
            both = sums_ref[z]
            inclusive = both
            everything = both
            shift = 1
            while shift < groups:
                moved = pltpu.roll(inclusive, shift * width, 1)
                inclusive = inclusive + jnp.where(group >= shift, moved, 0.0)
                everything = everything + pltpu.roll(everything, shift * width, 1)
                shift *= 2
            start_ref[z] = inclusive - both
            packed = jnp.where(group == k, everything, packed)
        total_ref[offset + chunk] = packed
        return carry

    lax.fori_loop(0, slots // groups, scan_groups, 0, unroll=4)


def bin_edges(bins):
    return lax.broadcasted_iota(jnp.int32, (bins, LANES), 0).astype(jnp.float32) - 1.0


def properties(s, size, table, bins):
    edge = bin_edges(bins).astype(jnp.bfloat16)
    zero = jnp.zeros((bins, LANES), jnp.bfloat16)
    one = jnp.ones((bins, LANES), jnp.bfloat16)
    lower_bin = jnp.floor(s)
    frac = s - lower_bin
    coarse = frac.astype(jnp.bfloat16).astype(jnp.float32)
    fine = frac - coarse

    def wide(value, r):
        return jnp.broadcast_to(value[r:r + 1], (bins, LANES)).astype(jnp.bfloat16)

    columns = []
    for r in range(size):
        away = wide(lower_bin, r) - edge
        main = jnp.minimum(jnp.maximum(away + wide(coarse, r), zero), one)
        rest = jnp.where(away == zero, wide(fine, r), zero)
        columns.append(jnp.concatenate([main, main, rest], axis=0))
    return jnp.dot(table, jnp.concatenate(columns, axis=1), preferred_element_type=jnp.float32)


def render_rows(bins, ratio, s_ref, table_ref, lit_ref, unlit_ref, through_ref, depth):
    steps, layers, colors, _ = lit_ref.shape
    depth[...] = jnp.zeros(depth.shape, jnp.float32)
    table = table_ref[...]
    block = 8

    def advance(step, carry):
        through = jnp.ones((colors, LANES), jnp.float32)
        unlit = jnp.zeros((colors, LANES), jnp.float32)
        for place in range(0, layers, block):
            size = min(block, layers - place)
            props = properties(s_ref[step, place:place + block, :], size, table, bins)
            for r in range(size):
                part = props[:, r * LANES:(r + 1) * LANES]
                sigma, color = part[:colors], part[colors:]
                later = through * jnp.exp2(sigma)
                seen = (through - later) * color
                above = depth[place + r]
                unlit = unlit + seen
                lit_ref[step, place + r] = seen * jnp.exp2(above)
                depth[place + r] = above + sigma * ratio
                through = later
        unlit_ref[step], through_ref[step] = unlit, through
        return carry

    lax.fori_loop(0, steps, advance, 0, unroll=4)


def near_kernel(groups, width, bins, ratio, count, *refs):
    pieces = refs[:count // 2]
    (table_ref, lit_ref, unlit_ref, through_ref, start_ref, total_ref, raw, s_ref,
     depth) = refs[count // 2:]
    smooth_layers(groups, width, float(bins - 1), False, count, pieces, s_ref, raw)
    render_rows(bins, ratio, s_ref, table_ref, lit_ref, unlit_ref, through_ref, depth)
    scan_quarters(groups, width, depth, start_ref, total_ref, 0)


def render_near(pieces, table, colors, groups, width, bins, ratio, count):
    steps, depth = pieces[0].shape[0] - 1, pieces[0].shape[1]
    layers = depth * len(pieces)
    plane = jax.ShapeDtypeStruct((steps, colors, LANES), jnp.float32)
    return pl.pallas_call(
        functools.partial(near_kernel, groups, width, bins, ratio, count),
        out_shape=(
            jax.ShapeDtypeStruct((steps, layers, colors, LANES), jnp.float32),
            plane,
            plane,
            jax.ShapeDtypeStruct((layers, colors, LANES), jnp.float32),
            jax.ShapeDtypeStruct((layers // groups, colors, LANES), jnp.float32),
        ),
        in_specs=[pl.BlockSpec(memory_space=pltpu.VMEM)] * (len(pieces) + 1),
        out_specs=[pl.BlockSpec(memory_space=pltpu.VMEM)] * 5,
        scratch_shapes=[
            pltpu.VMEM((steps + 2, layers + 2 * depth, LANES), jnp.float32),
            pltpu.VMEM((steps, layers, LANES), jnp.float32),
            pltpu.VMEM((layers, colors, LANES), jnp.float32),
        ],
        compiler_params=pltpu.CompilerParams(vmem_limit_bytes=20 * MIB),
        cost_estimate=pl.CostEstimate(flops=0, bytes_accessed=0, transcendentals=0),
        name="render_near",
    )(*pieces, table)


def depth_kernel(groups, width, bins, count, *refs):
    pieces = refs[:count]
    near_ref, table_ref, s_ref, start_ref, total_ref, raw, sums, products_ref = refs[count:]
    steps, depth = pieces[0].shape[-3] - 1, pieces[0].shape[-2]
    layers = depth * (count // 2)
    slots = s_ref.shape[1]
    smooth_layers(groups, width, float(bins - 1), True, count, pieces, s_ref, raw)
    edge = bin_edges(bins) + 1.0
    first_bin = lax.broadcasted_iota(jnp.int32, (bins, LANES), 0) == 0

    def count_layer(z, carry):
        acc = [jnp.zeros((bins, LANES), jnp.float32)] * 2
        for step in range(steps):
            row = jnp.broadcast_to(s_ref[step, pl.ds(z, 1), :], (bins, LANES))
            acc[step % 2] = acc[step % 2] + jnp.minimum(row, edge)
        high = acc[0] + acc[1]
        low = jnp.where(first_bin, -1.0 * steps, pltpu.roll(high, 1, 0))
        sums[z] = high - low
        return carry

    lax.fori_loop(0, layers, count_layer, 0, unroll=2)
    count_layer(layers, 0)
    for z in range(layers + 1, slots):
        sums[z] = jnp.zeros((bins, LANES), jnp.float32)
    table = table_ref[...]
    at_once = 8

    def products(chunk, carry):
        wide = [sums[chunk * at_once + k] for k in range(at_once)]
        out = split_sum(table, jnp.concatenate(wide, axis=1))
        for k in range(at_once):
            products_ref[chunk * at_once + k] = out[:, k * LANES:(k + 1) * LANES]
        return carry

    lax.fori_loop(0, slots // at_once, products, 0, unroll=True)
    ahead = near_ref.shape[0]
    total_ref[0:ahead] = near_ref[...]
    scan_quarters(groups, width, products_ref, start_ref, total_ref, ahead)


def far_depths(pieces, near_total, table, groups, width, bins):
    count = len(pieces)
    steps, depth = pieces[0].shape[0] - 1, pieces[0].shape[1]
    layers = depth * (count // 2)
    slots = layers + max(groups, depth)
    colors = table.shape[0]
    limit = 8 * MIB + slots * (LANES * 4) * (bins + 2 * colors)
    return pl.pallas_call(
        functools.partial(depth_kernel, groups, width, bins, count),
        out_shape=(
            jax.ShapeDtypeStruct((steps, slots, LANES), jnp.float32),
            jax.ShapeDtypeStruct((slots, colors, LANES), jnp.float32),
            jax.ShapeDtypeStruct((near_total.shape[0] + slots // groups, colors, LANES),
                                 jnp.float32),
        ),
        in_specs=[pl.BlockSpec(memory_space=pltpu.VMEM)] * (count + 2),
        out_specs=[pl.BlockSpec(memory_space=pltpu.VMEM)] * 3,
        scratch_shapes=[
            pltpu.VMEM((steps + 2, layers + 2 * depth, LANES), jnp.float32),
            pltpu.VMEM((slots, bins, LANES), jnp.float32),
            pltpu.VMEM((slots, colors, LANES), jnp.float32),
        ],
        compiler_params=pltpu.CompilerParams(vmem_limit_bytes=limit),
        cost_estimate=pl.CostEstimate(flops=0, bytes_accessed=0, transcendentals=0),
        name="far_depths",
    )(*pieces, near_total, table)


def render_far(s, table, colors, bins, ratio, layers):
    steps = s.shape[0]
    plane = jax.ShapeDtypeStruct((steps, colors, LANES), jnp.float32)
    return pl.pallas_call(
        functools.partial(render_rows, bins, ratio),
        out_shape=(jax.ShapeDtypeStruct((steps, layers, colors, LANES), jnp.float32), plane, plane),
        in_specs=[pl.BlockSpec(memory_space=pltpu.VMEM)] * 2,
        out_specs=[pl.BlockSpec(memory_space=pltpu.VMEM)] * 3,
        scratch_shapes=[pltpu.VMEM((layers, colors, LANES), jnp.float32)],
        compiler_params=pltpu.CompilerParams(vmem_limit_bytes=20 * MIB),
        cost_estimate=pl.CostEstimate(
            flops=10 ** 10, bytes_accessed=10 ** 7, transcendentals=10 ** 7),
        name="render_far",
    )(s, table)


def join_kernel(groups, width, turn, blocks, columns_ref, *refs):
    near_lit, near_unlit, near_through, far_lit, far_unlit, far_through = refs[:6]
    if turn:
        near_start, far_start = refs[6:8]
        before_refs, out_ref, near_light, far_light, image = refs[8:-4], *refs[-4:]
    else:
        near_light, far_light, out_ref, image = refs[6:]
    rows, colors, _ = image.shape
    layers, far_layers = near_lit.shape[1], far_lit.shape[1]
    me = lax.axis_index("gz")
    lower = me < blocks
    half = (me + turn) % 2
    position = lax.axis_index("gx")
    group = group_ids((colors, LANES), width)
    ahead = layers // groups

    def begin(chunk, start_ref, offset, light):
        packed = jnp.zeros((colors, LANES), jnp.float32)
        for hop, ref in enumerate(before_refs, 1):
            packed = packed + jnp.where(position >= hop, ref[offset + chunk], 0.0)
        for k in range(groups):
            value = jnp.where(group == k, packed, 0.0)
            shift = 1
            while shift < groups:
                value = value + pltpu.roll(value, shift * width, 1)
                shift *= 2
            z = chunk * groups + k
            light[z] = jnp.exp2(start_ref[z] + value)

    def begin_near(chunk, carry):
        begin(chunk, near_start, 0, near_light)
        return carry

    def begin_far(chunk, carry):
        begin(chunk, far_start, ahead, far_light)
        return carry

    if turn:
        lax.fori_loop(0, ahead, begin_near, 0, unroll=4)
        lax.fori_loop(0, far_start.shape[0] // groups, begin_far, 0, unroll=4)
    ambient = columns_ref[1]
    backdrop = columns_ref[2]
    at_once = 4 if rows % 4 == 0 else 2

    def light_rows(chunk, carry):
        place = [chunk * at_once + k for k in range(at_once)]

        def lit_sum(lit, unlit, light, count):
            sums = [unlit[half * rows + row] * ambient for row in place]
            for z in range(count):
                factor = light[z]
                for k, row in enumerate(place):
                    sums[k] = sums[k] + lit[half * rows + row, z] * factor
            return sums

        near = lit_sum(near_lit, near_unlit, near_light, layers)
        far = lit_sum(far_lit, far_unlit, far_light, far_layers)
        for k, row in enumerate(place):
            through = far_through[half * rows + row]
            passed = near_through[half * rows + row]
            front = jnp.where(lower, near[k], far[k])
            back = jnp.where(lower, far[k], near[k])
            image[row] = (front + jnp.where(lower, passed, through) * back
                          + through * passed * backdrop)
        return carry

    lax.fori_loop(0, rows // at_once, light_rows, 0, unroll=2)
    if len(out_ref.shape) == 3:
        out_ref[...] = image[...]
        return
    for chunk in range(rows // groups):
        tiles = swap_groups([image[chunk * groups + k] for k in range(groups)], groups, width)
        for part in range(groups):
            image[chunk * groups + part] = tiles[part]
    for slot in range(groups):
        part = slot ^ (me // 2)
        for chunk in range(rows // groups):
            out_ref[slot, chunk] = image[chunk * groups + part]


def join(columns, near, far, light, groups, width, turn, blocks):
    steps, layers, colors, _ = near[0].shape
    share = steps // 2
    shape = (share, colors, LANES)
    if share % groups == 0:
        shape = (groups, share // groups, colors, LANES)
    shapes = [jax.ShapeDtypeStruct(shape, jnp.float32)]
    if turn:
        shapes += [jax.ShapeDtypeStruct(start.shape, jnp.float32) for start in light[:2]]
    operands = [columns, *near, *far, *light]
    return pl.pallas_call(
        functools.partial(join_kernel, groups, width, turn, blocks),
        out_shape=shapes,
        in_specs=[pl.BlockSpec(memory_space=pltpu.VMEM)] * len(operands),
        out_specs=[pl.BlockSpec(memory_space=pltpu.VMEM)] * len(shapes),
        scratch_shapes=[pltpu.VMEM((share, colors, LANES), jnp.float32)],
        compiler_params=pltpu.CompilerParams(vmem_limit_bytes=24 * MIB),
        cost_estimate=pl.CostEstimate(flops=0, bytes_accessed=0, transcendentals=0),
        name="join",
    )(*operands)


def unpack_kernel(groups, width, *refs):
    arrived, out_ref, pieces = refs[:-2], refs[-2], refs[-1]
    count = 2 * len(arrived)
    me = lax.axis_index("gz")
    for apart in range(count):
        pieces[me ^ apart] = arrived[apart // 2][apart % 2]
    for tile in range(count // groups):
        for chunk in range(arrived[0].shape[1]):
            tiles = swap_groups(
                [pieces[tile * groups + part, chunk] for part in range(groups)], groups, width)
            for part in range(groups):
                out_ref[chunk * groups + part, :, tile * LANES:(tile + 1) * LANES] = tiles[part]


def unpack(arrived, groups, width):
    count = 2 * len(arrived)
    _, chunks, colors, _ = arrived[0].shape
    return pl.pallas_call(
        functools.partial(unpack_kernel, groups, width),
        out_shape=jax.ShapeDtypeStruct((chunks * groups, colors, count * width), jnp.float32),
        in_specs=[pl.BlockSpec(memory_space=pltpu.VMEM)] * len(arrived),
        out_specs=pl.BlockSpec(memory_space=pltpu.VMEM),
        scratch_shapes=[pltpu.VMEM((count, chunks, colors, LANES), jnp.float32)],
        compiler_params=pltpu.CompilerParams(vmem_limit_bytes=8 * MIB),
        name="unpack",
    )(*arrived)


def table_kernel(step_x, step_z, bins_ref, extinction_ref, color_ref, columns_ref, sum_ref,
                 split_ref):
    rows, bins = extinction_ref.shape[1], bins_ref.shape[1]
    colors = extinction_ref.shape[0]
    row = lax.broadcasted_iota(jnp.int32, (rows, bins), 0)
    bin_id = lax.broadcasted_iota(jnp.int32, (rows, bins), 1)
    here = (row == bins_ref[0:1, :]).astype(jnp.float32)
    below = ((row == bins_ref[1:2, :]) & (bin_id > 0)).astype(jnp.float32)

    def rise(ref):
        now = jnp.dot(ref[...], here, precision=lax.Precision.HIGHEST,
                      preferred_element_type=jnp.float32)
        then = jnp.dot(ref[...], below, precision=lax.Precision.HIGHEST,
                       preferred_element_type=jnp.float32)
        return now - then

    def split(value):
        coarse = value.astype(jnp.bfloat16)
        fine = (value - coarse.astype(jnp.float32)).astype(jnp.bfloat16)
        return jnp.concatenate([coarse, fine, coarse], axis=1)

    sigma = rise(extinction_ref) * columns_ref[0, :, 0:bins]
    sum_ref[...] = split(sigma * (-step_x * LOG2E))
    split_ref[0:colors] = split(sigma * (-step_z * LOG2E))
    split_ref[colors:2 * colors] = split(rise(color_ref))


def tables(bin_rows, tf_extinction, tf_color, columns, step_x, step_z):
    bins = bin_rows.shape[0]
    colors = tf_color.shape[1]
    shifted = jnp.stack([bin_rows, jnp.roll(bin_rows, 1)])
    return pl.pallas_call(
        functools.partial(table_kernel, step_x, step_z),
        out_shape=(
            jax.ShapeDtypeStruct((colors, 3 * bins), jnp.bfloat16),
            jax.ShapeDtypeStruct((2 * colors, 3 * bins), jnp.bfloat16),
        ),
        in_specs=[pl.BlockSpec(memory_space=pltpu.VMEM)] * 4,
        out_specs=[pl.BlockSpec(memory_space=pltpu.VMEM)] * 2,
        compiler_params=pltpu.CompilerParams(vmem_limit_bytes=4 * MIB),
        name="tables",
    )(shifted, tf_extinction.T, tf_color.T, columns)


def exchange(value, axis, apart):
    pairs = [(source, source ^ apart) for source in range(lax.axis_size(axis))]
    return lax.ppermute(value, axis, pairs)


def local(density, bin_rows, tf_extinction, tf_color, extinction_scale, ambient, backdrop):
    rows_x, depth, width_y = density.shape
    colors = tf_color.shape[1]
    bins = bin_rows.shape[0]
    count = lax.axis_size("gz")
    size_x = lax.axis_size("gx")
    me = lax.axis_index("gz")
    width = width_y // count
    groups = LANES // width
    steps = rows_x // groups
    step_x = 1.0 / (rows_x * size_x)
    step_z = 1.0 / (depth * count)

    up = [(i, (i + 1) % size_x) for i in range(size_x)]
    down = [(j, i) for i, j in up]
    before = lax.ppermute(density[rows_x - 1:], "gx", up)
    after = lax.ppermute(density[:1], "gx", down)

    packed = pack(density, groups, width)
    pieces = list(address(packed, before, after, groups, width))
    for apart in range(1, count):
        give = pieces[apart]
        if apart > count // 2:
            ahead = min(apart - count // 2 + 1, count // 2 - 1)
            give, _ = lax.optimization_barrier((give, pieces[ahead]))
        pieces[apart] = exchange(give, "gz", apart)
    bin_rows, extinction_scale, ambient, backdrop, _ = lax.optimization_barrier(
        (bin_rows, extinction_scale, ambient, backdrop, pieces[2]))
    columns = jnp.broadcast_to(
        jnp.stack([extinction_scale, ambient, backdrop])[:, :, None], (3, colors, LANES))
    sum_table, table = tables(bin_rows, tf_extinction, tf_color, columns, step_x, step_z)

    blocks = count // 2
    ratio = step_x / step_z
    *near, near_start, near_total = render_near(
        pieces[:blocks], table, colors, groups, width, bins, ratio, count)
    s, start, total = far_depths(pieces, near_total, sum_table, groups, width, bins)
    sums = [lax.ppermute(total, "gx", [(i, (i + hop) % size_x) for i in range(size_x)])
            for hop in range(1, size_x)]

    layers = depth * blocks
    far = render_far(s, table, colors, bins, ratio, layers + 1)
    other, *light = join(
        columns, near, far, [near_start, start, *sums], groups, width, 1, blocks)

    share = steps // 2
    if share % groups == 0:
        joined = exchange(other, "gz", 1)
        own, = join(columns, near, far, light, groups, width, 0, blocks)
        both = jnp.stack([own, joined], axis=1)
        arrived = []
        for slot in range(count // 2):
            arrived.append(exchange(both[slot], "gz", 2 * slot) if slot else both[0])
        return unpack(arrived, groups, width)
    halves = [*join(columns, near, far, light, groups, width, 0, blocks), other]
    even = me % 2 == 0
    image = jnp.stack([jnp.where(even, halves[0], halves[1]),
                       jnp.where(even, halves[1], halves[0])])
    image = image.reshape(2, share, colors, groups, width).transpose(3, 0, 1, 2, 4)
    image = lax.all_to_all(image.reshape(count, share, colors, width), "gz", 0, 0)
    return image.transpose(1, 2, 0, 3).reshape(share, colors, width_y)


def solution(mesh):
    in_specs = (P("gx", "gz", None), P(), P(), P(), P(), P(), P())
    out_specs = P(("gx", "gz"), None, None)
    return jax.shard_map(local, mesh=mesh, in_specs=in_specs, out_specs=out_specs, check_vma=False)
```

```python
import functools

import jax
import jax.numpy as jnp
from jax import lax
from jax.experimental import pallas as pl
from jax.experimental.pallas import tpu as pltpu
from jax.sharding import PartitionSpec as P

LANES = 128
LOG2E = 1.4426950408889634
MIB = 1 << 20


def group_ids(shape, width):
    return lax.broadcasted_iota(jnp.int32, shape, len(shape) - 1) // width


def swap_groups(tiles, groups, width):
    tiles = list(tiles)
    lane = group_ids(tiles[0].shape, width)
    bit = 1
    while bit < groups:
        upper = (lane & bit) != 0
        shift = bit * width
        for first in range(groups):
            if first & bit:
                continue
            a, b = tiles[first], tiles[first | bit]
            axis = a.ndim - 1
            if 2 * shift == LANES:
                moved = pltpu.roll(jnp.where(upper, a, b), shift, axis)
                tiles[first] = jnp.where(upper, moved, a)
                tiles[first | bit] = jnp.where(upper, b, moved)
            else:
                tiles[first] = jnp.where(upper, pltpu.roll(b, shift, axis), a)
                tiles[first | bit] = jnp.where(upper, b, pltpu.roll(a, LANES - shift, axis))
        bit *= 2
    return tiles


def blur_rows(parts, lane):
    out = []
    for tiles in parts:
        axis = tiles[0].ndim - 1
        up = [pltpu.roll(tile, 1, axis) for tile in tiles]
        down = [pltpu.roll(tile, LANES - 1, axis) for tile in tiles]
        row = []
        for t in range(len(tiles)):
            before = up[t - 1] if t > 0 else jnp.zeros_like(up[0])
            after = down[t + 1] if t + 1 < len(tiles) else jnp.zeros_like(up[0])
            low = jnp.where(lane == 0, before, up[t])
            high = jnp.where(lane == LANES - 1, after, down[t])
            row.append(low + 2.0 * tiles[t] + high)
        out.append(row)
    return out


def pack_kernel(groups, width, x_ref, out_ref, blurred):
    tile_count = x_ref.shape[3] // LANES
    steps, depth, width_y = x_ref.shape[1:]
    row = lax.broadcasted_iota(jnp.int32, (width_y, width_y), 0)
    column = lax.broadcasted_iota(jnp.int32, (width_y, width_y), 1)
    weights = jnp.maximum(2 - jnp.abs(row - column), 0).astype(jnp.float32).astype(jnp.bfloat16)
    for group in range(groups):
        x = x_ref[group].reshape(steps * depth, width_y)
        coarse = x.astype(jnp.bfloat16)
        fine = (x - coarse.astype(jnp.float32)).astype(jnp.bfloat16)
        blurred[group] = (jnp.dot(coarse, weights, preferred_element_type=jnp.float32)
                          + jnp.dot(fine, weights, preferred_element_type=jnp.float32)
                          ).reshape(steps, depth, width_y)
    size = 4
    for first in range(0, steps, size):
        place = pl.ds(first, size)
        for t in range(tile_count):
            swapped = swap_groups(
                [blurred[group, place, :, t * LANES:(t + 1) * LANES] for group in range(groups)],
                groups, width)
            for group in range(groups):
                out_ref[t * groups + group, place] = swapped[group]


def pack(x, groups, width):
    steps = x.shape[0] // groups
    blocks = x.shape[2] // width
    depth, width_y = x.shape[1:]
    return pl.pallas_call(
        functools.partial(pack_kernel, groups, width),
        out_shape=jax.ShapeDtypeStruct((blocks, steps, depth, LANES), jnp.float32),
        in_specs=[pl.BlockSpec(memory_space=pltpu.VMEM)],
        out_specs=pl.BlockSpec(memory_space=pltpu.VMEM),
        scratch_shapes=[pltpu.VMEM((groups, steps, depth, width_y), jnp.float32)],
        compiler_params=pltpu.CompilerParams(vmem_limit_bytes=8 * MIB),
        name="pack",
    )(x.reshape(groups, steps, depth, width_y))


def address_kernel(groups, width, packed_ref, before_ref, after_ref, *refs):
    out_refs, halo = refs[:-1], refs[-1]
    count, steps, depth, _ = packed_ref.shape
    me = lax.axis_index("gz")
    tile_count = before_ref.shape[2] // LANES
    lane = lax.broadcasted_iota(jnp.int32, (depth, LANES), 1)
    position = lax.axis_index("gx")
    inside = (position > 0, position < lax.axis_size("gx") - 1)
    ends = blur_rows(
        [[jnp.where(there, ref[0, :, t * LANES:(t + 1) * LANES], 0.0) for t in range(tile_count)]
         for ref, there in zip((before_ref, after_ref), inside)], lane)
    for t in range(tile_count):
        tiles = [ends[0][t]] * (groups - 1) + [ends[1][t]]
        swapped = swap_groups(tiles, groups, width)
        for part in range(groups):
            halo[t * groups + part] = swapped[part]
    for apart, out_ref in enumerate(out_refs):
        out_ref[0:steps] = packed_ref[me ^ apart]
        out_ref[steps] = halo[me ^ apart]


def address(packed, before, after, groups, width):
    count, steps, depth, _ = packed.shape
    shape = jax.ShapeDtypeStruct((steps + 1, depth, LANES), jnp.float32)
    return pl.pallas_call(
        functools.partial(address_kernel, groups, width),
        out_shape=[shape] * count,
        in_specs=[pl.BlockSpec(memory_space=pltpu.VMEM)] * 3,
        out_specs=[pl.BlockSpec(memory_space=pltpu.VMEM)] * count,
        scratch_shapes=[pltpu.VMEM((count, depth, LANES), jnp.float32)],
        compiler_params=pltpu.CompilerParams(vmem_limit_bytes=8 * MIB),
        name="address",
    )(packed, before, after)


def split_sum(table, wide):
    coarse = wide.astype(jnp.bfloat16)
    fine = (wide - coarse.astype(jnp.float32)).astype(jnp.bfloat16)
    weights = jnp.concatenate([coarse, coarse, fine], axis=0)
    return jnp.dot(table, weights, preferred_element_type=jnp.float32)


def smooth_layers(groups, width, scale, far, count, pieces, s_ref, raw):
    steps, depth = pieces[0].shape[-3] - 1, pieces[0].shape[-2]
    blocks = count // 2
    layers = depth * blocks
    slots = s_ref.shape[1]
    me = lax.axis_index("gz")
    lower = me < blocks
    lane = group_ids((depth, LANES), width)

    def place_piece(piece, row):
        place = pl.ds(row, depth)
        raw[1:steps + 1, place, :] = piece[0:steps]
        halo = piece[steps]
        low = pltpu.roll(piece[steps - 1], width, 1)
        high = pltpu.roll(piece[0], LANES - width, 1)
        raw[0, place, :] = jnp.where(lane == 0, halo, low)
        raw[steps + 1, place, :] = jnp.where(lane == groups - 1, halo, high)

    zeros = jnp.zeros((steps + 2, depth, LANES), jnp.float32)
    raw[:, 0:depth, :] = zeros
    raw[:, depth + layers:2 * depth + layers, :] = zeros
    for apart in range(len(pieces)):
        block = (me ^ apart) % blocks
        if far and apart < blocks:
            @pl.when(block == jnp.where(lower, blocks - 1, 0))
            def _():
                row = jnp.where(lower, 0, depth + layers)
                place_piece(pieces[apart], pl.multiple_of(row, 8))
        else:
            place_piece(pieces[apart], pl.multiple_of(depth + block * depth, 8))
    slot = lax.broadcasted_iota(jnp.int32, (layers + depth, LANES), 0)
    if far:
        empty = slot > layers
        if slots > layers + depth:
            s_ref[:, layers + depth:slots, :] = jnp.full(
                (steps, slots - layers - depth, LANES), -1.0, jnp.float32)
    else:
        empty = (slot == jnp.where(lower, layers - 1, 0))[:layers]

    def smooth(step, carry):
        v = raw[step] + 2.0 * raw[step + 1] + raw[step + 2]
        size = v.shape[0]
        before = pltpu.roll(v, 1, 0)
        after = pltpu.roll(v, size - 1, 0)
        total = (before + 2.0 * v + after) * (scale / 64.0)
        if far:
            shifted = pltpu.roll(total, size - (depth - 1), 0)[:layers + depth]
            value = jnp.where(lower, shifted, total[depth:2 * depth + layers])
            s_ref[step, 0:layers + depth] = jnp.where(empty, -1.0, value)
        else:
            s_ref[step] = jnp.where(empty, -1.0, total[depth:depth + layers])
        return carry

    lax.fori_loop(0, steps, smooth, 0, unroll=2)


def scan_quarters(groups, width, sums_ref, start_ref, total_ref, offset):
    slots, colors = sums_ref.shape[0], sums_ref.shape[1]
    group = group_ids((colors, LANES), width)

    def scan_groups(chunk, carry):
        packed = jnp.zeros((colors, LANES), jnp.float32)
        for k in range(groups):
            z = chunk * groups + k
            both = sums_ref[z]
            inclusive = both
            everything = both
            shift = 1
            while shift < groups:
                moved = pltpu.roll(inclusive, shift * width, 1)
                inclusive = inclusive + jnp.where(group >= shift, moved, 0.0)
                everything = everything + pltpu.roll(everything, shift * width, 1)
                shift *= 2
            start_ref[z] = inclusive - both
            packed = jnp.where(group == k, everything, packed)
        total_ref[offset + chunk] = packed
        return carry

    lax.fori_loop(0, slots // groups, scan_groups, 0, unroll=4)


def bin_edges(bins):
    return lax.broadcasted_iota(jnp.int32, (bins, LANES), 0).astype(jnp.float32) - 1.0


def properties(s, size, table, bins):
    edge = bin_edges(bins).astype(jnp.bfloat16)
    zero = jnp.zeros((bins, LANES), jnp.bfloat16)
    one = jnp.ones((bins, LANES), jnp.bfloat16)
    lower_bin = jnp.floor(s)
    frac = s - lower_bin
    coarse = frac.astype(jnp.bfloat16).astype(jnp.float32)
    fine = frac - coarse

    def wide(value, r):
        return jnp.broadcast_to(value[r:r + 1], (bins, LANES)).astype(jnp.bfloat16)

    columns = []
    for r in range(size):
        away = wide(lower_bin, r) - edge
        main = jnp.minimum(jnp.maximum(away + wide(coarse, r), zero), one)
        rest = jnp.where(away == zero, wide(fine, r), zero)
        columns.append(jnp.concatenate([main, main, rest], axis=0))
    return jnp.dot(table, jnp.concatenate(columns, axis=1), preferred_element_type=jnp.float32)


def render_rows(bins, ratio, s_ref, table_ref, lit_ref, unlit_ref, through_ref, depth):
    steps, layers, colors, _ = lit_ref.shape
    depth[...] = jnp.zeros(depth.shape, jnp.float32)
    table = table_ref[...]
    block = 8

    def advance(step, carry):
        through = jnp.ones((colors, LANES), jnp.float32)
        unlit = jnp.zeros((colors, LANES), jnp.float32)
        for place in range(0, layers, block):
            size = min(block, layers - place)
            props = properties(s_ref[step, place:place + block, :], size, table, bins)
            for r in range(size):
                part = props[:, r * LANES:(r + 1) * LANES]
                sigma, color = part[:colors], part[colors:]
                later = through * jnp.exp2(sigma)
                seen = (through - later) * color
                above = depth[place + r]
                unlit = unlit + seen
                lit_ref[step, place + r] = seen * jnp.exp2(above)
                depth[place + r] = above + sigma * ratio
                through = later
        unlit_ref[step], through_ref[step] = unlit, through
        return carry

    lax.fori_loop(0, steps, advance, 0, unroll=4)


def near_kernel(groups, width, bins, ratio, count, *refs):
    pieces = refs[:count // 2]
    (table_ref, lit_ref, unlit_ref, through_ref, start_ref, total_ref, raw, s_ref,
     depth) = refs[count // 2:]
    smooth_layers(groups, width, float(bins - 1), False, count, pieces, s_ref, raw)
    render_rows(bins, ratio, s_ref, table_ref, lit_ref, unlit_ref, through_ref, depth)
    scan_quarters(groups, width, depth, start_ref, total_ref, 0)


def render_near(pieces, table, colors, groups, width, bins, ratio, count):
    steps, depth = pieces[0].shape[0] - 1, pieces[0].shape[1]
    layers = depth * len(pieces)
    plane = jax.ShapeDtypeStruct((steps, colors, LANES), jnp.float32)
    return pl.pallas_call(
        functools.partial(near_kernel, groups, width, bins, ratio, count),
        out_shape=(
            jax.ShapeDtypeStruct((steps, layers, colors, LANES), jnp.float32),
            plane,
            plane,
            jax.ShapeDtypeStruct((layers, colors, LANES), jnp.float32),
            jax.ShapeDtypeStruct((layers // groups, colors, LANES), jnp.float32),
        ),
        in_specs=[pl.BlockSpec(memory_space=pltpu.VMEM)] * (len(pieces) + 1),
        out_specs=[pl.BlockSpec(memory_space=pltpu.VMEM)] * 5,
        scratch_shapes=[
            pltpu.VMEM((steps + 2, layers + 2 * depth, LANES), jnp.float32),
            pltpu.VMEM((steps, layers, LANES), jnp.float32),
            pltpu.VMEM((layers, colors, LANES), jnp.float32),
        ],
        compiler_params=pltpu.CompilerParams(vmem_limit_bytes=20 * MIB),
        cost_estimate=pl.CostEstimate(flops=0, bytes_accessed=0, transcendentals=0),
        name="render_near",
    )(*pieces, table)


def depth_kernel(groups, width, bins, count, *refs):
    pieces = refs[:count]
    near_ref, table_ref, s_ref, start_ref, total_ref, raw, sums, products_ref = refs[count:]
    steps, depth = pieces[0].shape[-3] - 1, pieces[0].shape[-2]
    layers = depth * (count // 2)
    slots = s_ref.shape[1]
    smooth_layers(groups, width, float(bins - 1), True, count, pieces, s_ref, raw)
    edge = bin_edges(bins) + 1.0
    first_bin = lax.broadcasted_iota(jnp.int32, (bins, LANES), 0) == 0

    def count_layer(z, carry):
        acc = [jnp.zeros((bins, LANES), jnp.float32)] * 2
        for step in range(steps):
            row = jnp.broadcast_to(s_ref[step, pl.ds(z, 1), :], (bins, LANES))
            acc[step % 2] = acc[step % 2] + jnp.minimum(row, edge)
        high = acc[0] + acc[1]
        low = jnp.where(first_bin, -1.0 * steps, pltpu.roll(high, 1, 0))
        sums[z] = high - low
        return carry

    lax.fori_loop(0, layers, count_layer, 0, unroll=2)
    count_layer(layers, 0)
    for z in range(layers + 1, slots):
        sums[z] = jnp.zeros((bins, LANES), jnp.float32)
    table = table_ref[...]
    at_once = 8

    def products(chunk, carry):
        wide = [sums[chunk * at_once + k] for k in range(at_once)]
        out = split_sum(table, jnp.concatenate(wide, axis=1))
        for k in range(at_once):
            products_ref[chunk * at_once + k] = out[:, k * LANES:(k + 1) * LANES]
        return carry

    lax.fori_loop(0, slots // at_once, products, 0, unroll=True)
    ahead = near_ref.shape[0]
    total_ref[0:ahead] = near_ref[...]
    scan_quarters(groups, width, products_ref, start_ref, total_ref, ahead)


def far_depths(pieces, near_total, table, groups, width, bins):
    count = len(pieces)
    steps, depth = pieces[0].shape[0] - 1, pieces[0].shape[1]
    layers = depth * (count // 2)
    slots = layers + max(groups, depth)
    colors = table.shape[0]
    limit = 8 * MIB + slots * (LANES * 4) * (bins + 2 * colors)
    return pl.pallas_call(
        functools.partial(depth_kernel, groups, width, bins, count),
        out_shape=(
            jax.ShapeDtypeStruct((steps, slots, LANES), jnp.float32),
            jax.ShapeDtypeStruct((slots, colors, LANES), jnp.float32),
            jax.ShapeDtypeStruct((near_total.shape[0] + slots // groups, colors, LANES),
                                 jnp.float32),
        ),
        in_specs=[pl.BlockSpec(memory_space=pltpu.VMEM)] * (count + 2),
        out_specs=[pl.BlockSpec(memory_space=pltpu.VMEM)] * 3,
        scratch_shapes=[
            pltpu.VMEM((steps + 2, layers + 2 * depth, LANES), jnp.float32),
            pltpu.VMEM((slots, bins, LANES), jnp.float32),
            pltpu.VMEM((slots, colors, LANES), jnp.float32),
        ],
        compiler_params=pltpu.CompilerParams(vmem_limit_bytes=limit),
        cost_estimate=pl.CostEstimate(flops=0, bytes_accessed=0, transcendentals=0),
        name="far_depths",
    )(*pieces, near_total, table)


def render_far(s, table, colors, bins, ratio, layers):
    steps = s.shape[0]
    plane = jax.ShapeDtypeStruct((steps, colors, LANES), jnp.float32)
    return pl.pallas_call(
        functools.partial(render_rows, bins, ratio),
        out_shape=(jax.ShapeDtypeStruct((steps, layers, colors, LANES), jnp.float32), plane, plane),
        in_specs=[pl.BlockSpec(memory_space=pltpu.VMEM)] * 2,
        out_specs=[pl.BlockSpec(memory_space=pltpu.VMEM)] * 3,
        scratch_shapes=[pltpu.VMEM((layers, colors, LANES), jnp.float32)],
        compiler_params=pltpu.CompilerParams(vmem_limit_bytes=20 * MIB),
        cost_estimate=pl.CostEstimate(
            flops=10 ** 10, bytes_accessed=10 ** 7, transcendentals=10 ** 7),
        name="render_far",
    )(s, table)


def join_kernel(groups, width, turn, blocks, columns_ref, *refs):
    near_lit, near_unlit, near_through, far_lit, far_unlit, far_through = refs[:6]
    if turn:
        near_start, far_start = refs[6:8]
        before_refs, out_ref, near_light, far_light, image = refs[8:-4], *refs[-4:]
    else:
        near_light, far_light, out_ref, image = refs[6:]
    rows, colors, _ = image.shape
    layers, far_layers = near_lit.shape[1], far_lit.shape[1]
    me = lax.axis_index("gz")
    lower = me < blocks
    half = (me + turn) % 2
    position = lax.axis_index("gx")
    group = group_ids((colors, LANES), width)
    ahead = layers // groups

    def begin(chunk, start_ref, offset, light):
        packed = jnp.zeros((colors, LANES), jnp.float32)
        for hop, ref in enumerate(before_refs, 1):
            packed = packed + jnp.where(position >= hop, ref[offset + chunk], 0.0)
        moved = [packed] + [pltpu.roll(packed, k * width, 1) for k in range(1, groups)]
        for k in range(groups):
            value = moved[-k % groups]
            for place in range(1, groups):
                value = jnp.where(group == place, moved[(place - k) % groups], value)
            z = chunk * groups + k
            light[z] = jnp.exp2(start_ref[z] + value)

    def begin_near(chunk, carry):
        begin(chunk, near_start, 0, near_light)
        return carry

    def begin_far(chunk, carry):
        begin(chunk, far_start, ahead, far_light)
        return carry

    if turn:
        lax.fori_loop(0, ahead, begin_near, 0, unroll=4)
        lax.fori_loop(0, far_start.shape[0] // groups, begin_far, 0, unroll=4)
    ambient = columns_ref[1]
    backdrop = columns_ref[2]
    at_once = 4 if rows % 4 == 0 else 2

    def light_rows(chunk, carry):
        place = [chunk * at_once + k for k in range(at_once)]

        def lit_sum(lit, unlit, light, count):
            sums = [unlit[half * rows + row] * ambient for row in place]
            for z in range(count):
                factor = light[z]
                for k, row in enumerate(place):
                    sums[k] = sums[k] + lit[half * rows + row, z] * factor
            return sums

        near = lit_sum(near_lit, near_unlit, near_light, layers)
        far = lit_sum(far_lit, far_unlit, far_light, far_layers)
        for k, row in enumerate(place):
            through = far_through[half * rows + row]
            passed = near_through[half * rows + row]
            front = jnp.where(lower, near[k], far[k])
            back = jnp.where(lower, far[k], near[k])
            image[row] = (front + jnp.where(lower, passed, through) * back
                          + through * passed * backdrop)
        return carry

    lax.fori_loop(0, rows // at_once, light_rows, 0, unroll=2)
    if len(out_ref.shape) == 3:
        out_ref[...] = image[...]
        return
    for chunk in range(rows // groups):
        tiles = swap_groups([image[chunk * groups + k] for k in range(groups)], groups, width)
        for part in range(groups):
            image[chunk * groups + part] = tiles[part]
    for slot in range(groups):
        part = slot ^ (me // 2)
        for chunk in range(rows // groups):
            out_ref[slot, chunk] = image[chunk * groups + part]


def join(columns, near, far, light, groups, width, turn, blocks):
    steps, layers, colors, _ = near[0].shape
    share = steps // 2
    shape = (share, colors, LANES)
    if share % groups == 0:
        shape = (groups, share // groups, colors, LANES)
    shapes = [jax.ShapeDtypeStruct(shape, jnp.float32)]
    if turn:
        shapes += [jax.ShapeDtypeStruct(start.shape, jnp.float32) for start in light[:2]]
    operands = [columns, *near, *far, *light]
    return pl.pallas_call(
        functools.partial(join_kernel, groups, width, turn, blocks),
        out_shape=shapes,
        in_specs=[pl.BlockSpec(memory_space=pltpu.VMEM)] * len(operands),
        out_specs=[pl.BlockSpec(memory_space=pltpu.VMEM)] * len(shapes),
        scratch_shapes=[pltpu.VMEM((share, colors, LANES), jnp.float32)],
        compiler_params=pltpu.CompilerParams(vmem_limit_bytes=24 * MIB),
        cost_estimate=pl.CostEstimate(flops=0, bytes_accessed=0, transcendentals=0),
        name="join",
    )(*operands)


def unpack_kernel(groups, width, *refs):
    arrived, out_ref, pieces = refs[:-2], refs[-2], refs[-1]
    count = 2 * len(arrived)
    me = lax.axis_index("gz")
    for apart in range(count):
        pieces[me ^ apart] = arrived[apart // 2][apart % 2]
    for tile in range(count // groups):
        for chunk in range(arrived[0].shape[1]):
            tiles = swap_groups(
                [pieces[tile * groups + part, chunk] for part in range(groups)], groups, width)
            for part in range(groups):
                out_ref[chunk * groups + part, :, tile * LANES:(tile + 1) * LANES] = tiles[part]


def unpack(arrived, groups, width):
    count = 2 * len(arrived)
    _, chunks, colors, _ = arrived[0].shape
    return pl.pallas_call(
        functools.partial(unpack_kernel, groups, width),
        out_shape=jax.ShapeDtypeStruct((chunks * groups, colors, count * width), jnp.float32),
        in_specs=[pl.BlockSpec(memory_space=pltpu.VMEM)] * len(arrived),
        out_specs=pl.BlockSpec(memory_space=pltpu.VMEM),
        scratch_shapes=[pltpu.VMEM((count, chunks, colors, LANES), jnp.float32)],
        compiler_params=pltpu.CompilerParams(vmem_limit_bytes=8 * MIB),
        name="unpack",
    )(*arrived)


def table_kernel(step_x, step_z, bins_ref, extinction_ref, color_ref, columns_ref, sum_ref,
                 split_ref):
    rows, bins = extinction_ref.shape[1], bins_ref.shape[1]
    colors = extinction_ref.shape[0]
    row = lax.broadcasted_iota(jnp.int32, (rows, bins), 0)
    bin_id = lax.broadcasted_iota(jnp.int32, (rows, bins), 1)
    here = (row == bins_ref[0:1, :]).astype(jnp.float32)
    below = ((row == bins_ref[1:2, :]) & (bin_id > 0)).astype(jnp.float32)

    def rise(ref):
        now = jnp.dot(ref[...], here, precision=lax.Precision.HIGHEST,
                      preferred_element_type=jnp.float32)
        then = jnp.dot(ref[...], below, precision=lax.Precision.HIGHEST,
                       preferred_element_type=jnp.float32)
        return now - then

    def split(value):
        coarse = value.astype(jnp.bfloat16)
        fine = (value - coarse.astype(jnp.float32)).astype(jnp.bfloat16)
        return jnp.concatenate([coarse, fine, coarse], axis=1)

    sigma = rise(extinction_ref) * columns_ref[0, :, 0:bins]
    sum_ref[...] = split(sigma * (-step_x * LOG2E))
    split_ref[0:colors] = split(sigma * (-step_z * LOG2E))
    split_ref[colors:2 * colors] = split(rise(color_ref))


def tables(bin_rows, tf_extinction, tf_color, columns, step_x, step_z):
    bins = bin_rows.shape[0]
    colors = tf_color.shape[1]
    shifted = jnp.stack([bin_rows, jnp.roll(bin_rows, 1)])
    return pl.pallas_call(
        functools.partial(table_kernel, step_x, step_z),
        out_shape=(
            jax.ShapeDtypeStruct((colors, 3 * bins), jnp.bfloat16),
            jax.ShapeDtypeStruct((2 * colors, 3 * bins), jnp.bfloat16),
        ),
        in_specs=[pl.BlockSpec(memory_space=pltpu.VMEM)] * 4,
        out_specs=[pl.BlockSpec(memory_space=pltpu.VMEM)] * 2,
        compiler_params=pltpu.CompilerParams(vmem_limit_bytes=4 * MIB),
        name="tables",
    )(shifted, tf_extinction.T, tf_color.T, columns)


def exchange(value, axis, apart):
    pairs = [(source, source ^ apart) for source in range(lax.axis_size(axis))]
    return lax.ppermute(value, axis, pairs)


def local(density, bin_rows, tf_extinction, tf_color, extinction_scale, ambient, backdrop):
    rows_x, depth, width_y = density.shape
    colors = tf_color.shape[1]
    bins = bin_rows.shape[0]
    count = lax.axis_size("gz")
    size_x = lax.axis_size("gx")
    me = lax.axis_index("gz")
    width = width_y // count
    groups = LANES // width
    steps = rows_x // groups
    step_x = 1.0 / (rows_x * size_x)
    step_z = 1.0 / (depth * count)

    up = [(i, (i + 1) % size_x) for i in range(size_x)]
    down = [(j, i) for i, j in up]
    before = lax.ppermute(density[rows_x - 1:], "gx", up)
    after = lax.ppermute(density[:1], "gx", down)

    packed = pack(density, groups, width)
    pieces = list(address(packed, before, after, groups, width))
    for apart in range(1, count):
        give = pieces[apart]
        if apart > count // 2:
            ahead = min(apart - count // 2 + 1, count // 2 - 1)
            give, _ = lax.optimization_barrier((give, pieces[ahead]))
        pieces[apart] = exchange(give, "gz", apart)
    bin_rows, extinction_scale, ambient, backdrop, _ = lax.optimization_barrier(
        (bin_rows, extinction_scale, ambient, backdrop, pieces[2]))
    columns = jnp.broadcast_to(
        jnp.stack([extinction_scale, ambient, backdrop])[:, :, None], (3, colors, LANES))
    sum_table, table = tables(bin_rows, tf_extinction, tf_color, columns, step_x, step_z)

    blocks = count // 2
    ratio = step_x / step_z
    *near, near_start, near_total = render_near(
        pieces[:blocks], table, colors, groups, width, bins, ratio, count)
    s, start, total = far_depths(pieces, near_total, sum_table, groups, width, bins)
    sums = [lax.ppermute(total, "gx", [(i, (i + hop) % size_x) for i in range(size_x)])
            for hop in range(1, size_x)]

    layers = depth * blocks
    far = render_far(s, table, colors, bins, ratio, layers + 1)
    other, *light = join(
        columns, near, far, [near_start, start, *sums], groups, width, 1, blocks)

    share = steps // 2
    if share % groups == 0:
        joined = exchange(other, "gz", 1)
        own, = join(columns, near, far, light, groups, width, 0, blocks)
        both = jnp.stack([own, joined], axis=1)
        arrived = []
        for slot in range(count // 2):
            arrived.append(exchange(both[slot], "gz", 2 * slot) if slot else both[0])
        return unpack(arrived, groups, width)
    halves = [*join(columns, near, far, light, groups, width, 0, blocks), other]
    even = me % 2 == 0
    image = jnp.stack([jnp.where(even, halves[0], halves[1]),
                       jnp.where(even, halves[1], halves[0])])
    image = image.reshape(2, share, colors, groups, width).transpose(3, 0, 1, 2, 4)
    image = lax.all_to_all(image.reshape(count, share, colors, width), "gz", 0, 0)
    return image.transpose(1, 2, 0, 3).reshape(share, colors, width_y)


def solution(mesh):
    in_specs = (P("gx", "gz", None), P(), P(), P(), P(), P(), P())
    out_specs = P(("gx", "gz"), None, None)
    return jax.shard_map(local, mesh=mesh, in_specs=in_specs, out_specs=out_specs, check_vma=False)
```

```python
import functools

import jax
import jax.numpy as jnp
from jax import lax
from jax.experimental import pallas as pl
from jax.experimental.pallas import tpu as pltpu
from jax.sharding import PartitionSpec as P

LANES = 128
LOG2E = 1.4426950408889634
MIB = 1 << 20


def group_ids(shape, width):
    return lax.broadcasted_iota(jnp.int32, shape, len(shape) - 1) // width


def swap_groups(tiles, groups, width):
    tiles = list(tiles)
    lane = group_ids(tiles[0].shape, width)
    bit = 1
    while bit < groups:
        upper = (lane & bit) != 0
        shift = bit * width
        for first in range(groups):
            if first & bit:
                continue
            a, b = tiles[first], tiles[first | bit]
            axis = a.ndim - 1
            if 2 * shift == LANES:
                moved = pltpu.roll(jnp.where(upper, a, b), shift, axis)
                tiles[first] = jnp.where(upper, moved, a)
                tiles[first | bit] = jnp.where(upper, b, moved)
            else:
                tiles[first] = jnp.where(upper, pltpu.roll(b, shift, axis), a)
                tiles[first | bit] = jnp.where(upper, b, pltpu.roll(a, LANES - shift, axis))
        bit *= 2
    return tiles


def blur_rows(parts, lane):
    out = []
    for tiles in parts:
        axis = tiles[0].ndim - 1
        up = [pltpu.roll(tile, 1, axis) for tile in tiles]
        down = [pltpu.roll(tile, LANES - 1, axis) for tile in tiles]
        row = []
        for t in range(len(tiles)):
            before = up[t - 1] if t > 0 else jnp.zeros_like(up[0])
            after = down[t + 1] if t + 1 < len(tiles) else jnp.zeros_like(up[0])
            low = jnp.where(lane == 0, before, up[t])
            high = jnp.where(lane == LANES - 1, after, down[t])
            row.append(low + 2.0 * tiles[t] + high)
        out.append(row)
    return out


def pack_kernel(groups, width, x_ref, out_ref, blurred):
    tile_count = x_ref.shape[3] // LANES
    steps, depth, width_y = x_ref.shape[1:]
    row = lax.broadcasted_iota(jnp.int32, (width_y, width_y), 0)
    column = lax.broadcasted_iota(jnp.int32, (width_y, width_y), 1)
    weights = jnp.maximum(2 - jnp.abs(row - column), 0).astype(jnp.float32).astype(jnp.bfloat16)
    for group in range(groups):
        x = x_ref[group].reshape(steps * depth, width_y)
        coarse = x.astype(jnp.bfloat16)
        fine = (x - coarse.astype(jnp.float32)).astype(jnp.bfloat16)
        blurred[group] = (jnp.dot(coarse, weights, preferred_element_type=jnp.float32)
                          + jnp.dot(fine, weights, preferred_element_type=jnp.float32)
                          ).reshape(steps, depth, width_y)
    size = 4
    for first in range(0, steps, size):
        place = pl.ds(first, size)
        for t in range(tile_count):
            swapped = swap_groups(
                [blurred[group, place, :, t * LANES:(t + 1) * LANES] for group in range(groups)],
                groups, width)
            for group in range(groups):
                out_ref[t * groups + group, place] = swapped[group]


def pack(x, groups, width):
    steps = x.shape[0] // groups
    blocks = x.shape[2] // width
    depth, width_y = x.shape[1:]
    return pl.pallas_call(
        functools.partial(pack_kernel, groups, width),
        out_shape=jax.ShapeDtypeStruct((blocks, steps, depth, LANES), jnp.float32),
        in_specs=[pl.BlockSpec(memory_space=pltpu.VMEM)],
        out_specs=pl.BlockSpec(memory_space=pltpu.VMEM),
        scratch_shapes=[pltpu.VMEM((groups, steps, depth, width_y), jnp.float32)],
        compiler_params=pltpu.CompilerParams(vmem_limit_bytes=8 * MIB),
        name="pack",
    )(x.reshape(groups, steps, depth, width_y))


def address_kernel(groups, width, packed_ref, before_ref, after_ref, *refs):
    out_refs, halo = refs[:-1], refs[-1]
    count, steps, depth, _ = packed_ref.shape
    me = lax.axis_index("gz")
    tile_count = before_ref.shape[2] // LANES
    lane = lax.broadcasted_iota(jnp.int32, (depth, LANES), 1)
    position = lax.axis_index("gx")
    inside = (position > 0, position < lax.axis_size("gx") - 1)
    ends = blur_rows(
        [[jnp.where(there, ref[0, :, t * LANES:(t + 1) * LANES], 0.0) for t in range(tile_count)]
         for ref, there in zip((before_ref, after_ref), inside)], lane)
    for t in range(tile_count):
        tiles = [ends[0][t]] * (groups - 1) + [ends[1][t]]
        swapped = swap_groups(tiles, groups, width)
        for part in range(groups):
            halo[t * groups + part] = swapped[part]
    for apart, out_ref in enumerate(out_refs):
        out_ref[0:steps] = packed_ref[me ^ apart]
        out_ref[steps] = halo[me ^ apart]


def address(packed, before, after, groups, width):
    count, steps, depth, _ = packed.shape
    shape = jax.ShapeDtypeStruct((steps + 1, depth, LANES), jnp.float32)
    return pl.pallas_call(
        functools.partial(address_kernel, groups, width),
        out_shape=[shape] * count,
        in_specs=[pl.BlockSpec(memory_space=pltpu.VMEM)] * 3,
        out_specs=[pl.BlockSpec(memory_space=pltpu.VMEM)] * count,
        scratch_shapes=[pltpu.VMEM((count, depth, LANES), jnp.float32)],
        compiler_params=pltpu.CompilerParams(vmem_limit_bytes=8 * MIB),
        name="address",
    )(packed, before, after)


def split_sum(table, wide):
    coarse = wide.astype(jnp.bfloat16)
    fine = (wide - coarse.astype(jnp.float32)).astype(jnp.bfloat16)
    weights = jnp.concatenate([coarse, coarse, fine], axis=0)
    return jnp.dot(table, weights, preferred_element_type=jnp.float32)


def smooth_layers(groups, width, scale, far, count, pieces, s_ref, raw):
    steps, depth = pieces[0].shape[-3] - 1, pieces[0].shape[-2]
    blocks = count // 2
    layers = depth * blocks
    slots = s_ref.shape[1]
    me = lax.axis_index("gz")
    lower = me < blocks
    lane = group_ids((depth, LANES), width)

    def place_piece(piece, row):
        place = pl.ds(row, depth)
        raw[1:steps + 1, place, :] = piece[0:steps]
        halo = piece[steps]
        low = pltpu.roll(piece[steps - 1], width, 1)
        high = pltpu.roll(piece[0], LANES - width, 1)
        raw[0, place, :] = jnp.where(lane == 0, halo, low)
        raw[steps + 1, place, :] = jnp.where(lane == groups - 1, halo, high)

    zeros = jnp.zeros((steps + 2, depth, LANES), jnp.float32)
    raw[:, 0:depth, :] = zeros
    raw[:, depth + layers:2 * depth + layers, :] = zeros
    for apart in range(len(pieces)):
        block = (me ^ apart) % blocks
        if far and apart < blocks:
            @pl.when(block == jnp.where(lower, blocks - 1, 0))
            def _():
                row = jnp.where(lower, 0, depth + layers)
                place_piece(pieces[apart], pl.multiple_of(row, 8))
        else:
            place_piece(pieces[apart], pl.multiple_of(depth + block * depth, 8))
    slot = lax.broadcasted_iota(jnp.int32, (layers + depth, LANES), 0)
    if far:
        empty = slot > layers
        if slots > layers + depth:
            s_ref[:, layers + depth:slots, :] = jnp.full(
                (steps, slots - layers - depth, LANES), -1.0, jnp.float32)
    else:
        empty = (slot == jnp.where(lower, layers - 1, 0))[:layers]

    def smooth(step, carry):
        v = raw[step] + 2.0 * raw[step + 1] + raw[step + 2]
        size = v.shape[0]
        before = pltpu.roll(v, 1, 0)
        after = pltpu.roll(v, size - 1, 0)
        total = (before + 2.0 * v + after) * (scale / 64.0)
        if far:
            shifted = pltpu.roll(total, size - (depth - 1), 0)[:layers + depth]
            value = jnp.where(lower, shifted, total[depth:2 * depth + layers])
            s_ref[step, 0:layers + depth] = jnp.where(empty, -1.0, value)
        else:
            s_ref[step] = jnp.where(empty, -1.0, total[depth:depth + layers])
        return carry

    lax.fori_loop(0, steps, smooth, 0, unroll=4)


def scan_quarters(groups, width, sums_ref, start_ref, total_ref, offset):
    slots, colors = sums_ref.shape[0], sums_ref.shape[1]
    group = group_ids((colors, LANES), width)

    def scan_groups(chunk, carry):
        packed = jnp.zeros((colors, LANES), jnp.float32)
        for k in range(groups):
            z = chunk * groups + k
            both = sums_ref[z]
            moved = [pltpu.roll(both, k * width, 1) for k in range(1, groups)]
            begin = jnp.zeros((colors, LANES), jnp.float32)
            everything = both
            for place, value in enumerate(moved, 1):
                begin = begin + jnp.where(group >= place, value, 0.0)
                everything = everything + value
            start_ref[z] = begin
            packed = jnp.where(group == k, everything, packed)
        total_ref[offset + chunk] = packed
        return carry

    lax.fori_loop(0, slots // groups, scan_groups, 0, unroll=4)


def bin_edges(bins):
    return lax.broadcasted_iota(jnp.int32, (bins, LANES), 0).astype(jnp.float32) - 1.0


def properties(s, size, table, bins):
    edge = bin_edges(bins).astype(jnp.bfloat16)
    zero = jnp.zeros((bins, LANES), jnp.bfloat16)
    one = jnp.ones((bins, LANES), jnp.bfloat16)
    lower_bin = jnp.floor(s)
    frac = s - lower_bin
    coarse = frac.astype(jnp.bfloat16).astype(jnp.float32)
    fine = frac - coarse

    def wide(value, r):
        return jnp.broadcast_to(value[r:r + 1], (bins, LANES)).astype(jnp.bfloat16)

    columns = []
    for r in range(size):
        away = wide(lower_bin, r) - edge
        main = jnp.minimum(jnp.maximum(away + wide(coarse, r), zero), one)
        rest = jnp.where(away == zero, wide(fine, r), zero)
        columns.append(jnp.concatenate([main, main, rest], axis=0))
    return jnp.dot(table, jnp.concatenate(columns, axis=1), preferred_element_type=jnp.float32)


def render_rows(bins, ratio, s_ref, table_ref, lit_ref, unlit_ref, through_ref, depth):
    steps, layers, colors, _ = lit_ref.shape
    depth[...] = jnp.zeros(depth.shape, jnp.float32)
    table = table_ref[...]
    block = 8

    def advance(step, carry):
        through = jnp.ones((colors, LANES), jnp.float32)
        unlit = jnp.zeros((colors, LANES), jnp.float32)
        for place in range(0, layers, block):
            size = min(block, layers - place)
            props = properties(s_ref[step, place:place + block, :], size, table, bins)
            for r in range(size):
                part = props[:, r * LANES:(r + 1) * LANES]
                sigma, color = part[:colors], part[colors:]
                later = through * jnp.exp2(sigma)
                seen = (through - later) * color
                above = depth[place + r]
                unlit = unlit + seen
                lit_ref[step, place + r] = seen * jnp.exp2(above)
                depth[place + r] = above + sigma * ratio
                through = later
        unlit_ref[step], through_ref[step] = unlit, through
        return carry

    lax.fori_loop(0, steps, advance, 0, unroll=4)


def near_kernel(groups, width, bins, ratio, count, *refs):
    pieces = refs[:count // 2]
    (table_ref, lit_ref, unlit_ref, through_ref, start_ref, total_ref, raw, s_ref,
     depth) = refs[count // 2:]
    smooth_layers(groups, width, float(bins - 1), False, count, pieces, s_ref, raw)
    render_rows(bins, ratio, s_ref, table_ref, lit_ref, unlit_ref, through_ref, depth)
    scan_quarters(groups, width, depth, start_ref, total_ref, 0)


def render_near(pieces, table, colors, groups, width, bins, ratio, count):
    steps, depth = pieces[0].shape[0] - 1, pieces[0].shape[1]
    layers = depth * len(pieces)
    plane = jax.ShapeDtypeStruct((steps, colors, LANES), jnp.float32)
    return pl.pallas_call(
        functools.partial(near_kernel, groups, width, bins, ratio, count),
        out_shape=(
            jax.ShapeDtypeStruct((steps, layers, colors, LANES), jnp.float32),
            plane,
            plane,
            jax.ShapeDtypeStruct((layers, colors, LANES), jnp.float32),
            jax.ShapeDtypeStruct((layers // groups, colors, LANES), jnp.float32),
        ),
        in_specs=[pl.BlockSpec(memory_space=pltpu.VMEM)] * (len(pieces) + 1),
        out_specs=[pl.BlockSpec(memory_space=pltpu.VMEM)] * 5,
        scratch_shapes=[
            pltpu.VMEM((steps + 2, layers + 2 * depth, LANES), jnp.float32),
            pltpu.VMEM((steps, layers, LANES), jnp.float32),
            pltpu.VMEM((layers, colors, LANES), jnp.float32),
        ],
        compiler_params=pltpu.CompilerParams(vmem_limit_bytes=20 * MIB),
        cost_estimate=pl.CostEstimate(flops=0, bytes_accessed=0, transcendentals=0),
        name="render_near",
    )(*pieces, table)


def depth_kernel(groups, width, bins, count, *refs):
    pieces = refs[:count]
    near_ref, table_ref, s_ref, start_ref, total_ref, raw, sums, products_ref = refs[count:]
    steps, depth = pieces[0].shape[-3] - 1, pieces[0].shape[-2]
    layers = depth * (count // 2)
    slots = s_ref.shape[1]
    smooth_layers(groups, width, float(bins - 1), True, count, pieces, s_ref, raw)
    edge = bin_edges(bins) + 1.0
    first_bin = lax.broadcasted_iota(jnp.int32, (bins, LANES), 0) == 0

    def count_layer(z, carry):
        acc = [jnp.zeros((bins, LANES), jnp.float32)] * 2
        for step in range(steps):
            row = jnp.broadcast_to(s_ref[step, pl.ds(z, 1), :], (bins, LANES))
            acc[step % 2] = acc[step % 2] + jnp.minimum(row, edge)
        high = acc[0] + acc[1]
        low = jnp.where(first_bin, -1.0 * steps, pltpu.roll(high, 1, 0))
        sums[z] = high - low
        return carry

    lax.fori_loop(0, layers, count_layer, 0, unroll=4)
    count_layer(layers, 0)
    for z in range(layers + 1, slots):
        sums[z] = jnp.zeros((bins, LANES), jnp.float32)
    table = table_ref[...]
    at_once = 8

    def products(chunk, carry):
        wide = [sums[chunk * at_once + k] for k in range(at_once)]
        out = split_sum(table, jnp.concatenate(wide, axis=1))
        for k in range(at_once):
            products_ref[chunk * at_once + k] = out[:, k * LANES:(k + 1) * LANES]
        return carry

    lax.fori_loop(0, slots // at_once, products, 0, unroll=True)
    ahead = near_ref.shape[0]
    total_ref[0:ahead] = near_ref[...]
    scan_quarters(groups, width, products_ref, start_ref, total_ref, ahead)


def far_depths(pieces, near_total, table, groups, width, bins):
    count = len(pieces)
    steps, depth = pieces[0].shape[0] - 1, pieces[0].shape[1]
    layers = depth * (count // 2)
    slots = layers + max(groups, depth)
    colors = table.shape[0]
    limit = 8 * MIB + slots * (LANES * 4) * (bins + 2 * colors)
    return pl.pallas_call(
        functools.partial(depth_kernel, groups, width, bins, count),
        out_shape=(
            jax.ShapeDtypeStruct((steps, slots, LANES), jnp.float32),
            jax.ShapeDtypeStruct((slots, colors, LANES), jnp.float32),
            jax.ShapeDtypeStruct((near_total.shape[0] + slots // groups, colors, LANES),
                                 jnp.float32),
        ),
        in_specs=[pl.BlockSpec(memory_space=pltpu.VMEM)] * (count + 2),
        out_specs=[pl.BlockSpec(memory_space=pltpu.VMEM)] * 3,
        scratch_shapes=[
            pltpu.VMEM((steps + 2, layers + 2 * depth, LANES), jnp.float32),
            pltpu.VMEM((slots, bins, LANES), jnp.float32),
            pltpu.VMEM((slots, colors, LANES), jnp.float32),
        ],
        compiler_params=pltpu.CompilerParams(vmem_limit_bytes=limit),
        cost_estimate=pl.CostEstimate(flops=0, bytes_accessed=0, transcendentals=0),
        name="far_depths",
    )(*pieces, near_total, table)


def render_far(s, table, colors, bins, ratio, layers):
    steps = s.shape[0]
    plane = jax.ShapeDtypeStruct((steps, colors, LANES), jnp.float32)
    return pl.pallas_call(
        functools.partial(render_rows, bins, ratio),
        out_shape=(jax.ShapeDtypeStruct((steps, layers, colors, LANES), jnp.float32), plane, plane),
        in_specs=[pl.BlockSpec(memory_space=pltpu.VMEM)] * 2,
        out_specs=[pl.BlockSpec(memory_space=pltpu.VMEM)] * 3,
        scratch_shapes=[pltpu.VMEM((layers, colors, LANES), jnp.float32)],
        compiler_params=pltpu.CompilerParams(vmem_limit_bytes=20 * MIB),
        cost_estimate=pl.CostEstimate(
            flops=10 ** 10, bytes_accessed=10 ** 7, transcendentals=10 ** 7),
        name="render_far",
    )(s, table)


def join_kernel(groups, width, turn, blocks, columns_ref, *refs):
    near_lit, near_unlit, near_through, far_lit, far_unlit, far_through = refs[:6]
    if turn:
        near_start, far_start = refs[6:8]
        before_refs, out_ref, near_light, far_light, image = refs[8:-4], *refs[-4:]
    else:
        near_light, far_light, out_ref, image = refs[6:]
    rows, colors, _ = image.shape
    layers, far_layers = near_lit.shape[1], far_lit.shape[1]
    me = lax.axis_index("gz")
    lower = me < blocks
    half = (me + turn) % 2
    position = lax.axis_index("gx")
    group = group_ids((colors, LANES), width)
    ahead = layers // groups

    def begin(chunk, start_ref, offset, light):
        packed = jnp.zeros((colors, LANES), jnp.float32)
        for hop, ref in enumerate(before_refs, 1):
            packed = packed + jnp.where(position >= hop, ref[offset + chunk], 0.0)
        moved = [packed] + [pltpu.roll(packed, k * width, 1) for k in range(1, groups)]
        for k in range(groups):
            value = moved[-k % groups]
            for place in range(1, groups):
                value = jnp.where(group == place, moved[(place - k) % groups], value)
            z = chunk * groups + k
            light[z] = jnp.exp2(start_ref[z] + value)

    def begin_near(chunk, carry):
        begin(chunk, near_start, 0, near_light)
        return carry

    def begin_far(chunk, carry):
        begin(chunk, far_start, ahead, far_light)
        return carry

    if turn:
        lax.fori_loop(0, ahead, begin_near, 0, unroll=4)
        lax.fori_loop(0, far_start.shape[0] // groups, begin_far, 0, unroll=4)
    ambient = columns_ref[1]
    backdrop = columns_ref[2]
    at_once = 4 if rows % 4 == 0 else 2

    def light_rows(chunk, carry):
        place = [chunk * at_once + k for k in range(at_once)]

        def lit_sum(lit, unlit, light, count):
            sums = [unlit[half * rows + row] * ambient for row in place]
            for z in range(count):
                factor = light[z]
                for k, row in enumerate(place):
                    sums[k] = sums[k] + lit[half * rows + row, z] * factor
            return sums

        near = lit_sum(near_lit, near_unlit, near_light, layers)
        far = lit_sum(far_lit, far_unlit, far_light, far_layers)
        for k, row in enumerate(place):
            through = far_through[half * rows + row]
            passed = near_through[half * rows + row]
            front = jnp.where(lower, near[k], far[k])
            back = jnp.where(lower, far[k], near[k])
            image[row] = (front + jnp.where(lower, passed, through) * back
                          + through * passed * backdrop)
        return carry

    lax.fori_loop(0, rows // at_once, light_rows, 0, unroll=2)
    if len(out_ref.shape) == 3:
        out_ref[...] = image[...]
        return
    for chunk in range(rows // groups):
        tiles = swap_groups([image[chunk * groups + k] for k in range(groups)], groups, width)
        for part in range(groups):
            image[chunk * groups + part] = tiles[part]
    for slot in range(groups):
        part = slot ^ (me // 2)
        for chunk in range(rows // groups):
            out_ref[slot, chunk] = image[chunk * groups + part]


def join(columns, near, far, light, groups, width, turn, blocks):
    steps, layers, colors, _ = near[0].shape
    share = steps // 2
    shape = (share, colors, LANES)
    if share % groups == 0:
        shape = (groups, share // groups, colors, LANES)
    shapes = [jax.ShapeDtypeStruct(shape, jnp.float32)]
    if turn:
        shapes += [jax.ShapeDtypeStruct(start.shape, jnp.float32) for start in light[:2]]
    operands = [columns, *near, *far, *light]
    return pl.pallas_call(
        functools.partial(join_kernel, groups, width, turn, blocks),
        out_shape=shapes,
        in_specs=[pl.BlockSpec(memory_space=pltpu.VMEM)] * len(operands),
        out_specs=[pl.BlockSpec(memory_space=pltpu.VMEM)] * len(shapes),
        scratch_shapes=[pltpu.VMEM((share, colors, LANES), jnp.float32)],
        compiler_params=pltpu.CompilerParams(vmem_limit_bytes=24 * MIB),
        cost_estimate=pl.CostEstimate(flops=0, bytes_accessed=0, transcendentals=0),
        name="join",
    )(*operands)


def unpack_kernel(groups, width, *refs):
    arrived, out_ref, pieces = refs[:-2], refs[-2], refs[-1]
    count = 2 * len(arrived)
    me = lax.axis_index("gz")
    for apart in range(count):
        pieces[me ^ apart] = arrived[apart // 2][apart % 2]
    for tile in range(count // groups):
        for chunk in range(arrived[0].shape[1]):
            tiles = swap_groups(
                [pieces[tile * groups + part, chunk] for part in range(groups)], groups, width)
            for part in range(groups):
                out_ref[chunk * groups + part, :, tile * LANES:(tile + 1) * LANES] = tiles[part]


def unpack(arrived, groups, width):
    count = 2 * len(arrived)
    _, chunks, colors, _ = arrived[0].shape
    return pl.pallas_call(
        functools.partial(unpack_kernel, groups, width),
        out_shape=jax.ShapeDtypeStruct((chunks * groups, colors, count * width), jnp.float32),
        in_specs=[pl.BlockSpec(memory_space=pltpu.VMEM)] * len(arrived),
        out_specs=pl.BlockSpec(memory_space=pltpu.VMEM),
        scratch_shapes=[pltpu.VMEM((count, chunks, colors, LANES), jnp.float32)],
        compiler_params=pltpu.CompilerParams(vmem_limit_bytes=8 * MIB),
        name="unpack",
    )(*arrived)


def table_kernel(step_x, step_z, bins_ref, scale_ref, ambient_ref, backdrop_ref, extinction_ref,
                 color_ref, sum_ref, split_ref, columns_ref):
    rows, bins = extinction_ref.shape[1], bins_ref.shape[0]
    colors = extinction_ref.shape[0]
    row = lax.broadcasted_iota(jnp.int32, (rows, bins), 0)
    lane = lax.broadcasted_iota(jnp.int32, (8, bins), 1)
    this = jnp.full((8, bins), -1, jnp.int32)
    last = jnp.full((8, bins), -1, jnp.int32)
    for k in range(bins):
        this = jnp.where(lane == k, bins_ref[k], this)
        if k:
            last = jnp.where(lane == k, bins_ref[k - 1], last)
    here = (row == this[0:1, :]).astype(jnp.float32)
    below = (row == last[0:1, :]).astype(jnp.float32)
    place = lax.broadcasted_iota(jnp.int32, (colors, LANES), 0)
    columns = []
    for ref in (scale_ref, ambient_ref, backdrop_ref):
        column = jnp.zeros((colors, LANES), jnp.float32)
        for k in range(colors):
            column = jnp.where(place == k, ref[k], column)
        columns.append(column)
    for k, column in enumerate(columns):
        columns_ref[k] = column

    def rise(ref):
        now = jnp.dot(ref[...], here, precision=lax.Precision.HIGHEST,
                      preferred_element_type=jnp.float32)
        then = jnp.dot(ref[...], below, precision=lax.Precision.HIGHEST,
                       preferred_element_type=jnp.float32)
        return now - then

    def split(value):
        coarse = value.astype(jnp.bfloat16)
        fine = (value - coarse.astype(jnp.float32)).astype(jnp.bfloat16)
        return jnp.concatenate([coarse, fine, coarse], axis=1)

    sigma = rise(extinction_ref) * columns[0][:, 0:bins]
    sum_ref[...] = split(sigma * (-step_x * LOG2E))
    split_ref[0:colors] = split(sigma * (-step_z * LOG2E))
    split_ref[colors:2 * colors] = split(rise(color_ref))


def tables(bin_rows, scale, ambient, backdrop, tf_extinction, tf_color, step_x, step_z):
    bins = bin_rows.shape[0]
    colors = tf_color.shape[1]
    return pl.pallas_call(
        functools.partial(table_kernel, step_x, step_z),
        out_shape=(
            jax.ShapeDtypeStruct((colors, 3 * bins), jnp.bfloat16),
            jax.ShapeDtypeStruct((2 * colors, 3 * bins), jnp.bfloat16),
            jax.ShapeDtypeStruct((3, colors, LANES), jnp.float32),
        ),
        in_specs=[pl.BlockSpec(memory_space=pltpu.SMEM)] * 4
        + [pl.BlockSpec(memory_space=pltpu.VMEM)] * 2,
        out_specs=[pl.BlockSpec(memory_space=pltpu.VMEM)] * 3,
        compiler_params=pltpu.CompilerParams(vmem_limit_bytes=4 * MIB),
        name="tables",
    )(bin_rows, scale, ambient, backdrop, tf_extinction.T, tf_color.T)


def exchange(value, axis, apart):
    pairs = [(source, source ^ apart) for source in range(lax.axis_size(axis))]
    return lax.ppermute(value, axis, pairs)


def local(density, bin_rows, tf_extinction, tf_color, extinction_scale, ambient, backdrop):
    rows_x, depth, width_y = density.shape
    colors = tf_color.shape[1]
    bins = bin_rows.shape[0]
    count = lax.axis_size("gz")
    size_x = lax.axis_size("gx")
    me = lax.axis_index("gz")
    width = width_y // count
    groups = LANES // width
    steps = rows_x // groups
    step_x = 1.0 / (rows_x * size_x)
    step_z = 1.0 / (depth * count)

    up = [(i, (i + 1) % size_x) for i in range(size_x)]
    down = [(j, i) for i, j in up]
    before = lax.ppermute(density[rows_x - 1:], "gx", up)
    after = lax.ppermute(density[:1], "gx", down)

    packed = pack(density, groups, width)
    pieces = list(address(packed, before, after, groups, width))
    for apart in range(1, count):
        give = pieces[apart]
        if apart > count // 2:
            ahead = max(apart - count // 2 - 1, 1)
            give, _ = lax.optimization_barrier((give, pieces[ahead]))
        pieces[apart] = exchange(give, "gz", apart)
    bin_rows, extinction_scale, ambient, backdrop, _ = lax.optimization_barrier(
        (bin_rows, extinction_scale, ambient, backdrop, pieces[2]))
    sum_table, table, columns = tables(
        bin_rows, extinction_scale, ambient, backdrop, tf_extinction, tf_color, step_x, step_z)

    blocks = count // 2
    ratio = step_x / step_z
    *near, near_start, near_total = render_near(
        pieces[:blocks], table, colors, groups, width, bins, ratio, count)
    s, start, total = far_depths(pieces, near_total, sum_table, groups, width, bins)
    sums = [lax.ppermute(total, "gx", [(i, (i + hop) % size_x) for i in range(size_x)])
            for hop in range(1, size_x)]

    layers = depth * blocks
    far = render_far(s, table, colors, bins, ratio, layers + 1)
    other, *light = join(
        columns, near, far, [near_start, start, *sums], groups, width, 1, blocks)

    share = steps // 2
    if share % groups == 0:
        joined = exchange(other, "gz", 1)
        own, = join(columns, near, far, light, groups, width, 0, blocks)
        both = jnp.stack([own, joined], axis=1)
        arrived = []
        for slot in range(count // 2):
            arrived.append(exchange(both[slot], "gz", 2 * slot) if slot else both[0])
        return unpack(arrived, groups, width)
    halves = [*join(columns, near, far, light, groups, width, 0, blocks), other]
    even = me % 2 == 0
    image = jnp.stack([jnp.where(even, halves[0], halves[1]),
                       jnp.where(even, halves[1], halves[0])])
    image = image.reshape(2, share, colors, groups, width).transpose(3, 0, 1, 2, 4)
    image = lax.all_to_all(image.reshape(count, share, colors, width), "gz", 0, 0)
    return image.transpose(1, 2, 0, 3).reshape(share, colors, width_y)


def solution(mesh):
    in_specs = (P("gx", "gz", None), P(), P(), P(), P(), P(), P())
    out_specs = P(("gx", "gz"), None, None)
    return jax.shard_map(local, mesh=mesh, in_specs=in_specs, out_specs=out_specs, check_vma=False)
```

```python
import functools

import jax
import jax.numpy as jnp
from jax import lax
from jax.experimental import pallas as pl
from jax.experimental.pallas import tpu as pltpu
from jax.sharding import PartitionSpec as P

LANES = 128
LOG2E = 1.4426950408889634
MIB = 1 << 20


def group_ids(shape, width):
    return lax.broadcasted_iota(jnp.int32, shape, len(shape) - 1) // width


def swap_groups(tiles, groups, width):
    tiles = list(tiles)
    lane = group_ids(tiles[0].shape, width)
    bit = 1
    while bit < groups:
        upper = (lane & bit) != 0
        shift = bit * width
        for first in range(groups):
            if first & bit:
                continue
            a, b = tiles[first], tiles[first | bit]
            axis = a.ndim - 1
            if 2 * shift == LANES:
                moved = pltpu.roll(jnp.where(upper, a, b), shift, axis)
                tiles[first] = jnp.where(upper, moved, a)
                tiles[first | bit] = jnp.where(upper, b, moved)
            else:
                tiles[first] = jnp.where(upper, pltpu.roll(b, shift, axis), a)
                tiles[first | bit] = jnp.where(upper, b, pltpu.roll(a, LANES - shift, axis))
        bit *= 2
    return tiles


def blur_rows(parts, lane):
    out = []
    for tiles in parts:
        axis = tiles[0].ndim - 1
        up = [pltpu.roll(tile, 1, axis) for tile in tiles]
        down = [pltpu.roll(tile, LANES - 1, axis) for tile in tiles]
        row = []
        for t in range(len(tiles)):
            before = up[t - 1] if t > 0 else jnp.zeros_like(up[0])
            after = down[t + 1] if t + 1 < len(tiles) else jnp.zeros_like(up[0])
            low = jnp.where(lane == 0, before, up[t])
            high = jnp.where(lane == LANES - 1, after, down[t])
            row.append(low + 2.0 * tiles[t] + high)
        out.append(row)
    return out


def pack_kernel(groups, width, x_ref, out_ref, blurred):
    tile_count = x_ref.shape[3] // LANES
    steps, depth, width_y = x_ref.shape[1:]
    row = lax.broadcasted_iota(jnp.int32, (width_y, width_y), 0)
    column = lax.broadcasted_iota(jnp.int32, (width_y, width_y), 1)
    weights = jnp.maximum(2 - jnp.abs(row - column), 0).astype(jnp.float32).astype(jnp.bfloat16)
    for group in range(groups):
        x = x_ref[group].reshape(steps * depth, width_y)
        coarse = x.astype(jnp.bfloat16)
        fine = (x - coarse.astype(jnp.float32)).astype(jnp.bfloat16)
        blurred[group] = (jnp.dot(coarse, weights, preferred_element_type=jnp.float32)
                          + jnp.dot(fine, weights, preferred_element_type=jnp.float32)
                          ).reshape(steps, depth, width_y)
    size = 4
    for first in range(0, steps, size):
        place = pl.ds(first, size)
        for t in range(tile_count):
            swapped = swap_groups(
                [blurred[group, place, :, t * LANES:(t + 1) * LANES] for group in range(groups)],
                groups, width)
            for group in range(groups):
                out_ref[t * groups + group, place] = swapped[group]


def pack(x, groups, width):
    steps = x.shape[0] // groups
    blocks = x.shape[2] // width
    depth, width_y = x.shape[1:]
    return pl.pallas_call(
        functools.partial(pack_kernel, groups, width),
        out_shape=jax.ShapeDtypeStruct((blocks, steps, depth, LANES), jnp.float32),
        in_specs=[pl.BlockSpec(memory_space=pltpu.VMEM)],
        out_specs=pl.BlockSpec(memory_space=pltpu.VMEM),
        scratch_shapes=[pltpu.VMEM((groups, steps, depth, width_y), jnp.float32)],
        compiler_params=pltpu.CompilerParams(vmem_limit_bytes=8 * MIB),
        name="pack",
    )(x.reshape(groups, steps, depth, width_y))


def address_kernel(groups, width, packed_ref, before_ref, after_ref, *refs):
    out_refs, halo = refs[:-1], refs[-1]
    count, steps, depth, _ = packed_ref.shape
    me = lax.axis_index("gz")
    tile_count = before_ref.shape[2] // LANES
    lane = lax.broadcasted_iota(jnp.int32, (depth, LANES), 1)
    position = lax.axis_index("gx")
    inside = (position > 0, position < lax.axis_size("gx") - 1)
    ends = blur_rows(
        [[jnp.where(there, ref[0, :, t * LANES:(t + 1) * LANES], 0.0) for t in range(tile_count)]
         for ref, there in zip((before_ref, after_ref), inside)], lane)
    for t in range(tile_count):
        tiles = [ends[0][t]] * (groups - 1) + [ends[1][t]]
        swapped = swap_groups(tiles, groups, width)
        for part in range(groups):
            halo[t * groups + part] = swapped[part]
    for apart, out_ref in enumerate(out_refs):
        out_ref[0:steps] = packed_ref[me ^ apart]
        out_ref[steps] = halo[me ^ apart]


def address(packed, before, after, groups, width):
    count, steps, depth, _ = packed.shape
    shape = jax.ShapeDtypeStruct((steps + 1, depth, LANES), jnp.float32)
    return pl.pallas_call(
        functools.partial(address_kernel, groups, width),
        out_shape=[shape] * count,
        in_specs=[pl.BlockSpec(memory_space=pltpu.VMEM)] * 3,
        out_specs=[pl.BlockSpec(memory_space=pltpu.VMEM)] * count,
        scratch_shapes=[pltpu.VMEM((count, depth, LANES), jnp.float32)],
        compiler_params=pltpu.CompilerParams(vmem_limit_bytes=8 * MIB),
        name="address",
    )(packed, before, after)


def split_sum(table, wide):
    coarse = wide.astype(jnp.bfloat16)
    fine = (wide - coarse.astype(jnp.float32)).astype(jnp.bfloat16)
    weights = jnp.concatenate([coarse, coarse, fine], axis=0)
    return jnp.dot(table, weights, preferred_element_type=jnp.float32)


def smooth_layers(groups, width, scale, far, count, pieces, s_ref, raw):
    steps, depth = pieces[0].shape[-3] - 1, pieces[0].shape[-2]
    blocks = count // 2
    layers = depth * blocks
    slots = s_ref.shape[1]
    me = lax.axis_index("gz")
    lower = me < blocks
    lane = group_ids((depth, LANES), width)

    def place_piece(piece, row):
        place = pl.ds(row, depth)
        raw[1:steps + 1, place, :] = piece[0:steps]
        halo = piece[steps]
        low = pltpu.roll(piece[steps - 1], width, 1)
        high = pltpu.roll(piece[0], LANES - width, 1)
        raw[0, place, :] = jnp.where(lane == 0, halo, low)
        raw[steps + 1, place, :] = jnp.where(lane == groups - 1, halo, high)

    zeros = jnp.zeros((steps + 2, depth, LANES), jnp.float32)
    raw[:, 0:depth, :] = zeros
    raw[:, depth + layers:2 * depth + layers, :] = zeros
    for apart in range(len(pieces)):
        block = (me ^ apart) % blocks
        if far and apart < blocks:
            @pl.when(block == jnp.where(lower, blocks - 1, 0))
            def _():
                row = jnp.where(lower, 0, depth + layers)
                place_piece(pieces[apart], pl.multiple_of(row, 8))
        else:
            place_piece(pieces[apart], pl.multiple_of(depth + block * depth, 8))
    slot = lax.broadcasted_iota(jnp.int32, (layers + depth, LANES), 0)
    if far:
        empty = slot > layers
        if slots > layers + depth:
            s_ref[:, layers + depth:slots, :] = jnp.full(
                (steps, slots - layers - depth, LANES), -1.0, jnp.float32)
    else:
        empty = (slot == jnp.where(lower, layers - 1, 0))[:layers]

    def smooth(step, carry):
        v = raw[step] + 2.0 * raw[step + 1] + raw[step + 2]
        size = v.shape[0]
        before = pltpu.roll(v, 1, 0)
        after = pltpu.roll(v, size - 1, 0)
        total = (before + 2.0 * v + after) * (scale / 64.0)
        if far:
            shifted = pltpu.roll(total, size - (depth - 1), 0)[:layers + depth]
            value = jnp.where(lower, shifted, total[depth:2 * depth + layers])
            s_ref[step, 0:layers + depth] = jnp.where(empty, -1.0, value)
        else:
            s_ref[step] = jnp.where(empty, -1.0, total[depth:depth + layers])
        return carry

    lax.fori_loop(0, steps, smooth, 0, unroll=4)


def scan_quarters(groups, width, sums_ref, start_ref, total_ref, offset):
    colors = sums_ref.shape[1]
    group = group_ids((colors, LANES), width)

    def scan_groups(chunk, carry):
        packed = jnp.zeros((colors, LANES), jnp.float32)
        for k in range(groups):
            z = chunk * groups + k
            both = sums_ref[z]
            moved = [pltpu.roll(both, k * width, 1) for k in range(1, groups)]
            begin = jnp.zeros((colors, LANES), jnp.float32)
            everything = both
            for place, value in enumerate(moved, 1):
                begin = begin + jnp.where(group >= place, value, 0.0)
                everything = everything + value
            start_ref[z] = begin
            packed = jnp.where(group == k, everything, packed)
        total_ref[offset + chunk] = packed
        return carry

    lax.fori_loop(0, total_ref.shape[0] - offset, scan_groups, 0, unroll=4)


def bin_edges(bins):
    return lax.broadcasted_iota(jnp.int32, (bins, LANES), 0).astype(jnp.float32) - 1.0


def properties(s, size, table, bins):
    edge = bin_edges(bins).astype(jnp.bfloat16)
    zero = jnp.zeros((bins, LANES), jnp.bfloat16)
    one = jnp.ones((bins, LANES), jnp.bfloat16)
    lower_bin = jnp.floor(s)
    frac = s - lower_bin
    coarse = frac.astype(jnp.bfloat16).astype(jnp.float32)
    fine = frac - coarse

    def wide(value, r):
        return jnp.broadcast_to(value[r:r + 1], (bins, LANES)).astype(jnp.bfloat16)

    columns = []
    for r in range(size):
        away = wide(lower_bin, r) - edge
        main = jnp.minimum(jnp.maximum(away + wide(coarse, r), zero), one)
        rest = jnp.where(away == zero, wide(fine, r), zero)
        columns.append(jnp.concatenate([main, main, rest], axis=0))
    return jnp.dot(table, jnp.concatenate(columns, axis=1), preferred_element_type=jnp.float32)


def render_rows(bins, ratio, s_ref, table_ref, lit_ref, unlit_ref, through_ref, depth):
    steps, layers, colors, _ = lit_ref.shape
    depth[...] = jnp.zeros(depth.shape, jnp.float32)
    table = table_ref[...]
    block = 8

    def advance(step, carry):
        through = jnp.ones((colors, LANES), jnp.float32)
        unlit = jnp.zeros((colors, LANES), jnp.float32)
        for place in range(0, layers, block):
            size = min(block, layers - place)
            props = properties(s_ref[step, place:place + block, :], size, table, bins)
            for r in range(size):
                part = props[:, r * LANES:(r + 1) * LANES]
                sigma, color = part[:colors], part[colors:]
                later = through * jnp.exp2(sigma)
                seen = (through - later) * color
                above = depth[place + r]
                unlit = unlit + seen
                lit_ref[step, place + r] = seen * jnp.exp2(above)
                depth[place + r] = above + sigma * ratio
                through = later
        unlit_ref[step], through_ref[step] = unlit, through
        return carry

    lax.fori_loop(0, steps, advance, 0, unroll=4)


def near_kernel(groups, width, bins, ratio, count, *refs):
    pieces = refs[:count // 2]
    (table_ref, lit_ref, unlit_ref, through_ref, start_ref, total_ref, raw, s_ref,
     depth) = refs[count // 2:]
    smooth_layers(groups, width, float(bins - 1), False, count, pieces, s_ref, raw)
    render_rows(bins, ratio, s_ref, table_ref, lit_ref, unlit_ref, through_ref, depth)
    scan_quarters(groups, width, depth, start_ref, total_ref, 0)


def render_near(pieces, table, colors, groups, width, bins, ratio, count):
    steps, depth = pieces[0].shape[0] - 1, pieces[0].shape[1]
    layers = depth * len(pieces)
    plane = jax.ShapeDtypeStruct((steps, colors, LANES), jnp.float32)
    return pl.pallas_call(
        functools.partial(near_kernel, groups, width, bins, ratio, count),
        out_shape=(
            jax.ShapeDtypeStruct((steps, layers, colors, LANES), jnp.float32),
            plane,
            plane,
            jax.ShapeDtypeStruct((layers, colors, LANES), jnp.float32),
            jax.ShapeDtypeStruct((layers // groups, colors, LANES), jnp.float32),
        ),
        in_specs=[pl.BlockSpec(memory_space=pltpu.VMEM)] * (len(pieces) + 1),
        out_specs=[pl.BlockSpec(memory_space=pltpu.VMEM)] * 5,
        scratch_shapes=[
            pltpu.VMEM((steps + 2, layers + 2 * depth, LANES), jnp.float32),
            pltpu.VMEM((steps, layers, LANES), jnp.float32),
            pltpu.VMEM((layers, colors, LANES), jnp.float32),
        ],
        compiler_params=pltpu.CompilerParams(vmem_limit_bytes=20 * MIB),
        cost_estimate=pl.CostEstimate(flops=0, bytes_accessed=0, transcendentals=0),
        name="render_near",
    )(*pieces, table)


def depth_kernel(groups, width, bins, count, *refs):
    pieces = refs[:count]
    near_ref, table_ref, s_ref, start_ref, total_ref, raw, sums, products_ref = refs[count:]
    steps, depth = pieces[0].shape[-3] - 1, pieces[0].shape[-2]
    layers = depth * (count // 2)
    slots = s_ref.shape[1]
    smooth_layers(groups, width, float(bins - 1), True, count, pieces, s_ref, raw)
    edge = bin_edges(bins) + 1.0
    first_bin = lax.broadcasted_iota(jnp.int32, (bins, LANES), 0) == 0

    def count_layer(z, carry):
        acc = [jnp.zeros((bins, LANES), jnp.float32)] * 2
        for step in range(steps):
            row = jnp.broadcast_to(s_ref[step, pl.ds(z, 1), :], (bins, LANES))
            acc[step % 2] = acc[step % 2] + jnp.minimum(row, edge)
        high = acc[0] + acc[1]
        low = jnp.where(first_bin, -1.0 * steps, pltpu.roll(high, 1, 0))
        sums[z] = high - low
        return carry

    lax.fori_loop(0, layers, count_layer, 0, unroll=4)
    count_layer(layers, 0)
    for z in range(layers + 1, slots):
        sums[z] = jnp.zeros((bins, LANES), jnp.float32)
    table = table_ref[...]
    at_once = 8

    def products(chunk, carry):
        wide = [sums[chunk * at_once + k] for k in range(at_once)]
        out = split_sum(table, jnp.concatenate(wide, axis=1))
        for k in range(at_once):
            products_ref[chunk * at_once + k] = out[:, k * LANES:(k + 1) * LANES]
        return carry

    lax.fori_loop(0, slots // at_once, products, 0, unroll=True)
    ahead = near_ref.shape[0]
    total_ref[0:ahead] = near_ref[...]
    scan_quarters(groups, width, products_ref, start_ref, total_ref, ahead)


def far_depths(pieces, near_total, table, groups, width, bins):
    count = len(pieces)
    steps, depth = pieces[0].shape[0] - 1, pieces[0].shape[1]
    layers = depth * (count // 2)
    slots = layers + max(groups, depth)
    colors = table.shape[0]
    limit = 8 * MIB + slots * (LANES * 4) * (bins + 2 * colors)
    return pl.pallas_call(
        functools.partial(depth_kernel, groups, width, bins, count),
        out_shape=(
            jax.ShapeDtypeStruct((steps, slots, LANES), jnp.float32),
            jax.ShapeDtypeStruct((slots, colors, LANES), jnp.float32),
            jax.ShapeDtypeStruct((near_total.shape[0] + layers // groups + 1, colors, LANES),
                                 jnp.float32),
        ),
        in_specs=[pl.BlockSpec(memory_space=pltpu.VMEM)] * (count + 2),
        out_specs=[pl.BlockSpec(memory_space=pltpu.VMEM)] * 3,
        scratch_shapes=[
            pltpu.VMEM((steps + 2, layers + 2 * depth, LANES), jnp.float32),
            pltpu.VMEM((slots, bins, LANES), jnp.float32),
            pltpu.VMEM((slots, colors, LANES), jnp.float32),
        ],
        compiler_params=pltpu.CompilerParams(vmem_limit_bytes=limit),
        cost_estimate=pl.CostEstimate(flops=0, bytes_accessed=0, transcendentals=0),
        name="far_depths",
    )(*pieces, near_total, table)


def render_far(s, table, colors, bins, ratio, layers):
    steps = s.shape[0]
    plane = jax.ShapeDtypeStruct((steps, colors, LANES), jnp.float32)
    return pl.pallas_call(
        functools.partial(render_rows, bins, ratio),
        out_shape=(jax.ShapeDtypeStruct((steps, layers, colors, LANES), jnp.float32), plane, plane),
        in_specs=[pl.BlockSpec(memory_space=pltpu.VMEM)] * 2,
        out_specs=[pl.BlockSpec(memory_space=pltpu.VMEM)] * 3,
        scratch_shapes=[pltpu.VMEM((layers, colors, LANES), jnp.float32)],
        compiler_params=pltpu.CompilerParams(vmem_limit_bytes=20 * MIB),
        cost_estimate=pl.CostEstimate(
            flops=10 ** 10, bytes_accessed=10 ** 7, transcendentals=10 ** 7),
        name="render_far",
    )(s, table)


def join_kernel(groups, width, turn, blocks, columns_ref, *refs):
    near_lit, near_unlit, near_through, far_lit, far_unlit, far_through = refs[:6]
    if turn:
        near_start, far_start = refs[6:8]
        before_refs, out_ref, near_light, far_light, image = refs[8:-4], *refs[-4:]
    else:
        near_light, far_light, out_ref, image = refs[6:]
    rows, colors, _ = image.shape
    layers, far_layers = near_lit.shape[1], far_lit.shape[1]
    me = lax.axis_index("gz")
    lower = me < blocks
    half = (me + turn) % 2
    position = lax.axis_index("gx")
    group = group_ids((colors, LANES), width)
    ahead = layers // groups

    def begin(chunk, start_ref, offset, light):
        packed = jnp.zeros((colors, LANES), jnp.float32)
        for hop, ref in enumerate(before_refs, 1):
            packed = packed + jnp.where(position >= hop, ref[offset + chunk], 0.0)
        moved = [packed] + [pltpu.roll(packed, k * width, 1) for k in range(1, groups)]
        for k in range(groups):
            value = moved[-k % groups]
            for place in range(1, groups):
                value = jnp.where(group == place, moved[(place - k) % groups], value)
            z = chunk * groups + k
            light[z] = jnp.exp2(start_ref[z] + value)

    def begin_near(chunk, carry):
        begin(chunk, near_start, 0, near_light)
        return carry

    def begin_far(chunk, carry):
        begin(chunk, far_start, ahead, far_light)
        return carry

    if turn:
        lax.fori_loop(0, ahead, begin_near, 0, unroll=4)
        lax.fori_loop(0, before_refs[0].shape[0] - ahead, begin_far, 0, unroll=4)
    ambient = columns_ref[1]
    backdrop = columns_ref[2]
    at_once = 4 if rows % 4 == 0 else 2

    def light_rows(chunk, carry):
        place = [chunk * at_once + k for k in range(at_once)]

        def lit_sum(lit, unlit, light, count):
            sums = [unlit[half * rows + row] * ambient for row in place]
            for z in range(count):
                factor = light[z]
                for k, row in enumerate(place):
                    sums[k] = sums[k] + lit[half * rows + row, z] * factor
            return sums

        near = lit_sum(near_lit, near_unlit, near_light, layers)
        far = lit_sum(far_lit, far_unlit, far_light, far_layers)
        for k, row in enumerate(place):
            through = far_through[half * rows + row]
            passed = near_through[half * rows + row]
            front = jnp.where(lower, near[k], far[k])
            back = jnp.where(lower, far[k], near[k])
            image[row] = (front + jnp.where(lower, passed, through) * back
                          + through * passed * backdrop)
        return carry

    lax.fori_loop(0, rows // at_once, light_rows, 0, unroll=2)
    if len(out_ref.shape) == 3:
        out_ref[...] = image[...]
        return
    for chunk in range(rows // groups):
        tiles = swap_groups([image[chunk * groups + k] for k in range(groups)], groups, width)
        for part in range(groups):
            image[chunk * groups + part] = tiles[part]
    for slot in range(groups):
        part = slot ^ (me // 2)
        for chunk in range(rows // groups):
            out_ref[slot, chunk] = image[chunk * groups + part]


def join(columns, near, far, light, groups, width, turn, blocks):
    steps, layers, colors, _ = near[0].shape
    share = steps // 2
    shape = (share, colors, LANES)
    if share % groups == 0:
        shape = (groups, share // groups, colors, LANES)
    shapes = [jax.ShapeDtypeStruct(shape, jnp.float32)]
    if turn:
        shapes += [jax.ShapeDtypeStruct(start.shape, jnp.float32) for start in light[:2]]
    operands = [columns, *near, *far, *light]
    return pl.pallas_call(
        functools.partial(join_kernel, groups, width, turn, blocks),
        out_shape=shapes,
        in_specs=[pl.BlockSpec(memory_space=pltpu.VMEM)] * len(operands),
        out_specs=[pl.BlockSpec(memory_space=pltpu.VMEM)] * len(shapes),
        scratch_shapes=[pltpu.VMEM((share, colors, LANES), jnp.float32)],
        compiler_params=pltpu.CompilerParams(vmem_limit_bytes=24 * MIB),
        cost_estimate=pl.CostEstimate(flops=0, bytes_accessed=0, transcendentals=0),
        name="join",
    )(*operands)


def unpack_kernel(groups, width, *refs):
    arrived, out_ref, pieces = refs[:-2], refs[-2], refs[-1]
    count = 2 * len(arrived)
    me = lax.axis_index("gz")
    for apart in range(count):
        pieces[me ^ apart] = arrived[apart // 2][apart % 2]
    for tile in range(count // groups):
        for chunk in range(arrived[0].shape[1]):
            tiles = swap_groups(
                [pieces[tile * groups + part, chunk] for part in range(groups)], groups, width)
            for part in range(groups):
                out_ref[chunk * groups + part, :, tile * LANES:(tile + 1) * LANES] = tiles[part]


def unpack(arrived, groups, width):
    count = 2 * len(arrived)
    _, chunks, colors, _ = arrived[0].shape
    return pl.pallas_call(
        functools.partial(unpack_kernel, groups, width),
        out_shape=jax.ShapeDtypeStruct((chunks * groups, colors, count * width), jnp.float32),
        in_specs=[pl.BlockSpec(memory_space=pltpu.VMEM)] * len(arrived),
        out_specs=pl.BlockSpec(memory_space=pltpu.VMEM),
        scratch_shapes=[pltpu.VMEM((count, chunks, colors, LANES), jnp.float32)],
        compiler_params=pltpu.CompilerParams(vmem_limit_bytes=8 * MIB),
        name="unpack",
    )(*arrived)


def table_kernel(step_x, step_z, bins_ref, scale_ref, ambient_ref, backdrop_ref, extinction_ref,
                 color_ref, sum_ref, split_ref, columns_ref):
    rows, bins = extinction_ref.shape[1], bins_ref.shape[0]
    colors = extinction_ref.shape[0]
    row = lax.broadcasted_iota(jnp.int32, (rows, bins), 0)
    lane = lax.broadcasted_iota(jnp.int32, (8, bins), 1)
    this = jnp.full((8, bins), -1, jnp.int32)
    last = jnp.full((8, bins), -1, jnp.int32)
    for k in range(bins):
        this = jnp.where(lane == k, bins_ref[k], this)
        if k:
            last = jnp.where(lane == k, bins_ref[k - 1], last)
    here = (row == this[0:1, :]).astype(jnp.float32)
    below = (row == last[0:1, :]).astype(jnp.float32)
    place = lax.broadcasted_iota(jnp.int32, (colors, LANES), 0)
    columns = []
    for ref in (scale_ref, ambient_ref, backdrop_ref):
        column = jnp.zeros((colors, LANES), jnp.float32)
        for k in range(colors):
            column = jnp.where(place == k, ref[k], column)
        columns.append(column)
    for k, column in enumerate(columns):
        columns_ref[k] = column

    def rise(ref):
        now = jnp.dot(ref[...], here, precision=lax.Precision.HIGHEST,
                      preferred_element_type=jnp.float32)
        then = jnp.dot(ref[...], below, precision=lax.Precision.HIGHEST,
                       preferred_element_type=jnp.float32)
        return now - then

    def split(value):
        coarse = value.astype(jnp.bfloat16)
        fine = (value - coarse.astype(jnp.float32)).astype(jnp.bfloat16)
        return jnp.concatenate([coarse, fine, coarse], axis=1)

    sigma = rise(extinction_ref) * columns[0][:, 0:bins]
    sum_ref[...] = split(sigma * (-step_x * LOG2E))
    split_ref[0:colors] = split(sigma * (-step_z * LOG2E))
    split_ref[colors:2 * colors] = split(rise(color_ref))


def tables(bin_rows, scale, ambient, backdrop, tf_extinction, tf_color, step_x, step_z):
    bins = bin_rows.shape[0]
    colors = tf_color.shape[1]
    return pl.pallas_call(
        functools.partial(table_kernel, step_x, step_z),
        out_shape=(
            jax.ShapeDtypeStruct((colors, 3 * bins), jnp.bfloat16),
            jax.ShapeDtypeStruct((2 * colors, 3 * bins), jnp.bfloat16),
            jax.ShapeDtypeStruct((3, colors, LANES), jnp.float32),
        ),
        in_specs=[pl.BlockSpec(memory_space=pltpu.SMEM)] * 4
        + [pl.BlockSpec(memory_space=pltpu.VMEM)] * 2,
        out_specs=[pl.BlockSpec(memory_space=pltpu.VMEM)] * 3,
        compiler_params=pltpu.CompilerParams(vmem_limit_bytes=4 * MIB),
        name="tables",
    )(bin_rows, scale, ambient, backdrop, tf_extinction.T, tf_color.T)


def exchange(value, axis, apart):
    pairs = [(source, source ^ apart) for source in range(lax.axis_size(axis))]
    return lax.ppermute(value, axis, pairs)


def local(density, bin_rows, tf_extinction, tf_color, extinction_scale, ambient, backdrop):
    rows_x, depth, width_y = density.shape
    colors = tf_color.shape[1]
    bins = bin_rows.shape[0]
    count = lax.axis_size("gz")
    size_x = lax.axis_size("gx")
    me = lax.axis_index("gz")
    width = width_y // count
    groups = LANES // width
    steps = rows_x // groups
    step_x = 1.0 / (rows_x * size_x)
    step_z = 1.0 / (depth * count)

    up = [(i, (i + 1) % size_x) for i in range(size_x)]
    down = [(j, i) for i, j in up]
    before = lax.ppermute(density[rows_x - 1:], "gx", up)
    after = lax.ppermute(density[:1], "gx", down)

    packed = pack(density, groups, width)
    pieces = list(address(packed, before, after, groups, width))
    for apart in range(1, count):
        give = pieces[apart]
        if apart > count // 2:
            ahead = max(apart - count // 2 - 1, 1)
            give, _ = lax.optimization_barrier((give, pieces[ahead]))
        pieces[apart] = exchange(give, "gz", apart)
    bin_rows, extinction_scale, ambient, backdrop, _ = lax.optimization_barrier(
        (bin_rows, extinction_scale, ambient, backdrop, pieces[2]))
    sum_table, table, columns = tables(
        bin_rows, extinction_scale, ambient, backdrop, tf_extinction, tf_color, step_x, step_z)

    blocks = count // 2
    ratio = step_x / step_z
    *near, near_start, near_total = render_near(
        pieces[:blocks], table, colors, groups, width, bins, ratio, count)
    s, start, total = far_depths(pieces, near_total, sum_table, groups, width, bins)
    sums = [lax.ppermute(total, "gx", [(i, (i + hop) % size_x) for i in range(size_x)])
            for hop in range(1, size_x)]

    layers = depth * blocks
    far = render_far(s, table, colors, bins, ratio, layers + 1)
    other, *light = join(
        columns, near, far, [near_start, start, *sums], groups, width, 1, blocks)

    share = steps // 2
    if share % groups == 0:
        joined = exchange(other, "gz", 1)
        own, = join(columns, near, far, light, groups, width, 0, blocks)
        both = jnp.stack([own, joined], axis=1)
        arrived = []
        for slot in range(count // 2):
            arrived.append(exchange(both[slot], "gz", 2 * slot) if slot else both[0])
        return unpack(arrived, groups, width)
    halves = [*join(columns, near, far, light, groups, width, 0, blocks), other]
    even = me % 2 == 0
    image = jnp.stack([jnp.where(even, halves[0], halves[1]),
                       jnp.where(even, halves[1], halves[0])])
    image = image.reshape(2, share, colors, groups, width).transpose(3, 0, 1, 2, 4)
    image = lax.all_to_all(image.reshape(count, share, colors, width), "gz", 0, 0)
    return image.transpose(1, 2, 0, 3).reshape(share, colors, width_y)


def solution(mesh):
    in_specs = (P("gx", "gz", None), P(), P(), P(), P(), P(), P())
    out_specs = P(("gx", "gz"), None, None)
    return jax.shard_map(local, mesh=mesh, in_specs=in_specs, out_specs=out_specs, check_vma=False)
```

```python
import functools

import jax
import jax.numpy as jnp
from jax import lax
from jax.experimental import pallas as pl
from jax.experimental.pallas import tpu as pltpu
from jax.sharding import PartitionSpec as P

LANES = 128
LOG2E = 1.4426950408889634
MIB = 1 << 20


def group_ids(shape, width):
    return lax.broadcasted_iota(jnp.int32, shape, len(shape) - 1) // width


def swap_groups(tiles, groups, width):
    tiles = list(tiles)
    lane = group_ids(tiles[0].shape, width)
    bit = 1
    while bit < groups:
        upper = (lane & bit) != 0
        shift = bit * width
        for first in range(groups):
            if first & bit:
                continue
            a, b = tiles[first], tiles[first | bit]
            axis = a.ndim - 1
            if 2 * shift == LANES:
                moved = pltpu.roll(jnp.where(upper, a, b), shift, axis)
                tiles[first] = jnp.where(upper, moved, a)
                tiles[first | bit] = jnp.where(upper, b, moved)
            else:
                tiles[first] = jnp.where(upper, pltpu.roll(b, shift, axis), a)
                tiles[first | bit] = jnp.where(upper, b, pltpu.roll(a, LANES - shift, axis))
        bit *= 2
    return tiles


def blur_rows(parts, lane):
    out = []
    for tiles in parts:
        axis = tiles[0].ndim - 1
        up = [pltpu.roll(tile, 1, axis) for tile in tiles]
        down = [pltpu.roll(tile, LANES - 1, axis) for tile in tiles]
        row = []
        for t in range(len(tiles)):
            before = up[t - 1] if t > 0 else jnp.zeros_like(up[0])
            after = down[t + 1] if t + 1 < len(tiles) else jnp.zeros_like(up[0])
            low = jnp.where(lane == 0, before, up[t])
            high = jnp.where(lane == LANES - 1, after, down[t])
            row.append(low + 2.0 * tiles[t] + high)
        out.append(row)
    return out


def pack_kernel(groups, width, x_ref, out_ref, blurred):
    tile_count = x_ref.shape[3] // LANES
    steps, depth, width_y = x_ref.shape[1:]
    row = lax.broadcasted_iota(jnp.int32, (width_y, width_y), 0)
    column = lax.broadcasted_iota(jnp.int32, (width_y, width_y), 1)
    weights = jnp.maximum(2 - jnp.abs(row - column), 0).astype(jnp.float32).astype(jnp.bfloat16)
    for group in range(groups):
        x = x_ref[group].reshape(steps * depth, width_y)
        coarse = x.astype(jnp.bfloat16)
        fine = (x - coarse.astype(jnp.float32)).astype(jnp.bfloat16)
        blurred[group] = (jnp.dot(coarse, weights, preferred_element_type=jnp.float32)
                          + jnp.dot(fine, weights, preferred_element_type=jnp.float32)
                          ).reshape(steps, depth, width_y)
    size = 4
    for first in range(0, steps, size):
        place = pl.ds(first, size)
        for t in range(tile_count):
            swapped = swap_groups(
                [blurred[group, place, :, t * LANES:(t + 1) * LANES] for group in range(groups)],
                groups, width)
            for group in range(groups):
                out_ref[t * groups + group, place] = swapped[group]


def pack(x, groups, width):
    steps = x.shape[0] // groups
    blocks = x.shape[2] // width
    depth, width_y = x.shape[1:]
    return pl.pallas_call(
        functools.partial(pack_kernel, groups, width),
        out_shape=jax.ShapeDtypeStruct((blocks, steps, depth, LANES), jnp.float32),
        in_specs=[pl.BlockSpec(memory_space=pltpu.VMEM)],
        out_specs=pl.BlockSpec(memory_space=pltpu.VMEM),
        scratch_shapes=[pltpu.VMEM((groups, steps, depth, width_y), jnp.float32)],
        compiler_params=pltpu.CompilerParams(vmem_limit_bytes=8 * MIB),
        name="pack",
    )(x.reshape(groups, steps, depth, width_y))


def address_kernel(groups, width, packed_ref, before_ref, after_ref, *refs):
    out_refs, halo = refs[:-1], refs[-1]
    count, steps, depth, _ = packed_ref.shape
    me = lax.axis_index("gz")
    tile_count = before_ref.shape[2] // LANES
    lane = lax.broadcasted_iota(jnp.int32, (depth, LANES), 1)
    position = lax.axis_index("gx")
    inside = (position > 0, position < lax.axis_size("gx") - 1)
    ends = blur_rows(
        [[jnp.where(there, ref[0, :, t * LANES:(t + 1) * LANES], 0.0) for t in range(tile_count)]
         for ref, there in zip((before_ref, after_ref), inside)], lane)
    for t in range(tile_count):
        tiles = [ends[0][t]] * (groups - 1) + [ends[1][t]]
        swapped = swap_groups(tiles, groups, width)
        for part in range(groups):
            halo[t * groups + part] = swapped[part]
    for apart, out_ref in enumerate(out_refs):
        out_ref[0:steps] = packed_ref[me ^ apart]
        out_ref[steps] = halo[me ^ apart]


def address(packed, before, after, groups, width):
    count, steps, depth, _ = packed.shape
    shape = jax.ShapeDtypeStruct((steps + 1, depth, LANES), jnp.float32)
    return pl.pallas_call(
        functools.partial(address_kernel, groups, width),
        out_shape=[shape] * count,
        in_specs=[pl.BlockSpec(memory_space=pltpu.VMEM)] * 3,
        out_specs=[pl.BlockSpec(memory_space=pltpu.VMEM)] * count,
        scratch_shapes=[pltpu.VMEM((count, depth, LANES), jnp.float32)],
        compiler_params=pltpu.CompilerParams(vmem_limit_bytes=8 * MIB),
        name="address",
    )(packed, before, after)


def split_sum(table, wide):
    coarse = wide.astype(jnp.bfloat16)
    fine = (wide - coarse.astype(jnp.float32)).astype(jnp.bfloat16)
    weights = jnp.concatenate([coarse, coarse, fine], axis=0)
    return jnp.dot(table, weights, preferred_element_type=jnp.float32)


def smooth_layers(groups, width, scale, far, count, pieces, s_ref, raw):
    steps, depth = pieces[0].shape[-3] - 1, pieces[0].shape[-2]
    blocks = count // 2
    layers = depth * blocks
    slots = s_ref.shape[1]
    me = lax.axis_index("gz")
    lower = me < blocks
    lane = group_ids((depth, LANES), width)

    def place_piece(piece, row):
        place = pl.ds(row, depth)
        raw[1:steps + 1, place, :] = piece[0:steps]
        halo = piece[steps]
        low = pltpu.roll(piece[steps - 1], width, 1)
        high = pltpu.roll(piece[0], LANES - width, 1)
        raw[0, place, :] = jnp.where(lane == 0, halo, low)
        raw[steps + 1, place, :] = jnp.where(lane == groups - 1, halo, high)

    zeros = jnp.zeros((steps + 2, depth, LANES), jnp.float32)
    raw[:, 0:depth, :] = zeros
    raw[:, depth + layers:2 * depth + layers, :] = zeros
    for apart in range(len(pieces)):
        block = (me ^ apart) % blocks
        if far and apart < blocks:
            @pl.when(block == jnp.where(lower, blocks - 1, 0))
            def _():
                row = jnp.where(lower, 0, depth + layers)
                place_piece(pieces[apart], pl.multiple_of(row, 8))
        else:
            place_piece(pieces[apart], pl.multiple_of(depth + block * depth, 8))
    slot = lax.broadcasted_iota(jnp.int32, (layers + depth, LANES), 0)
    if far:
        empty = slot > layers
        if slots > layers + depth:
            s_ref[:, layers + depth:slots, :] = jnp.full(
                (steps, slots - layers - depth, LANES), -1.0, jnp.float32)
    else:
        empty = (slot == jnp.where(lower, layers - 1, 0))[:layers]

    def smooth(step, carry):
        v = raw[step] + 2.0 * raw[step + 1] + raw[step + 2]
        size = v.shape[0]
        before = pltpu.roll(v, 1, 0)
        after = pltpu.roll(v, size - 1, 0)
        total = (before + 2.0 * v + after) * (scale / 64.0)
        if far:
            shifted = pltpu.roll(total, size - (depth - 1), 0)[:layers + depth]
            value = jnp.where(lower, shifted, total[depth:2 * depth + layers])
            s_ref[step, 0:layers + depth] = jnp.where(empty, -1.0, value)
        else:
            s_ref[step] = jnp.where(empty, -1.0, total[depth:depth + layers])
        return carry

    lax.fori_loop(0, steps, smooth, 0, unroll=8)


def scan_quarters(groups, width, sums_ref, start_ref, total_ref, offset):
    colors = sums_ref.shape[1]
    group = group_ids((colors, LANES), width)

    def scan_groups(chunk, carry):
        packed = jnp.zeros((colors, LANES), jnp.float32)
        for k in range(groups):
            z = chunk * groups + k
            both = sums_ref[z]
            moved = [pltpu.roll(both, k * width, 1) for k in range(1, groups)]
            begin = jnp.zeros((colors, LANES), jnp.float32)
            everything = both
            for place, value in enumerate(moved, 1):
                begin = begin + jnp.where(group >= place, value, 0.0)
                everything = everything + value
            start_ref[z] = begin
            packed = jnp.where(group == k, everything, packed)
        total_ref[offset + chunk] = packed
        return carry

    lax.fori_loop(0, total_ref.shape[0] - offset, scan_groups, 0, unroll=4)


def bin_edges(bins):
    return lax.broadcasted_iota(jnp.int32, (bins, LANES), 0).astype(jnp.float32) - 1.0


def properties(s, size, table, bins):
    edge = bin_edges(bins).astype(jnp.bfloat16)
    zero = jnp.zeros((bins, LANES), jnp.bfloat16)
    one = jnp.ones((bins, LANES), jnp.bfloat16)
    lower_bin = jnp.floor(s)
    frac = s - lower_bin
    coarse = frac.astype(jnp.bfloat16).astype(jnp.float32)
    fine = frac - coarse

    def wide(value, r):
        return jnp.broadcast_to(value[r:r + 1], (bins, LANES)).astype(jnp.bfloat16)

    columns = []
    for r in range(size):
        away = wide(lower_bin, r) - edge
        main = jnp.minimum(jnp.maximum(away + wide(coarse, r), zero), one)
        rest = jnp.where(away == zero, wide(fine, r), zero)
        columns.append(jnp.concatenate([main, main, rest], axis=0))
    return jnp.dot(table, jnp.concatenate(columns, axis=1), preferred_element_type=jnp.float32)


def render_rows(bins, ratio, s_ref, table_ref, lit_ref, unlit_ref, through_ref, depth):
    steps, layers, colors, _ = lit_ref.shape
    depth[...] = jnp.zeros(depth.shape, jnp.float32)
    table = table_ref[...]
    block = 8

    def advance(step, carry):
        through = jnp.ones((colors, LANES), jnp.float32)
        unlit = jnp.zeros((colors, LANES), jnp.float32)
        for place in range(0, layers, block):
            size = min(block, layers - place)
            props = properties(s_ref[step, place:place + block, :], size, table, bins)
            for r in range(size):
                part = props[:, r * LANES:(r + 1) * LANES]
                sigma, color = part[:colors], part[colors:]
                later = through * jnp.exp2(sigma)
                seen = (through - later) * color
                above = depth[place + r]
                unlit = unlit + seen
                lit_ref[step, place + r] = seen * jnp.exp2(above)
                depth[place + r] = above + sigma * ratio
                through = later
        unlit_ref[step], through_ref[step] = unlit, through
        return carry

    lax.fori_loop(0, steps, advance, 0, unroll=8)


def near_kernel(groups, width, bins, ratio, count, *refs):
    pieces = refs[:count // 2]
    (table_ref, lit_ref, unlit_ref, through_ref, start_ref, total_ref, raw, s_ref,
     depth) = refs[count // 2:]
    smooth_layers(groups, width, float(bins - 1), False, count, pieces, s_ref, raw)
    render_rows(bins, ratio, s_ref, table_ref, lit_ref, unlit_ref, through_ref, depth)
    scan_quarters(groups, width, depth, start_ref, total_ref, 0)


def render_near(pieces, table, colors, groups, width, bins, ratio, count):
    steps, depth = pieces[0].shape[0] - 1, pieces[0].shape[1]
    layers = depth * len(pieces)
    plane = jax.ShapeDtypeStruct((steps, colors, LANES), jnp.float32)
    return pl.pallas_call(
        functools.partial(near_kernel, groups, width, bins, ratio, count),
        out_shape=(
            jax.ShapeDtypeStruct((steps, layers, colors, LANES), jnp.float32),
            plane,
            plane,
            jax.ShapeDtypeStruct((layers, colors, LANES), jnp.float32),
            jax.ShapeDtypeStruct((layers // groups, colors, LANES), jnp.float32),
        ),
        in_specs=[pl.BlockSpec(memory_space=pltpu.VMEM)] * (len(pieces) + 1),
        out_specs=[pl.BlockSpec(memory_space=pltpu.VMEM)] * 5,
        scratch_shapes=[
            pltpu.VMEM((steps + 2, layers + 2 * depth, LANES), jnp.float32),
            pltpu.VMEM((steps, layers, LANES), jnp.float32),
            pltpu.VMEM((layers, colors, LANES), jnp.float32),
        ],
        compiler_params=pltpu.CompilerParams(vmem_limit_bytes=20 * MIB),
        cost_estimate=pl.CostEstimate(flops=0, bytes_accessed=0, transcendentals=0),
        name="render_near",
    )(*pieces, table)


def depth_kernel(groups, width, bins, count, *refs):
    pieces = refs[:count]
    _, table_ref, s_ref, start_ref, total_ref, raw, sums, products_ref = refs[count:]
    steps, depth = pieces[0].shape[-3] - 1, pieces[0].shape[-2]
    layers = depth * (count // 2)
    slots = s_ref.shape[1]
    smooth_layers(groups, width, float(bins - 1), True, count, pieces, s_ref, raw)
    edge = bin_edges(bins) + 1.0
    first_bin = lax.broadcasted_iota(jnp.int32, (bins, LANES), 0) == 0

    def count_layer(z, carry):
        acc = [jnp.zeros((bins, LANES), jnp.float32)] * 2
        for step in range(steps):
            row = jnp.broadcast_to(s_ref[step, pl.ds(z, 1), :], (bins, LANES))
            acc[step % 2] = acc[step % 2] + jnp.minimum(row, edge)
        high = acc[0] + acc[1]
        low = jnp.where(first_bin, -1.0 * steps, pltpu.roll(high, 1, 0))
        sums[z] = high - low
        return carry

    lax.fori_loop(0, layers, count_layer, 0, unroll=4)
    count_layer(layers, 0)
    for z in range(layers + 1, slots):
        sums[z] = jnp.zeros((bins, LANES), jnp.float32)
    table = table_ref[...]
    at_once = 8

    def products(chunk, carry):
        wide = [sums[chunk * at_once + k] for k in range(at_once)]
        out = split_sum(table, jnp.concatenate(wide, axis=1))
        for k in range(at_once):
            products_ref[chunk * at_once + k] = out[:, k * LANES:(k + 1) * LANES]
        return carry

    lax.fori_loop(0, slots // at_once, products, 0, unroll=True)
    scan_quarters(groups, width, products_ref, start_ref, total_ref, 0)


def far_depths(pieces, near_total, table, groups, width, bins):
    count = len(pieces)
    steps, depth = pieces[0].shape[0] - 1, pieces[0].shape[1]
    layers = depth * (count // 2)
    slots = layers + max(groups, depth)
    colors = table.shape[0]
    limit = 8 * MIB + slots * (LANES * 4) * (bins + 2 * colors)
    return pl.pallas_call(
        functools.partial(depth_kernel, groups, width, bins, count),
        out_shape=(
            jax.ShapeDtypeStruct((steps, slots, LANES), jnp.float32),
            jax.ShapeDtypeStruct((slots, colors, LANES), jnp.float32),
            jax.ShapeDtypeStruct((layers // groups + 1, colors, LANES), jnp.float32),
        ),
        in_specs=[pl.BlockSpec(memory_space=pltpu.VMEM)] * (count + 2),
        out_specs=[pl.BlockSpec(memory_space=pltpu.VMEM)] * 3,
        scratch_shapes=[
            pltpu.VMEM((steps + 2, layers + 2 * depth, LANES), jnp.float32),
            pltpu.VMEM((slots, bins, LANES), jnp.float32),
            pltpu.VMEM((slots, colors, LANES), jnp.float32),
        ],
        compiler_params=pltpu.CompilerParams(vmem_limit_bytes=limit),
        cost_estimate=pl.CostEstimate(flops=0, bytes_accessed=0, transcendentals=0),
        name="far_depths",
    )(*pieces, near_total, table)


def render_far(s, table, colors, bins, ratio, layers):
    steps = s.shape[0]
    plane = jax.ShapeDtypeStruct((steps, colors, LANES), jnp.float32)
    return pl.pallas_call(
        functools.partial(render_rows, bins, ratio),
        out_shape=(jax.ShapeDtypeStruct((steps, layers, colors, LANES), jnp.float32), plane, plane),
        in_specs=[pl.BlockSpec(memory_space=pltpu.VMEM)] * 2,
        out_specs=[pl.BlockSpec(memory_space=pltpu.VMEM)] * 3,
        scratch_shapes=[pltpu.VMEM((layers, colors, LANES), jnp.float32)],
        compiler_params=pltpu.CompilerParams(vmem_limit_bytes=20 * MIB),
        cost_estimate=pl.CostEstimate(
            flops=10 ** 10, bytes_accessed=10 ** 7, transcendentals=10 ** 7),
        name="render_far",
    )(s, table)


def join_kernel(groups, width, turn, blocks, columns_ref, *refs):
    near_lit, near_unlit, near_through, far_lit, far_unlit, far_through = refs[:6]
    if turn:
        near_start, far_start = refs[6:8]
        before_refs, out_ref, near_light, far_light, image = refs[8:-4], *refs[-4:]
        hops = len(before_refs) // 2
    else:
        near_light, far_light, out_ref, image = refs[6:]
    rows, colors, _ = image.shape
    layers, far_layers = near_lit.shape[1], far_lit.shape[1]
    me = lax.axis_index("gz")
    lower = me < blocks
    half = (me + turn) % 2
    position = lax.axis_index("gx")
    group = group_ids((colors, LANES), width)
    ahead = layers // groups

    def begin(chunk, start_ref, refs, light):
        packed = jnp.zeros((colors, LANES), jnp.float32)
        for hop, ref in enumerate(refs, 1):
            packed = packed + jnp.where(position >= hop, ref[chunk], 0.0)
        moved = [packed] + [pltpu.roll(packed, k * width, 1) for k in range(1, groups)]
        for k in range(groups):
            value = moved[-k % groups]
            for place in range(1, groups):
                value = jnp.where(group == place, moved[(place - k) % groups], value)
            z = chunk * groups + k
            light[z] = jnp.exp2(start_ref[z] + value)

    def begin_near(chunk, carry):
        begin(chunk, near_start, before_refs[:hops], near_light)
        return carry

    def begin_far(chunk, carry):
        begin(chunk, far_start, before_refs[hops:], far_light)
        return carry

    if turn:
        lax.fori_loop(0, ahead, begin_near, 0, unroll=4)
        lax.fori_loop(0, before_refs[hops].shape[0], begin_far, 0, unroll=3)
    ambient = columns_ref[1]
    backdrop = columns_ref[2]
    at_once = 4 if rows % 4 == 0 else 2

    def light_rows(chunk, carry):
        place = [chunk * at_once + k for k in range(at_once)]

        def lit_sum(lit, unlit, light, count):
            sums = [unlit[half * rows + row] * ambient for row in place]
            for z in range(count):
                factor = light[z]
                for k, row in enumerate(place):
                    sums[k] = sums[k] + lit[half * rows + row, z] * factor
            return sums

        near = lit_sum(near_lit, near_unlit, near_light, layers)
        far = lit_sum(far_lit, far_unlit, far_light, far_layers)
        for k, row in enumerate(place):
            through = far_through[half * rows + row]
            passed = near_through[half * rows + row]
            front = jnp.where(lower, near[k], far[k])
            back = jnp.where(lower, far[k], near[k])
            image[row] = (front + jnp.where(lower, passed, through) * back
                          + through * passed * backdrop)
        return carry

    lax.fori_loop(0, rows // at_once, light_rows, 0, unroll=2)
    if len(out_ref.shape) == 3:
        out_ref[...] = image[...]
        return
    for chunk in range(rows // groups):
        tiles = swap_groups([image[chunk * groups + k] for k in range(groups)], groups, width)
        for part in range(groups):
            image[chunk * groups + part] = tiles[part]
    for slot in range(groups):
        part = slot ^ (me // 2)
        for chunk in range(rows // groups):
            out_ref[slot, chunk] = image[chunk * groups + part]


def join(columns, near, far, light, groups, width, turn, blocks):
    steps, layers, colors, _ = near[0].shape
    share = steps // 2
    shape = (share, colors, LANES)
    if share % groups == 0:
        shape = (groups, share // groups, colors, LANES)
    shapes = [jax.ShapeDtypeStruct(shape, jnp.float32)]
    if turn:
        shapes += [jax.ShapeDtypeStruct(start.shape, jnp.float32) for start in light[:2]]
    operands = [columns, *near, *far, *light]
    return pl.pallas_call(
        functools.partial(join_kernel, groups, width, turn, blocks),
        out_shape=shapes,
        in_specs=[pl.BlockSpec(memory_space=pltpu.VMEM)] * len(operands),
        out_specs=[pl.BlockSpec(memory_space=pltpu.VMEM)] * len(shapes),
        scratch_shapes=[pltpu.VMEM((share, colors, LANES), jnp.float32)],
        compiler_params=pltpu.CompilerParams(vmem_limit_bytes=24 * MIB),
        cost_estimate=pl.CostEstimate(flops=0, bytes_accessed=0, transcendentals=0),
        name="join",
    )(*operands)


def unpack_kernel(groups, width, *refs):
    arrived, out_ref, pieces = refs[:-2], refs[-2], refs[-1]
    count = 2 * len(arrived)
    me = lax.axis_index("gz")
    for apart in range(count):
        pieces[me ^ apart] = arrived[apart // 2][apart % 2]
    for tile in range(count // groups):
        for chunk in range(arrived[0].shape[1]):
            tiles = swap_groups(
                [pieces[tile * groups + part, chunk] for part in range(groups)], groups, width)
            for part in range(groups):
                out_ref[chunk * groups + part, :, tile * LANES:(tile + 1) * LANES] = tiles[part]


def unpack(arrived, groups, width):
    count = 2 * len(arrived)
    _, chunks, colors, _ = arrived[0].shape
    return pl.pallas_call(
        functools.partial(unpack_kernel, groups, width),
        out_shape=jax.ShapeDtypeStruct((chunks * groups, colors, count * width), jnp.float32),
        in_specs=[pl.BlockSpec(memory_space=pltpu.VMEM)] * len(arrived),
        out_specs=pl.BlockSpec(memory_space=pltpu.VMEM),
        scratch_shapes=[pltpu.VMEM((count, chunks, colors, LANES), jnp.float32)],
        compiler_params=pltpu.CompilerParams(vmem_limit_bytes=8 * MIB),
        name="unpack",
    )(*arrived)


def table_kernel(step_x, step_z, bins_ref, scale_ref, ambient_ref, backdrop_ref, extinction_ref,
                 color_ref, sum_ref, split_ref, columns_ref):
    rows, bins = extinction_ref.shape[1], bins_ref.shape[0]
    colors = extinction_ref.shape[0]
    row = lax.broadcasted_iota(jnp.int32, (rows, bins), 0)
    lane = lax.broadcasted_iota(jnp.int32, (8, bins), 1)
    this = jnp.full((8, bins), -1, jnp.int32)
    last = jnp.full((8, bins), -1, jnp.int32)
    for k in range(bins):
        this = jnp.where(lane == k, bins_ref[k], this)
        if k:
            last = jnp.where(lane == k, bins_ref[k - 1], last)
    here = (row == this[0:1, :]).astype(jnp.float32)
    below = (row == last[0:1, :]).astype(jnp.float32)
    place = lax.broadcasted_iota(jnp.int32, (colors, LANES), 0)
    columns = []
    for ref in (scale_ref, ambient_ref, backdrop_ref):
        column = jnp.zeros((colors, LANES), jnp.float32)
        for k in range(colors):
            column = jnp.where(place == k, ref[k], column)
        columns.append(column)
    for k, column in enumerate(columns):
        columns_ref[k] = column

    def rise(ref):
        now = jnp.dot(ref[...], here, precision=lax.Precision.HIGHEST,
                      preferred_element_type=jnp.float32)
        then = jnp.dot(ref[...], below, precision=lax.Precision.HIGHEST,
                       preferred_element_type=jnp.float32)
        return now - then

    def split(value):
        coarse = value.astype(jnp.bfloat16)
        fine = (value - coarse.astype(jnp.float32)).astype(jnp.bfloat16)
        return jnp.concatenate([coarse, fine, coarse], axis=1)

    sigma = rise(extinction_ref) * columns[0][:, 0:bins]
    sum_ref[...] = split(sigma * (-step_x * LOG2E))
    split_ref[0:colors] = split(sigma * (-step_z * LOG2E))
    split_ref[colors:2 * colors] = split(rise(color_ref))


def tables(bin_rows, scale, ambient, backdrop, tf_extinction, tf_color, step_x, step_z):
    bins = bin_rows.shape[0]
    colors = tf_color.shape[1]
    return pl.pallas_call(
        functools.partial(table_kernel, step_x, step_z),
        out_shape=(
            jax.ShapeDtypeStruct((colors, 3 * bins), jnp.bfloat16),
            jax.ShapeDtypeStruct((2 * colors, 3 * bins), jnp.bfloat16),
            jax.ShapeDtypeStruct((3, colors, LANES), jnp.float32),
        ),
        in_specs=[pl.BlockSpec(memory_space=pltpu.SMEM)] * 4
        + [pl.BlockSpec(memory_space=pltpu.VMEM)] * 2,
        out_specs=[pl.BlockSpec(memory_space=pltpu.VMEM)] * 3,
        compiler_params=pltpu.CompilerParams(vmem_limit_bytes=4 * MIB),
        name="tables",
    )(bin_rows, scale, ambient, backdrop, tf_extinction.T, tf_color.T)


def exchange(value, axis, apart):
    pairs = [(source, source ^ apart) for source in range(lax.axis_size(axis))]
    return lax.ppermute(value, axis, pairs)


def local(density, bin_rows, tf_extinction, tf_color, extinction_scale, ambient, backdrop):
    rows_x, depth, width_y = density.shape
    colors = tf_color.shape[1]
    bins = bin_rows.shape[0]
    count = lax.axis_size("gz")
    size_x = lax.axis_size("gx")
    me = lax.axis_index("gz")
    width = width_y // count
    groups = LANES // width
    steps = rows_x // groups
    step_x = 1.0 / (rows_x * size_x)
    step_z = 1.0 / (depth * count)

    up = [(i, (i + 1) % size_x) for i in range(size_x)]
    down = [(j, i) for i, j in up]
    before = lax.ppermute(density[rows_x - 1:], "gx", up)
    after = lax.ppermute(density[:1], "gx", down)

    packed = pack(density, groups, width)
    pieces = list(address(packed, before, after, groups, width))
    for apart in range(1, count):
        give = pieces[apart]
        if apart > count // 2:
            ahead = max(apart - count // 2 - 1, 1)
            give, _ = lax.optimization_barrier((give, pieces[ahead]))
        pieces[apart] = exchange(give, "gz", apart)
    bin_rows, extinction_scale, ambient, backdrop, _ = lax.optimization_barrier(
        (bin_rows, extinction_scale, ambient, backdrop, pieces[2]))
    sum_table, table, columns = tables(
        bin_rows, extinction_scale, ambient, backdrop, tf_extinction, tf_color, step_x, step_z)

    blocks = count // 2
    ratio = step_x / step_z
    *near, near_start, near_total = render_near(
        pieces[:blocks], table, colors, groups, width, bins, ratio, count)
    s, start, far_total = far_depths(pieces, near_total, sum_table, groups, width, bins)
    sums = [lax.ppermute(total, "gx", [(i, (i + hop) % size_x) for i in range(size_x)])
            for total in (near_total, far_total) for hop in range(1, size_x)]
    layers = depth * blocks
    far = render_far(s, table, colors, bins, ratio, layers + 1)
    other, *light = join(
        columns, near, far, [near_start, start, *sums], groups, width, 1, blocks)

    share = steps // 2
    if share % groups == 0:
        joined = exchange(other, "gz", 1)
        own, = join(columns, near, far, light, groups, width, 0, blocks)
        both = jnp.stack([own, joined], axis=1)
        arrived = []
        for slot in range(count // 2):
            arrived.append(exchange(both[slot], "gz", 2 * slot) if slot else both[0])
        return unpack(arrived, groups, width)
    halves = [*join(columns, near, far, light, groups, width, 0, blocks), other]
    even = me % 2 == 0
    image = jnp.stack([jnp.where(even, halves[0], halves[1]),
                       jnp.where(even, halves[1], halves[0])])
    image = image.reshape(2, share, colors, groups, width).transpose(3, 0, 1, 2, 4)
    image = lax.all_to_all(image.reshape(count, share, colors, width), "gz", 0, 0)
    return image.transpose(1, 2, 0, 3).reshape(share, colors, width_y)


def solution(mesh):
    in_specs = (P("gx", "gz", None), P(), P(), P(), P(), P(), P())
    out_specs = P(("gx", "gz"), None, None)
    return jax.shard_map(local, mesh=mesh, in_specs=in_specs, out_specs=out_specs, check_vma=False)
```
